32 devices in a mesh: slab: 4 (over x, core), clip: 8 (over z, y).
Axes of the slice: x: 2, y: 2, z: 4, core: 2. Of those that a mesh axis runs over, the one named last changes fastest.
Arguments:
- tokens: bfloat16 [8, 4, 1024, 512], P('clip', 'slab'), may hold values from -6 to 6
- y_grad: bfloat16 [8, 4, 1024, 512], P('clip', 'slab'), may hold values from -6 to 6
- clip_rows: int32 [8, 4], P('clip'), may hold values from 0 to 192, as said below
- qkv_weight: float32 [512, 1536], P('clip', 'slab'), may hold values from -0.25 to 0.25
- proj_weight: float32 [512, 512], P('clip', 'slab'), may hold values from -0.75 to 0.75
- up_weight: float32 [512, 2048], P('clip', 'slab'), may hold values from -0.25 to 0.25
- down_weight: float32 [2048, 512], P('clip', 'slab'), may hold values from -0.1875 to 0.1875
- qkv_m: float32 [512, 1536], P('clip', 'slab'), may hold values from -1.2 to 1.2
- proj_m: float32 [512, 512], P('clip', 'slab'), may hold values from -1.2 to 1.2
- up_m: float32 [512, 2048], P('clip', 'slab'), may hold values from -1.2 to 1.2
- down_m: float32 [2048, 512], P('clip', 'slab'), may hold values from -1.2 to 1.2
- qkv_v: float32 [512, 1536], P('clip', 'slab'), may hold values from 0.05 to 0.35
- proj_v: float32 [512, 512], P('clip', 'slab'), may hold values from 0.05 to 0.35
- up_v: float32 [512, 2048], P('clip', 'slab'), may hold values from 0.05 to 0.35
- down_v: float32 [2048, 512], P('clip', 'slab'), may hold values from 0.05 to 0.35
- vectors: float32 [12, 512], replicated, may hold values from -1.2 to 1.5, as said below
- vectors_m: float32 [12, 512], replicated, may hold values from -1.2 to 1.2
- vectors_v: float32 [12, 512], replicated, may hold values from 0.05 to 0.35
- table: float32 [49, 16], replicated, may hold values from -3 to 3
- table_m: float32 [49, 16], replicated, may hold values from -1.2 to 1.2
- table_v: float32 [49, 16], replicated, may hold values from 0.05 to 0.35
Outputs:
- block_out: bfloat16 [8, 4, 1024, 512], P('clip', 'slab')
- x_grad: float32 [8, 4, 1024, 512], P('clip', 'slab')
- qkv_new: float32 [512, 1536], P('clip', 'slab')
- qkv_m_new: float32 [512, 1536], P('clip', 'slab')
- qkv_v_new: float32 [512, 1536], P('clip', 'slab')
- proj_new: float32 [512, 512], P('clip', 'slab')
- proj_m_new: float32 [512, 512], P('clip', 'slab')
- proj_v_new: float32 [512, 512], P('clip', 'slab')
- up_new: float32 [512, 2048], P('clip', 'slab')
- up_m_new: float32 [512, 2048], P('clip', 'slab')
- up_v_new: float32 [512, 2048], P('clip', 'slab')
- down_new: float32 [2048, 512], P('clip', 'slab')
- down_m_new: float32 [2048, 512], P('clip', 'slab')
- down_v_new: float32 [2048, 512], P('clip', 'slab')
- vectors_new: float32 [12, 512], replicated
- vectors_m_new: float32 [12, 512], replicated
- vectors_v_new: float32 [12, 512], replicated
- table_new: float32 [49, 16], replicated
- table_m_new: float32 [49, 16], replicated
- table_v_new: float32 [49, 16], replicated
The draws below stay inside these ranges and needn't reach their ends.
Inputs may be any that keep to these rules, and one draw needn't show every extreme that they name: `clip_rows`: each entry is 0 (no clip), 64 or 192; in a row the nonzero entries come first and there is at least one; a row's entries sum to at most 512, and in every draw some row sums to exactly that and holds a clip of 192 rows. `vectors`: rows 0 and 5 lie in 0.5 to 1.5.
All inputs are finite; a program needn't handle non-finite values.
Results may differ from the reference program's by a relative error of at most 0.015.
Values may be sent and summed in bfloat16 or wider, within the bound.
A program may use at most 128 MiB of HBM per device.

```python
import math
import jax
import jax.numpy as jnp
from jax import lax

D = 512
FF = 2048
HEADS = 16
BINS = 8
WIN = 4
SHORT = 64
ROWS_DEV = 128
STEP = 10
HEAD = 32
RELS = 49
VROWS = 12
GROUPS = 8
SLABS = 4
SLOTS = 4
TOK_DEV = 1024
TOKENS = 32768


def draw_clip_rows(key, part):
    key = jax.random.fold_in(key, 11)
    pick_key, count_key, long_key, turn_key = jax.random.split(key, 4)
    units_all = SLABS * ROWS_DEV // SHORT
    groups_at = jnp.arange(GROUPS, dtype=jnp.int32)
    full_group = jax.random.randint(pick_key, (), 0, GROUPS)
    clips_live = jax.random.randint(count_key, (GROUPS,), 1, SLOTS + 1)
    long_room = jnp.minimum(clips_live, (units_all - clips_live) // 2)
    long_count = jax.random.randint(long_key, (GROUPS,), 0, 1 << 20) % (long_room + 1)
    full_long = max(1, (units_all - SLOTS + 1) // 2)
    long_count = jnp.where(groups_at == full_group, full_long, long_count)
    clips_live = jnp.where(groups_at == full_group, units_all - 2 * full_long, clips_live)
    turn_count = jax.random.randint(turn_key, (GROUPS,), 0, 1 << 20) % clips_live
    slot_ids = jnp.arange(SLOTS, dtype=jnp.int32)[None, :]
    is_long = (slot_ids + turn_count[:, None]) % clips_live[:, None] < long_count[:, None]
    lengths = jnp.where(is_long, 3 * SHORT, SHORT)
    return jnp.where(slot_ids < clips_live[:, None], lengths, 0).astype(jnp.int32)


def draw_vectors(key, part):
    key = jax.random.fold_in(key, 7)
    gain_key, bias_key = jax.random.split(key)
    gain_rows = jax.random.uniform(gain_key, (VROWS, D), jnp.float32, 0.5, 1.5)
    bias_rows = jnp.clip(0.3 * jax.random.normal(bias_key, (VROWS, D), jnp.float32), -1.2, 1.2)
    row_ids = jnp.arange(VROWS)[:, None]
    return jnp.where((row_ids == 0) | (row_ids == 5), gain_rows, bias_rows)


def block_levels(rng, dims, cuts, least, top_value):
    factor_of, own = 1.0, jax.random.fold_in(rng, 6)
    for position, parts in cuts:
        steps = jnp.exp(jax.random.uniform(jax.random.fold_in(own, position), (parts,), jnp.float32, least / len(cuts), top_value / len(cuts)))
        factor_of = factor_of * jnp.repeat(steps, dims[position] // parts).reshape([-1 if axis == position else 1 for axis in range(len(dims))])
    return factor_of


def noise(own_key, extent, deviation, most, cuts=(), kind=jnp.bfloat16):
    gain = block_levels(own_key, extent, cuts, -0.22, 0.18) if cuts else 1.0
    values = jax.random.normal(own_key, extent, jnp.float32) * deviation * gain
    return jnp.minimum(jnp.maximum(values, -most), most).astype(kind)


def setup_inputs(seed: int = 0) -> dict:
    key_of = jax.random.split(jax.random.key(seed), 22)
    return {
        "tokens": noise(key_of[0], (GROUPS, SLABS, TOK_DEV, D), 1.0, 6.0, ((0, 8), (1, 4))),
        "y_grad": noise(key_of[1], (GROUPS, SLABS, TOK_DEV, D), 1.0, 6.0, ((0, 8), (1, 4))),
        "clip_rows": draw_clip_rows(jax.random.fold_in(key_of[21], 71), 0),
        "qkv_weight": noise(key_of[3], (D, 3 * D), D ** -0.5, 0.25, ((0, 8), (1, 4)), jnp.float32),
        "proj_weight": noise(key_of[4], (D, D), (D // 8) ** -0.5, 0.75, ((0, 8), (1, 4)), jnp.float32),
        "up_weight": noise(key_of[5], (D, FF), D ** -0.5, 0.25, ((0, 8), (1, 4)), jnp.float32),
        "down_weight": noise(key_of[6], (FF, D), (FF // 2) ** -0.5, 0.1875, ((0, 8), (1, 4)), jnp.float32),
        "qkv_m": noise(key_of[7], (D, 3 * D), 0.3, 1.2, ((0, 8), (1, 4)), jnp.float32),
        "proj_m": noise(key_of[8], (D, D), 0.3, 1.2, ((0, 8), (1, 4)), jnp.float32),
        "up_m": noise(key_of[9], (D, FF), 0.3, 1.2, ((0, 8), (1, 4)), jnp.float32),
        "down_m": noise(key_of[10], (FF, D), 0.3, 1.2, ((0, 8), (1, 4)), jnp.float32),
        "qkv_v": jnp.clip(jnp.exp(math.log(0.35) - 1.9459101 * jax.random.uniform(key_of[11], (D, 3 * D), jnp.float32) ** block_levels(key_of[11], (D, 3 * D), ((0, 8), (1, 4)), -0.2, 0.2)), 0.05, 0.35),
        "proj_v": jnp.clip(jnp.exp(math.log(0.35) - 1.9459101 * jax.random.uniform(key_of[12], (D, D), jnp.float32) ** block_levels(key_of[12], (D, D), ((0, 8), (1, 4)), -0.2, 0.2)), 0.05, 0.35),
        "up_v": jnp.clip(jnp.exp(math.log(0.35) - 1.9459101 * jax.random.uniform(key_of[13], (D, FF), jnp.float32) ** block_levels(key_of[13], (D, FF), ((0, 8), (1, 4)), -0.2, 0.2)), 0.05, 0.35),
        "down_v": jnp.clip(jnp.exp(math.log(0.35) - 1.9459101 * jax.random.uniform(key_of[14], (FF, D), jnp.float32) ** block_levels(key_of[14], (FF, D), ((0, 8), (1, 4)), -0.2, 0.2)), 0.05, 0.35),
        "vectors": draw_vectors(jax.random.fold_in(key_of[21], 71), 0),
        "vectors_m": noise(key_of[16], (VROWS, D), 0.3, 1.2, (), jnp.float32),
        "vectors_v": jnp.clip(jnp.exp(jax.random.uniform(key_of[17], (VROWS, D), jnp.float32, math.log(0.05), math.log(0.35))), 0.05, 0.35),
        "table": noise(key_of[18], (RELS, HEADS), 0.7, 3.0, (), jnp.float32),
        "table_m": noise(key_of[19], (RELS, HEADS), 0.3, 1.2, (), jnp.float32),
        "table_v": jnp.clip(jnp.exp(jax.random.uniform(key_of[20], (RELS, HEADS), jnp.float32, math.log(0.05), math.log(0.35))), 0.05, 0.35),
    }


HIGHEST = lax.Precision.HIGHEST
norm_epsilon = 1e-06
beta_first = 0.5
beta_second = 0.5
adam_epsilon = 1e-08
rate_matrix = 0.05
rate_vector = 0.5
weight_decay = 0.05
masked_score = -1e+30

@jax.custom_vjp
def low(v):
    return lax.optimization_barrier(v.astype(jnp.bfloat16)).astype(jnp.float32)

@jax.custom_vjp
def low_back(v):
    return v

def low_keep(v):
    return (low(v), None)

def low_pass(kept, grad):
    return (grad,)

def back_keep(v):
    return (v, None)

def back_low(kept, grad):
    return (low(grad),)
low.defvjp(low_keep, low_pass)
low_back.defvjp(back_keep, back_low)

def layer_norm(values):
    center = values - lax.optimization_barrier(jnp.mean(values, -1, keepdims=True))
    spread = lax.optimization_barrier(jnp.mean(center * center, -1, keepdims=True))
    return center * lax.rsqrt(spread + norm_epsilon)

def window_rows(lengths, slab_index, slab_count, rows_dev):
    segment = (lengths // slab_count).astype(jnp.int32)
    seg_ends = jnp.cumsum(segment).astype(jnp.int32)
    seg_starts = (seg_ends - segment).astype(jnp.int32)
    row_base = WIN * jnp.arange(rows_dev // WIN, dtype=jnp.int32)
    inside = (row_base[:, None] >= seg_starts[None, :]) & (row_base[:, None] < seg_ends[None, :])
    in_clip = jnp.any(inside, axis=1)
    slot_ids = jnp.arange(lengths.shape[0], dtype=jnp.int32)
    clip_end = lax.optimization_barrier(jnp.sum(jnp.where(inside, seg_ends[None, :], 0), axis=1)).astype(jnp.int32)
    clip_slot = lax.optimization_barrier(jnp.sum(jnp.where(inside, slot_ids[None, :], 0), axis=1)).astype(jnp.int32)
    row_ids = row_base[:, None] + jnp.where(in_clip, WIN // 2, 0)[:, None] + jnp.arange(WIN, dtype=jnp.int32)[None, :]
    beyond = in_clip[:, None] & (row_ids >= clip_end[:, None])
    source = jnp.where(beyond, rows_dev + 2 * clip_slot[:, None] + row_ids - clip_end[:, None], row_ids)
    time_wraps = in_clip & (row_base + WIN == clip_end) & (slab_index == slab_count - 1)
    return (source.astype(jnp.int32), time_wraps, seg_starts)

def window_mask(time_wraps, bin_folds):
    positions = jnp.arange(WIN * WIN, dtype=jnp.int32)
    row_half = positions // WIN >= WIN // 2
    bin_half = positions % WIN >= WIN // 2
    same_row = row_half[:, None] == row_half[None, :]
    same_bin = bin_half[:, None] == bin_half[None, :]
    return (~time_wraps[:, None, None] | same_row[None]) & (~bin_folds[:, None, None] | same_bin[None])

def offset_table():
    positions = jnp.arange(WIN * WIN, dtype=jnp.int32)
    row_pos = positions // WIN
    bin_pos = positions % WIN
    offsets = (row_pos[:, None] - row_pos[None, :] + WIN - 1) * (2 * WIN - 1) + (bin_pos[:, None] - bin_pos[None, :] + WIN - 1)
    return (offsets.reshape(-1)[:, None] == jnp.arange(RELS, dtype=jnp.int32)[None, :]).astype(jnp.float32)

def group_layout(lengths):
    bin_order = ((jnp.arange(BINS, dtype=jnp.int32) + WIN // 2) % BINS).astype(jnp.int32)
    tables = []
    wrap_list = []
    for slab_index in range(SLABS):
        source, time_wraps, seg_starts = window_rows(lengths, slab_index, SLABS, ROWS_DEV)
        extra_row = source - ROWS_DEV
        slot_pick = jnp.clip(extra_row // 2, 0, lengths.shape[0] - 1)
        remote = (slab_index + 1) % SLABS * ROWS_DEV + seg_starts[slot_pick] + extra_row % 2
        flat_rows = jnp.where(source < ROWS_DEV, slab_index * ROWS_DEV + source, remote)
        tokens_at = flat_rows[:, :, None] * BINS + bin_order[None, None, :]
        win_rows = source.shape[0]
        tokens_at = tokens_at.reshape(win_rows, WIN, BINS // WIN, WIN).transpose(0, 2, 1, 3)
        tables.append(tokens_at.reshape(win_rows * (BINS // WIN), WIN * WIN).astype(jnp.int32))
        wrap_list.append(jnp.repeat(time_wraps, BINS // WIN))
    token_index = jnp.concatenate(tables).astype(jnp.int32)
    time_wraps = jnp.concatenate(wrap_list)
    bin_folds = jnp.arange(token_index.shape[0]) % (BINS // WIN) == BINS // WIN - 1
    used_rows = jnp.sum(lengths) // SLABS
    live_rows = jnp.arange(SLABS * ROWS_DEV * BINS) // BINS % ROWS_DEV < used_rows
    return (token_index, window_mask(time_wraps, bin_folds), live_rows.astype(jnp.float32))

def block(inputs, qkv_master, proj_master, up_master, down_master, vectors, table, token_index, allowed, offset_hot, live_rows):
    width = inputs.shape[1]
    attn_input = low(layer_norm(inputs) * vectors[0] + vectors[1])
    bias_row = jnp.concatenate([vectors[2], jnp.zeros_like(vectors[2]), vectors[3]])
    qkv_rows = low(low_back(jnp.dot(attn_input, low(qkv_master), precision=HIGHEST) + bias_row))
    windows = qkv_rows[token_index]
    count_win = windows.shape[0]
    query_win = windows[:, :, :width].reshape(count_win, WIN * WIN, HEADS, HEAD)
    key_win = windows[:, :, width:2 * width].reshape(count_win, WIN * WIN, HEADS, HEAD)
    value_win = windows[:, :, 2 * width:].reshape(count_win, WIN * WIN, HEADS, HEAD)
    rel_bias = jnp.dot(offset_hot, table, precision=HIGHEST).reshape(WIN * WIN, WIN * WIN, HEADS).transpose(2, 0, 1)
    scores = jnp.einsum('wqhd,wkhd->whqk', query_win, key_win, precision=HIGHEST) * HEAD ** (-0.5) + rel_bias[None]
    scores = low_back(scores)
    scores = jnp.where(allowed[:, None], scores, masked_score)
    top_score = lax.optimization_barrier(jnp.max(scores, -1, keepdims=True))
    expo = jnp.exp(scores - top_score)
    probs = expo / lax.optimization_barrier(jnp.sum(expo, -1, keepdims=True))
    attended = jnp.einsum('whqk,wkhd->wqhd', low(probs), value_win, precision=HIGHEST).reshape(count_win * WIN * WIN, width)
    placed = jnp.zeros((inputs.shape[0], width), jnp.float32).at[token_index.reshape(-1)].set(attended)
    placed = low(low_back(placed))
    residual = inputs + low_back(jnp.dot(placed, low(proj_master), precision=HIGHEST) + vectors[4])
    mlp_input = low(layer_norm(residual) * vectors[5] + vectors[6])
    pre_gelu = low_back(jnp.dot(mlp_input, low(up_master), precision=HIGHEST) + vectors[8:].reshape(-1))
    activated = low(jax.nn.gelu(pre_gelu, approximate=False))
    result = residual + jnp.dot(activated, low(down_master), precision=HIGHEST) + vectors[7]
    return result * live_rows[:, None]

def adamw(weight, first, second, grad, rate, decay):
    first = beta_first * first + (1.0 - beta_first) * grad
    second = beta_second * second + (1.0 - beta_second) * grad * grad
    fix_first = 1.0 - beta_first ** STEP
    fix_second = 1.0 - beta_second ** STEP
    update = first / fix_first / (jnp.sqrt(second / fix_second) + adam_epsilon)
    return (weight - rate * (update + decay * weight), first, second)

def reference(tokens, y_grad, clip_rows, qkv_weight, proj_weight, up_weight, down_weight, qkv_m, proj_m, up_m, down_m, qkv_v, proj_v, up_v, down_v, vectors, vectors_m, vectors_v, table, table_m, table_v):
    offset_hot = offset_table()
    params = (qkv_weight, proj_weight, up_weight, down_weight, vectors, table)

    def group_step(totals, group_items):
        group_x, group_grad, lengths = group_items
        token_index, allowed, live_rows = group_layout(lengths)

        def forward(inputs, *weights_all):
            return block(inputs, *weights_all, token_index, allowed, offset_hot, live_rows)
        flat_x = group_x.astype(jnp.float32).reshape(-1, D)
        result, pullback = jax.vjp(forward, flat_x, *params)
        grad_list = pullback(group_grad.astype(jnp.float32).reshape(-1, D))
        totals = tuple((running + fresh_grad for running, fresh_grad in zip(totals, grad_list[1:])))
        return (totals, (result.astype(jnp.bfloat16).reshape(group_x.shape), grad_list[0].reshape(group_x.shape)))
    start_sums = tuple((jnp.zeros_like(weight) for weight in params))
    sums, (block_out, x_grad) = lax.scan(group_step, start_sums, (tokens, y_grad, clip_rows))
    grad_scale = float(TOKENS) ** (-0.5)
    grads = [running * grad_scale for running in sums]
    qkv_new, qkv_m_new, qkv_v_new = adamw(qkv_weight, qkv_m, qkv_v, grads[0], rate_matrix, weight_decay)
    proj_new, proj_m_new, proj_v_new = adamw(proj_weight, proj_m, proj_v, grads[1], rate_matrix, weight_decay)
    up_new, up_m_new, up_v_new = adamw(up_weight, up_m, up_v, grads[2], rate_matrix, weight_decay)
    down_new, down_m_new, down_v_new = adamw(down_weight, down_m, down_v, grads[3], rate_matrix, weight_decay)
    vectors_new, vectors_m_new, vectors_v_new = adamw(vectors, vectors_m, vectors_v, grads[4], rate_vector, 0.0)
    table_new, table_m_new, table_v_new = adamw(table, table_m, table_v, grads[5], rate_vector, 0.0)
    return (block_out, x_grad, qkv_new, qkv_m_new, qkv_v_new, proj_new, proj_m_new, proj_v_new, up_new, up_m_new, up_v_new, down_new, down_m_new, down_v_new, vectors_new, vectors_m_new, vectors_v_new, table_new, table_m_new, table_v_new)
```

```python
import functools
import itertools

import jax
import jax.numpy as jnp
from jax import lax
from jax.experimental import pallas as pl
from jax.experimental.pallas import tpu as pltpu
from jax.sharding import PartitionSpec as P

HEADS = 16
BINS = 8
WIN = 4
STEP = 10
RELS = 49


HIGHEST = lax.Precision.HIGHEST
norm_epsilon = 1e-06
beta_first = 0.5
beta_second = 0.5
adam_epsilon = 1e-08
rate_matrix = 0.05
rate_vector = 0.5
weight_decay = 0.05
masked_score = -1e30


def from_behind(block, axis, distance):
    devices = range(lax.axis_size(axis))
    route = [((i - distance) % len(devices), i) for i in devices]
    return lax.ppermute(block, axis, route)


def layer_norm(values):
    center = values - jnp.mean(values, -1, keepdims=True)
    spread = jnp.mean(center * center, -1, keepdims=True)
    return center * lax.rsqrt(spread + norm_epsilon)


def affine_norm(values, gain, offset):
    return layer_norm(values) * gain + offset


def gelu_exact(values):
    return jax.nn.gelu(values, approximate=False)


def window_rows(lengths, slab_index, slab_count, rows_dev):
    segment = lengths // slab_count
    seg_ends = jnp.cumsum(segment)
    seg_starts = seg_ends - segment
    row_base = WIN * jnp.arange(rows_dev // WIN, dtype=jnp.int32)
    inside = (row_base[:, None] >= seg_starts[None, :]) & (row_base[:, None] < seg_ends[None, :])
    in_clip = jnp.any(inside, axis=1)
    slot_ids = jnp.arange(lengths.shape[0], dtype=jnp.int32)
    clip_end = jnp.sum(jnp.where(inside, seg_ends[None, :], 0), axis=1)
    clip_slot = jnp.sum(jnp.where(inside, slot_ids[None, :], 0), axis=1)
    row_ids = (
        row_base[:, None]
        + jnp.where(in_clip, WIN // 2, 0)[:, None]
        + jnp.arange(WIN, dtype=jnp.int32)[None, :]
    )
    beyond = in_clip[:, None] & (row_ids >= clip_end[:, None])
    source = jnp.where(
        beyond, rows_dev + 2 * clip_slot[:, None] + row_ids - clip_end[:, None], row_ids
    )
    time_wraps = in_clip & (row_base + WIN == clip_end) & (slab_index == slab_count - 1)
    return (source, time_wraps, seg_starts)


def window_mask(time_wraps, bin_folds):
    positions = jnp.arange(WIN * WIN, dtype=jnp.int32)
    row_half = positions // WIN >= WIN // 2
    bin_half = positions % WIN >= WIN // 2
    same_row = row_half[:, None] == row_half[None, :]
    same_bin = bin_half[:, None] == bin_half[None, :]
    return (~time_wraps[:, None, None] | same_row[None]) & (
        ~bin_folds[:, None, None] | same_bin[None]
    )


def offset_table():
    positions = jnp.arange(WIN * WIN, dtype=jnp.int32)
    row_pos = positions // WIN
    bin_pos = positions % WIN
    offsets = (row_pos[:, None] - row_pos[None, :] + WIN - 1) * (2 * WIN - 1) + (
        bin_pos[:, None] - bin_pos[None, :] + WIN - 1
    )
    return (offsets.reshape(-1)[:, None] == jnp.arange(RELS, dtype=jnp.int32)[None, :]).astype(
        jnp.float32
    )


def to_windows(extended, source):
    gathered = jnp.roll(extended[source], -(WIN // 2), axis=2)
    win_rows = source.shape[0]
    width = extended.shape[-1]
    gathered = gathered.reshape(win_rows, WIN, BINS // WIN, WIN, width).transpose(0, 2, 1, 3, 4)
    return gathered.reshape(win_rows * (BINS // WIN), WIN * WIN, width)


def from_windows(windows, source, total_rows):
    win_rows = source.shape[0]
    width = windows.shape[-1]
    placed = windows.reshape(win_rows, BINS // WIN, WIN, WIN, width).transpose(0, 2, 1, 3, 4)
    placed = jnp.roll(placed.reshape(win_rows, WIN, BINS, width), WIN // 2, axis=2)
    blank = jnp.zeros((total_rows, BINS, width), windows.dtype)
    return blank.at[source.reshape(-1)].set(placed.reshape(win_rows * WIN, BINS, width))


def adamw(weight, first, second, grad, rate, decay):
    first = beta_first * first + (1.0 - beta_first) * grad
    second = beta_second * second + (1.0 - beta_second) * grad * grad
    fix_first = 1.0 - beta_first**STEP
    fix_second = 1.0 - beta_second**STEP
    update = first / fix_first / (jnp.sqrt(second / fix_second) + adam_epsilon)
    return (weight - rate * (update + decay * weight), first, second)


MESH = pl.DeviceIdType.MESH


class Links:
    def __init__(self, send_sems, recv_sems):
        self.send_sems, self.recv_sems = send_sems, recv_sems
        self.count, self.started = 0, []

    def send(self, source, target, device):
        copy = pltpu.make_async_remote_copy(
            src_ref=source,
            dst_ref=target,
            send_sem=self.send_sems.at[self.count],
            recv_sem=self.recv_sems.at[self.count],
            device_id=device,
            device_id_type=MESH,
        )
        copy.start()
        self.count += 1
        self.started.append(copy)
        return copy

    def drain(self):
        for copy in self.started:
            copy.wait_send()


class Place:
    def __init__(self, clip_size):
        self.slab, self.clip = lax.axis_index("slab"), lax.axis_index("clip")
        self.x, self.core = self.slab // 2, self.slab % 2
        self.z, self.y = self.clip // 2, self.clip % 2
        self.depth = clip_size // 2
        self.over_core = (self.x * 2 + 1 - self.core, self.clip)
        self.over_x = ((1 - self.x) * 2 + self.core, self.clip)
        self.over_y = (self.slab, self.z * 2 + 1 - self.y)
        self.x_slab = (1 - self.x) * 2 + self.core
        self.core_slab = self.x * 2 + 1 - self.core

    def z_at(self, step):
        return lax.rem(self.z + step, self.depth)

    def over_z(self, step):
        return (self.slab, self.z_at(step) * 2 + self.y)

    def greet(self):
        barrier = pltpu.get_barrier_semaphore()
        partners = [self.over_core, self.over_x, self.over_y]
        partners += [self.over_z(step) for step in range(1, self.depth)]
        for partner in partners:
            pl.semaphore_signal(barrier, inc=1, device_id=partner, device_id_type=MESH)
        pl.semaphore_wait(barrier, len(partners))


def wait_all(copies):
    for copy in copies:
        copy.wait_recv()


class Gather:
    def __init__(self, place, links, whole, width):
        self.place, self.links, self.whole, self.width = place, links, whole, width

    def columns(self, slab):
        return pl.ds(pl.multiple_of(slab * self.width, 128), self.width)

    def move(self, device, *index):
        block = self.whole.at[index]
        return self.links.send(block, block, device)

    def begin(self, master):
        place = self.place
        rows = self.whole.shape[3]
        for half in range(2):
            self.whole[place.z, place.y, half, :, self.columns(place.slab)] = master[
                half * rows : (half + 1) * rows, :
            ].astype(jnp.bfloat16)
        self.over_z = [
            [
                self.move(
                    place.over_z(step), place.z, place.y, half, slice(None), self.columns(place.slab)
                )
                for step in range(1, place.depth)
            ]
            for half in range(2)
        ]

    def second(self):
        place, every = self.place, slice(None)
        mine = self.columns(place.slab)
        wait_all(self.over_z[0])
        self.first_x = self.move(place.over_x, every, place.y, 0, every, mine)
        wait_all(self.over_z[1])
        self.first_y = self.move(place.over_y, every, place.y, 1, every, mine)

    def third(self):
        place, every = self.place, slice(None)
        mine, across = self.columns(place.slab), self.columns(place.x_slab)
        self.first_x.wait_recv()
        self.last_y = [
            self.move(place.over_y, every, place.y, 0, every, mine),
            self.move(place.over_y, every, place.y, 0, every, across),
        ]
        self.first_y.wait_recv()
        self.last_x = [self.move(place.over_x, every, every, 1, every, mine)]

    def fourth(self):
        place, every = self.place, slice(None)
        mine, across = self.columns(place.slab), self.columns(place.x_slab)
        wait_all(self.last_y)
        self.over_core = [
            self.move(place.over_core, every, every, 0, every, mine),
            self.move(place.over_core, every, every, 0, every, across),
        ]
        wait_all(self.last_x)
        self.over_core += [
            self.move(place.over_core, every, every, 1, every, mine),
            self.move(place.over_core, every, every, 1, every, across),
        ]

    def end(self):
        wait_all(self.over_core)


def gather_copies(place, clip_size):
    return 2 * (place - 1) + 9


def add_into(held, index, arrived, arrived_index):
    lead = arrived.shape[len(arrived_index) : -2]
    for at in itertools.product(*[range(n) for n in lead]):
        total = held[index + at].astype(jnp.float32) + arrived[arrived_index + at].astype(jnp.float32)
        held[index + at] = total.astype(jnp.bfloat16)


class Scatter:
    def __init__(self, place, links, held, from_core, first_y, first_x, last_x, last_y, from_z):
        self.place, self.links, self.held = place, links, held
        self.from_core, self.first_y, self.first_x = from_core, first_y, first_x
        self.last_x, self.last_y, self.from_z = last_x, last_y, from_z

    def begin(self):
        place = self.place
        self.copies = [
            self.links.send(
                self.held.at[2 * x + 1 - place.core], self.from_core.at[x], place.over_core
            )
            for x in range(2)
        ]

    def second(self):
        place = self.place
        for x in range(2):
            self.copies[x].wait_recv()
            add_into(self.held, (2 * x + place.core,), self.from_core, (x,))
        self.copies_a = [
            self.links.send(
                self.held.at[2 * x + place.core, 1 - place.y, 0], self.first_y.at[x], place.over_y
            )
            for x in range(2)
        ]
        self.copies_b = [
            self.links.send(
                self.held.at[place.x_slab, y, 1], self.first_x.at[y], place.over_x
            )
            for y in range(2)
        ]

    def third(self):
        place = self.place
        for x in range(2):
            self.copies_a[x].wait_recv()
            add_into(self.held, (2 * x + place.core, place.y, 0), self.first_y, (x,))
        self.copy_a = self.links.send(
            self.held.at[place.x_slab, place.y, 0], self.last_x, place.over_x
        )
        for y in range(2):
            self.copies_b[y].wait_recv()
            add_into(self.held, (place.slab, y, 1), self.first_x, (y,))
        self.copy_b = self.links.send(
            self.held.at[place.slab, 1 - place.y, 1], self.last_y, place.over_y
        )

    def fourth(self):
        place = self.place
        self.copies = []
        for half, copy, arrived in ((0, self.copy_a, self.last_x), (1, self.copy_b, self.last_y)):
            copy.wait_recv()
            add_into(self.held, (place.slab, place.y, half), arrived, ())
            self.copies.append([
                self.links.send(
                    self.held.at[place.slab, place.y, half, place.z_at(step)],
                    self.from_z.at[half, step - 1],
                    place.over_z(step),
                )
                for step in range(1, place.depth)
            ])

    def end(self):
        place, parts = self.place, []
        for half in range(2):
            total = self.held[place.slab, place.y, half, place.z].astype(jnp.float32)
            for step in range(1, place.depth):
                self.copies[half][step - 1].wait_recv()
                total += self.from_z[half, step - 1].astype(jnp.float32)
            parts.append(total)
        return parts


class Small:
    def __init__(self, place, links, held, arrived, line):
        self.place, self.links, self.held = place, links, held
        self.arrived, self.line = arrived, line

    def begin(self):
        self.copy = self.links.send(self.held.at[0], self.arrived.at[0], self.place.over_core)

    def second(self):
        self.copy.wait_recv()
        self.held[1] = self.held[0] + self.arrived[0]
        self.copy = self.links.send(self.held.at[1], self.arrived.at[1], self.place.over_x)

    def third(self):
        self.copy.wait_recv()
        self.held[2] = self.held[1] + self.arrived[1]
        self.copy = self.links.send(self.held.at[2], self.arrived.at[2], self.place.over_y)

    def fourth(self):
        place = self.place
        self.copy.wait_recv()
        self.line[place.z] = self.held[2] + self.arrived[2]
        self.copies = [
            self.links.send(self.line.at[place.z], self.line.at[place.z], place.over_z(step))
            for step in range(1, place.depth)
        ]

    def end(self):
        wait_all(self.copies)
        total = self.line[0]
        for z in range(1, self.place.depth):
            total += self.line[z]
        return total


def gather_kernel(clip_size, *refs):
    masters, wholes = refs[:4], refs[4:8]
    place, links = Place(clip_size), Links(*refs[8:])
    place.greet()
    flows = [
        Gather(place, links, whole, master.shape[1]) for master, whole in zip(masters, wholes)
    ]
    for stage in ("begin", "second", "third", "fourth", "end"):
        for position, flow in enumerate(flows):
            if stage == "begin":
                flow.begin(masters[position])
            else:
                getattr(flow, stage)()
    links.drain()


def gather_all(masters, clip_size):
    vmem = pl.BlockSpec(memory_space=pltpu.VMEM)
    depth = clip_size // 2
    shapes = [
        jax.ShapeDtypeStruct((depth, 2, 2, m.shape[0] // 2, 4 * m.shape[1]), jnp.bfloat16)
        for m in masters
    ]
    copies = 4 * (2 * (depth - 1) + 9)
    wholes = pl.pallas_call(
        functools.partial(gather_kernel, clip_size),
        out_shape=shapes,
        in_specs=[vmem] * 4,
        out_specs=[vmem] * 4,
        scratch_shapes=[pltpu.SemaphoreType.DMA((copies,)), pltpu.SemaphoreType.DMA((copies,))],
        compiler_params=pltpu.CompilerParams(
            collective_id=0, has_side_effects=True, vmem_limit_bytes=48 << 20
        ),
        name="gather_weights",
    )(*masters)
    return [w.reshape(-1, w.shape[-1]) for w in wholes]


def scatter_kernel(clip_size, shapes, *refs):
    small_in, helds_in = refs[0], refs[1:5]
    small_out, outs = refs[5], refs[6:10]
    rest = list(refs[10:])
    place = Place(clip_size)
    links = Links(rest.pop(0), rest.pop(0))
    place.greet()
    small = Small(place, links, rest.pop(0), rest.pop(0), rest.pop(0))
    small.held[0] = small_in[...]
    flows = []
    loads = rest.pop(0)
    for position, source in enumerate(helds_in):
        held = rest.pop(0)
        load = pltpu.make_async_copy(source, held, loads.at[position])
        load.start()
        flows.append(Scatter(place, links, held, *[rest.pop(0) for _ in range(6)]))
        flows[-1].load = load
    for flow in flows:
        flow.load.wait()
    flows = [small] + flows
    for stage in ("begin", "second", "third", "fourth"):
        for flow in flows:
            getattr(flow, stage)()
    small_out[...] = small.end()
    for flow, out in zip(flows[1:], outs):
        first, last = flow.end()
        rows = first.shape[0]
        out[:rows, :] = first
        out[rows:, :] = last
    links.drain()


def scatter_buffers(shape):
    slabs, _, _, depth, rows, columns = shape
    return [
        pltpu.VMEM((2, 2, 2, depth, rows, columns), jnp.bfloat16),
        pltpu.VMEM((2, depth, rows, columns), jnp.bfloat16),
        pltpu.VMEM((2, depth, rows, columns), jnp.bfloat16),
        pltpu.VMEM((depth, rows, columns), jnp.bfloat16),
        pltpu.VMEM((depth, rows, columns), jnp.bfloat16),
        pltpu.VMEM((2, depth - 1, rows, columns), jnp.bfloat16),
    ]


def scatter_all(small, grads, clip_size):
    vmem = pl.BlockSpec(memory_space=pltpu.VMEM)
    depth = clip_size // 2
    helds = []
    for grad in grads:
        rows, columns = grad.shape[0] // clip_size // 2, grad.shape[1] // 4
        held = grad.reshape(depth, 2, 2, rows, 4, columns).transpose(4, 1, 2, 0, 3, 5)
        helds.append(held.astype(jnp.bfloat16))
    copies = 4 * (2 + 4 + 2 + 2 * (depth - 1)) + 3 + depth - 1
    scratch = [
        pltpu.SemaphoreType.DMA((copies,)),
        pltpu.SemaphoreType.DMA((copies,)),
        pltpu.VMEM((3,) + small.shape, jnp.float32),
        pltpu.VMEM((3,) + small.shape, jnp.float32),
        pltpu.VMEM((depth,) + small.shape, jnp.float32),
        pltpu.SemaphoreType.DMA((4,)),
    ]
    for held in helds:
        scratch += [pltpu.VMEM(held.shape, held.dtype)] + scatter_buffers(held.shape)
    return pl.pallas_call(
        functools.partial(scatter_kernel, clip_size, [h.shape for h in helds]),
        out_shape=[jax.ShapeDtypeStruct(small.shape, jnp.float32)]
        + [jax.ShapeDtypeStruct((2 * h.shape[4], h.shape[5]), jnp.float32) for h in helds],
        in_specs=[vmem] + [pl.BlockSpec(memory_space=pl.ANY)] * 4,
        out_specs=[vmem] * 5,
        scratch_shapes=scratch,
        compiler_params=pltpu.CompilerParams(
            collective_id=1, has_side_effects=True, vmem_limit_bytes=48 << 20
        ),
        name="scatter_grads",
    )(small, *helds)


def shards(
    tokens,
    y_grad,
    clip_rows,
    qkv_weight,
    proj_weight,
    up_weight,
    down_weight,
    qkv_m,
    proj_m,
    up_m,
    down_m,
    qkv_v,
    proj_v,
    up_v,
    down_v,
    vectors,
    vectors_m,
    vectors_v,
    table,
    table_m,
    table_v,
):
    lengths = clip_rows[0]
    slab_count = lax.axis_size("slab")
    inputs = tokens[0, 0].astype(jnp.float32)
    tok_count, width = inputs.shape
    rows_dev = tok_count // BINS
    head_dim = width // HEADS
    score_scale = head_dim ** (-0.5)
    source, time_wraps, seg_starts = window_rows(
        lengths, lax.axis_index("slab"), slab_count, rows_dev
    )
    total_rows = rows_dev + 2 * lengths.shape[0]
    head_rows = jnp.minimum(
        seg_starts[:, None] + jnp.arange(2, dtype=jnp.int32)[None, :], rows_dev - 1
    ).reshape(-1)
    windows_count = source.shape[0] * (BINS // WIN)
    bin_folds = jnp.arange(windows_count) % (BINS // WIN) == BINS // WIN - 1
    allowed = window_mask(jnp.repeat(time_wraps, BINS // WIN), bin_folds)[:, None]
    offset_hot = offset_table()
    rel_bias = (
        jnp.dot(offset_hot, table, precision=HIGHEST)
        .reshape(WIN * WIN, WIN * WIN, HEADS)
        .transpose(2, 0, 1)
    )
    used_rows = jnp.sum(lengths) // slab_count
    live_rows = (jnp.arange(tok_count) // BINS < used_rows).astype(jnp.float32)[:, None]
    masters = (qkv_weight, proj_weight, up_weight, down_weight)
    clip_size = lax.axis_size("clip")
    aligned = slab_count == 4 and clip_size % 2 == 0 and all(m.shape[0] % 32 == 0 for m in masters)
    if aligned:
        copies = gather_all(masters, clip_size)
    else:
        part_copies = (
            lax.all_gather(qkv_weight.astype(jnp.bfloat16), "clip", axis=0, tiled=True),
            lax.all_gather(proj_weight.astype(jnp.bfloat16), "clip", axis=0, tiled=True),
            lax.all_gather(up_weight.astype(jnp.bfloat16), "clip", axis=0, tiled=True),
            lax.all_gather(down_weight.astype(jnp.bfloat16), "clip", axis=0, tiled=True),
        )
        copies = (
            lax.all_gather(part_copies[0], "slab", axis=1, tiled=True),
            lax.all_gather(part_copies[1], "slab", axis=1, tiled=True),
            lax.all_gather(part_copies[2], "slab", axis=1, tiled=True),
            lax.all_gather(part_copies[3], "slab", axis=1, tiled=True),
        )
    qkv_copy, proj_copy, up_copy, down_copy = copies
    attn_input = affine_norm(inputs, vectors[0], vectors[1]).astype(jnp.bfloat16)
    bias_row = jnp.concatenate([vectors[2], jnp.zeros_like(vectors[2]), vectors[3]])
    qkv_rows = (
        jnp.dot(attn_input, qkv_copy, preferred_element_type=jnp.float32) + bias_row
    ).astype(jnp.bfloat16)
    qkv_grid = qkv_rows.reshape(rows_dev, BINS, 3 * width)
    borrowed = from_behind(qkv_grid[head_rows], "slab", -1)
    qkv_windows = to_windows(jnp.concatenate([qkv_grid, borrowed], 0), source)
    query_win = qkv_windows[:, :, :width].reshape(windows_count, WIN * WIN, HEADS, head_dim)
    key_win = qkv_windows[:, :, width : 2 * width].reshape(
        windows_count, WIN * WIN, HEADS, head_dim
    )
    value_win = qkv_windows[:, :, 2 * width :].reshape(windows_count, WIN * WIN, HEADS, head_dim)

    def scores_of(queries, keys_all):
        raw = (
            jnp.einsum("wqhd,wkhd->whqk", queries, keys_all, preferred_element_type=jnp.float32)
            * score_scale
            + rel_bias[None]
        )
        return jnp.where(allowed, raw, masked_score)

    scores = scores_of(query_win, key_win)
    top_score = jnp.max(scores, -1, keepdims=True)
    exp_sum = jnp.sum(jnp.exp(scores - top_score), -1, keepdims=True)
    probs_low = (jnp.exp(scores - top_score) / exp_sum).astype(jnp.bfloat16)
    attended = jnp.einsum(
        "whqk,wkhd->wqhd", probs_low, value_win, preferred_element_type=jnp.float32
    )
    attended = attended.astype(jnp.bfloat16).reshape(windows_count, WIN * WIN, width)
    spread_out = from_windows(attended, source, total_rows)
    returned = from_behind(spread_out[rows_dev:], "slab", 1)
    attended_rows = spread_out[:rows_dev].at[head_rows].add(returned).reshape(tok_count, width)
    residual = (
        inputs + jnp.dot(attended_rows, proj_copy, preferred_element_type=jnp.float32) + vectors[4]
    )
    mlp_input = affine_norm(residual, vectors[5], vectors[6]).astype(jnp.bfloat16)
    pre_gelu = jnp.dot(mlp_input, up_copy, preferred_element_type=jnp.float32) + vectors[
        8:
    ].reshape(-1)
    activated, gelu_pull = jax.vjp(gelu_exact, pre_gelu)
    activated_low = activated.astype(jnp.bfloat16)
    block_out = (
        residual
        + jnp.dot(activated_low, down_copy, preferred_element_type=jnp.float32)
        + vectors[7]
    ) * live_rows
    out_grad = y_grad[0, 0].astype(jnp.float32) * live_rows
    out_low = out_grad.astype(jnp.bfloat16)
    down_grad = jnp.dot(activated_low.T, out_low, preferred_element_type=jnp.float32)
    act_grad = jnp.dot(out_low, down_copy.T, preferred_element_type=jnp.float32)
    pre_low = gelu_pull(act_grad)[0].astype(jnp.bfloat16)
    up_grad = jnp.dot(mlp_input.T, pre_low, preferred_element_type=jnp.float32)
    mlp_in_grad = jnp.dot(pre_low, up_copy.T, preferred_element_type=jnp.float32)
    norm_value, norm_pull = jax.vjp(affine_norm, residual, vectors[5], vectors[6])
    resid_norm_grad, gain_two_grad, shift_two_grad = norm_pull(mlp_in_grad)
    resid_grad = out_grad + resid_norm_grad
    attn_low = resid_grad.astype(jnp.bfloat16)
    proj_grad = jnp.dot(attended_rows.T, attn_low, preferred_element_type=jnp.float32)
    mixed_grad = jnp.dot(attn_low, proj_copy.T, preferred_element_type=jnp.float32).astype(
        jnp.bfloat16
    )
    mixed_grid = mixed_grad.reshape(rows_dev, BINS, width)
    sent_back = from_behind(mixed_grid[head_rows], "slab", -1)
    grad_windows = to_windows(jnp.concatenate([mixed_grid, sent_back], 0), source)
    grad_windows = grad_windows.reshape(windows_count, WIN * WIN, HEADS, head_dim)
    probs = jnp.exp(scores_of(query_win, key_win) - top_score) / exp_sum
    prob_grad = jnp.einsum(
        "wqhd,wkhd->whqk", grad_windows, value_win, preferred_element_type=jnp.float32
    )
    value_grad = jnp.einsum(
        "whqk,wqhd->wkhd", probs_low, grad_windows, preferred_element_type=jnp.float32
    )
    score_grad = (probs * (prob_grad - jnp.sum(probs * prob_grad, -1, keepdims=True))).astype(
        jnp.bfloat16
    )
    bias_grad = (
        jnp.sum(score_grad.astype(jnp.float32), 0)
        .transpose(1, 2, 0)
        .reshape(WIN * WIN * WIN * WIN, HEADS)
    )
    table_grad = jnp.dot(offset_hot.T, bias_grad, precision=HIGHEST)
    query_grad = (
        jnp.einsum("whqk,wkhd->wqhd", score_grad, key_win, preferred_element_type=jnp.float32)
        * score_scale
    )
    key_grad = (
        jnp.einsum("whqk,wqhd->wkhd", score_grad, query_win, preferred_element_type=jnp.float32)
        * score_scale
    )
    qkv_grad_win = jnp.concatenate(
        [
            query_grad.reshape(windows_count, WIN * WIN, width),
            key_grad.reshape(windows_count, WIN * WIN, width),
            value_grad.reshape(windows_count, WIN * WIN, width),
        ],
        -1,
    ).astype(jnp.bfloat16)
    qkv_spread = from_windows(qkv_grad_win, source, total_rows)
    given_back = from_behind(qkv_spread[rows_dev:], "slab", 1)
    qkv_grad_rows = (
        qkv_spread[:rows_dev].at[head_rows].add(given_back).reshape(tok_count, 3 * width)
    )
    qkv_w_grad = jnp.dot(attn_input.T, qkv_grad_rows, preferred_element_type=jnp.float32)
    bias_sums = jnp.sum(qkv_grad_rows.astype(jnp.float32), 0)
    attn_in_grad = jnp.dot(qkv_grad_rows, qkv_copy.T, preferred_element_type=jnp.float32)
    first_value, norm_pull_one = jax.vjp(affine_norm, inputs, vectors[0], vectors[1])
    inputs_norm_grad, gain_one_grad, shift_one_grad = norm_pull_one(attn_in_grad)
    x_grad = resid_grad + inputs_norm_grad
    vector_grad = jnp.concatenate(
        [
            jnp.stack(
                [
                    gain_one_grad,
                    shift_one_grad,
                    bias_sums[:width],
                    bias_sums[2 * width :],
                    jnp.sum(attn_low.astype(jnp.float32), 0),
                    gain_two_grad,
                    shift_two_grad,
                    jnp.sum(out_grad, 0),
                ]
            ),
            jnp.sum(pre_low.astype(jnp.float32), 0).reshape(-1, width),
        ],
        0,
    )
    grad_scale = float(tok_count * slab_count * lax.axis_size("clip")) ** (-0.5)
    if aligned:
        size = vector_grad.size + table_grad.size
        flat = jnp.concatenate([vector_grad.reshape(-1), table_grad.reshape(-1)]) * grad_scale
        flat = jnp.pad(flat, (0, -size % (8 * width))).reshape(-1, width)
        grads = [g * grad_scale for g in (qkv_w_grad, proj_grad, up_grad, down_grad)]
        summed, *owned = scatter_all(flat, grads, clip_size)
        summed = summed.reshape(-1)
        small_sums = (
            summed[: vector_grad.size].reshape(vector_grad.shape),
            summed[vector_grad.size : size].reshape(table_grad.shape),
        )
    else:
        part_sums = (
            lax.psum_scatter(
                (qkv_w_grad * grad_scale).astype(jnp.bfloat16), "slab", scatter_dimension=1, tiled=True
            ).astype(jnp.float32),
            lax.psum_scatter(
                (proj_grad * grad_scale).astype(jnp.bfloat16), "slab", scatter_dimension=1, tiled=True
            ).astype(jnp.float32),
            lax.psum_scatter(
                (up_grad * grad_scale).astype(jnp.bfloat16), "slab", scatter_dimension=1, tiled=True
            ).astype(jnp.float32),
            lax.psum_scatter(
                (down_grad * grad_scale).astype(jnp.bfloat16), "slab", scatter_dimension=1, tiled=True
            ).astype(jnp.float32),
        )
        owned = (
            lax.psum_scatter(part_sums[0], "clip", scatter_dimension=0, tiled=True),
            lax.psum_scatter(part_sums[1], "clip", scatter_dimension=0, tiled=True),
            lax.psum_scatter(part_sums[2], "clip", scatter_dimension=0, tiled=True),
            lax.psum_scatter(part_sums[3], "clip", scatter_dimension=0, tiled=True),
        )
        small_sums = lax.psum((vector_grad * grad_scale, table_grad * grad_scale), ("slab", "clip"))
    qkv_new, qkv_m_new, qkv_v_new = adamw(
        qkv_weight, qkv_m, qkv_v, owned[0], rate_matrix, weight_decay
    )
    proj_new, proj_m_new, proj_v_new = adamw(
        proj_weight, proj_m, proj_v, owned[1], rate_matrix, weight_decay
    )
    up_new, up_m_new, up_v_new = adamw(up_weight, up_m, up_v, owned[2], rate_matrix, weight_decay)
    down_new, down_m_new, down_v_new = adamw(
        down_weight, down_m, down_v, owned[3], rate_matrix, weight_decay
    )
    vectors_new, vectors_m_new, vectors_v_new = adamw(
        vectors, vectors_m, vectors_v, small_sums[0], rate_vector, 0.0
    )
    table_new, table_m_new, table_v_new = adamw(
        table, table_m, table_v, small_sums[1], rate_vector, 0.0
    )
    out_shape = (1, 1, tok_count, width)
    return (
        block_out.astype(jnp.bfloat16).reshape(out_shape),
        x_grad.reshape(out_shape),
        qkv_new,
        qkv_m_new,
        qkv_v_new,
        proj_new,
        proj_m_new,
        proj_v_new,
        up_new,
        up_m_new,
        up_v_new,
        down_new,
        down_m_new,
        down_v_new,
        vectors_new,
        vectors_m_new,
        vectors_v_new,
        table_new,
        table_m_new,
        table_v_new,
    )


def solution(mesh):
    return jax.shard_map(
        shards,
        mesh=mesh,
        in_specs=(
            P("clip", "slab", None, None),
            P("clip", "slab", None, None),
            P("clip", None),
            P("clip", "slab"),
            P("clip", "slab"),
            P("clip", "slab"),
            P("clip", "slab"),
            P("clip", "slab"),
            P("clip", "slab"),
            P("clip", "slab"),
            P("clip", "slab"),
            P("clip", "slab"),
            P("clip", "slab"),
            P("clip", "slab"),
            P("clip", "slab"),
            P(),
            P(),
            P(),
            P(),
            P(),
            P(),
        ),
        out_specs=(
            P("clip", "slab", None, None),
            P("clip", "slab", None, None),
            P("clip", "slab"),
            P("clip", "slab"),
            P("clip", "slab"),
            P("clip", "slab"),
            P("clip", "slab"),
            P("clip", "slab"),
            P("clip", "slab"),
            P("clip", "slab"),
            P("clip", "slab"),
            P("clip", "slab"),
            P("clip", "slab"),
            P("clip", "slab"),
            P(),
            P(),
            P(),
            P(),
            P(),
            P(),
        ),
        check_vma=False,
    )
```

```python
import functools
import itertools
import math
import typing

import jax
import jax.numpy as jnp
from jax import lax
from jax.experimental import pallas as pl
from jax.experimental.pallas import tpu as pltpu
from jax.sharding import PartitionSpec as P

HEADS = 16
BINS = 8
WIN = 4
STEP = 10
RELS = 49
SLAB, CLIP = "slab", "clip"
SHORT = 64


HIGHEST = lax.Precision.HIGHEST
norm_epsilon = 1e-06
beta_first = 0.5
beta_second = 0.5
adam_epsilon = 1e-08
rate_matrix = 0.05
rate_vector = 0.5
weight_decay = 0.05
masked_score = -1e30


def from_behind(block, axis, distance):
    devices = range(lax.axis_size(axis))
    route = [((i - distance) % len(devices), i) for i in devices]
    return lax.ppermute(block, axis, route)


def layer_norm(values):
    center = values - jnp.mean(values, -1, keepdims=True)
    spread = jnp.mean(center * center, -1, keepdims=True)
    return center * lax.rsqrt(spread + norm_epsilon)


def affine_norm(values, gain, offset):
    return layer_norm(values) * gain + offset


def gelu_exact(values):
    return jax.nn.gelu(values, approximate=False)


def window_rows(lengths, slab_index, slab_count, rows_dev):
    segment = lengths // slab_count
    seg_ends = jnp.cumsum(segment)
    seg_starts = seg_ends - segment
    row_base = WIN * jnp.arange(rows_dev // WIN, dtype=jnp.int32)
    inside = (row_base[:, None] >= seg_starts[None, :]) & (row_base[:, None] < seg_ends[None, :])
    in_clip = jnp.any(inside, axis=1)
    slot_ids = jnp.arange(lengths.shape[0], dtype=jnp.int32)
    clip_end = jnp.sum(jnp.where(inside, seg_ends[None, :], 0), axis=1)
    clip_slot = jnp.sum(jnp.where(inside, slot_ids[None, :], 0), axis=1)
    row_ids = (
        row_base[:, None]
        + jnp.where(in_clip, WIN // 2, 0)[:, None]
        + jnp.arange(WIN, dtype=jnp.int32)[None, :]
    )
    beyond = in_clip[:, None] & (row_ids >= clip_end[:, None])
    source = jnp.where(
        beyond, rows_dev + 2 * clip_slot[:, None] + row_ids - clip_end[:, None], row_ids
    )
    time_wraps = in_clip & (row_base + WIN == clip_end) & (slab_index == slab_count - 1)
    return (source, time_wraps, seg_starts)


def window_mask(time_wraps, bin_folds):
    positions = jnp.arange(WIN * WIN, dtype=jnp.int32)
    row_half = positions // WIN >= WIN // 2
    bin_half = positions % WIN >= WIN // 2
    same_row = row_half[:, None] == row_half[None, :]
    same_bin = bin_half[:, None] == bin_half[None, :]
    return (~time_wraps[:, None, None] | same_row[None]) & (
        ~bin_folds[:, None, None] | same_bin[None]
    )


def offset_table():
    positions = jnp.arange(WIN * WIN, dtype=jnp.int32)
    row_pos = positions // WIN
    bin_pos = positions % WIN
    offsets = (row_pos[:, None] - row_pos[None, :] + WIN - 1) * (2 * WIN - 1) + (
        bin_pos[:, None] - bin_pos[None, :] + WIN - 1
    )
    return (offsets.reshape(-1)[:, None] == jnp.arange(RELS, dtype=jnp.int32)[None, :]).astype(
        jnp.float32
    )


def to_windows(extended, source):
    gathered = jnp.roll(extended[source], -(WIN // 2), axis=2)
    win_rows = source.shape[0]
    width = extended.shape[-1]
    gathered = gathered.reshape(win_rows, WIN, BINS // WIN, WIN, width).transpose(0, 2, 1, 3, 4)
    return gathered.reshape(win_rows * (BINS // WIN), WIN * WIN, width)


def from_windows(windows, source, total_rows):
    win_rows = source.shape[0]
    width = windows.shape[-1]
    placed = windows.reshape(win_rows, BINS // WIN, WIN, WIN, width).transpose(0, 2, 1, 3, 4)
    placed = jnp.roll(placed.reshape(win_rows, WIN, BINS, width), WIN // 2, axis=2)
    blank = jnp.zeros((total_rows, BINS, width), windows.dtype)
    return blank.at[source.reshape(-1)].set(placed.reshape(win_rows * WIN, BINS, width))


def adamw(weight, first, second, grad, rate, decay):
    first = beta_first * first + (1.0 - beta_first) * grad
    second = beta_second * second + (1.0 - beta_second) * grad * grad
    fix_first = 1.0 - beta_first**STEP
    fix_second = 1.0 - beta_second**STEP
    update = first / fix_first / (jnp.sqrt(second / fix_second) + adam_epsilon)
    return (weight - rate * (update + decay * weight), first, second)


MESH = pl.DeviceIdType.MESH


class Links:
    def __init__(self, send_sems, recv_sems):
        self.send_sems, self.recv_sems = send_sems, recv_sems
        self.count, self.started = 0, []

    def send(self, source, target, device):
        copy = pltpu.make_async_remote_copy(
            src_ref=source,
            dst_ref=target,
            send_sem=self.send_sems.at[self.count],
            recv_sem=self.recv_sems.at[self.count],
            device_id=device,
            device_id_type=MESH,
        )
        copy.start()
        self.count += 1
        self.started.append(copy)
        return copy

    def drain(self):
        for copy in self.started:
            copy.wait_send()


class Place:
    def __init__(self, clip_size):
        self.slab, self.clip = lax.axis_index(SLAB), lax.axis_index(CLIP)
        self.x, self.core = self.slab // 2, self.slab % 2
        self.z, self.y = self.clip // 2, self.clip % 2
        self.depth = clip_size // 2
        self.over_core = (self.x * 2 + 1 - self.core, self.clip)
        self.over_x = ((1 - self.x) * 2 + self.core, self.clip)
        self.over_y = (self.slab, self.z * 2 + 1 - self.y)
        self.over_diagonal = ((1 - self.x) * 2 + 1 - self.core, self.clip)
        self.x_slab = (1 - self.x) * 2 + self.core
        self.core_slab = self.x * 2 + 1 - self.core

    def z_at(self, step):
        return lax.rem(self.z + step, self.depth)

    def over_z(self, step):
        return (self.slab, self.z_at(step) * 2 + self.y)

    def greet(self):
        barrier = pltpu.get_barrier_semaphore()
        partners = [self.over_core, self.over_x, self.over_y, self.over_diagonal]
        partners += [self.over_z(step) for step in range(1, self.depth)]
        for partner in partners:
            pl.semaphore_signal(barrier, inc=1, device_id=partner, device_id_type=MESH)
        pl.semaphore_wait(barrier, len(partners))


def wait_all(copies):
    for copy in copies:
        copy.wait_recv()


class Gather:
    def __init__(self, place, links, whole, width):
        self.place, self.links, self.whole, self.width = place, links, whole, width

    def columns(self, slab):
        return pl.ds(pl.multiple_of(slab * self.width, 128), self.width)

    def move(self, device, *index):
        block = self.whole.at[index]
        return self.links.send(block, block, device)

    def begin(self, master):
        place = self.place
        rows = self.whole.shape[3]
        for half in range(2):
            self.whole[place.z, place.y, half, :, self.columns(place.slab)] = master[
                half * rows : (half + 1) * rows, :
            ].astype(jnp.bfloat16)
        self.over_z = [
            [
                self.move(
                    place.over_z(step), place.z, place.y, half, slice(None), self.columns(place.slab)
                )
                for step in range(1, place.depth)
            ]
            for half in range(2)
        ]

    def second(self):
        place, every = self.place, slice(None)
        mine = self.columns(place.slab)
        wait_all(self.over_z[0])
        self.first_x = self.move(place.over_x, every, place.y, 0, every, mine)
        wait_all(self.over_z[1])
        self.first_y = self.move(place.over_y, every, place.y, 1, every, mine)

    def third(self):
        place, every = self.place, slice(None)
        mine, across = self.columns(place.slab), self.columns(place.x_slab)
        self.first_x.wait_recv()
        self.last_y = [
            self.move(place.over_y, every, place.y, 0, every, mine),
            self.move(place.over_y, every, place.y, 0, every, across),
        ]
        self.first_y.wait_recv()
        self.last_x = [self.move(place.over_x, every, every, 1, every, mine)]

    def fourth(self):
        place, every = self.place, slice(None)
        mine, across = self.columns(place.slab), self.columns(place.x_slab)
        wait_all(self.last_y)
        self.over_core = [
            self.move(place.over_core, every, every, 0, every, mine),
            self.move(place.over_core, every, every, 0, every, across),
        ]
        wait_all(self.last_x)
        self.over_core += [
            self.move(place.over_core, every, every, 1, every, mine),
            self.move(place.over_core, every, every, 1, every, across),
        ]

    def end(self):
        wait_all(self.over_core)


def add_into(held, index, arrived, arrived_index):
    lead = arrived.shape[len(arrived_index) : -2]
    for at in itertools.product(*[range(n) for n in lead]):
        total = held[index + at].astype(jnp.float32) + arrived[arrived_index + at].astype(jnp.float32)
        held[index + at] = total.astype(jnp.bfloat16)


class Scatter:
    def __init__(self, place, links, held, from_core, first_y, first_x, last_x, last_y, from_z):
        self.place, self.links, self.held = place, links, held
        self.from_core, self.first_y, self.first_x = from_core, first_y, first_x
        self.last_x, self.last_y, self.from_z = last_x, last_y, from_z

    def begin(self):
        place = self.place
        self.copies = [
            self.links.send(
                self.held.at[2 * x + 1 - place.core], self.from_core.at[x], place.over_core
            )
            for x in range(2)
        ]

    def second(self):
        place = self.place
        for x in range(2):
            self.copies[x].wait_recv()
            add_into(self.held, (2 * x + place.core,), self.from_core, (x,))
        self.copies_a = [
            self.links.send(
                self.held.at[2 * x + place.core, 1 - place.y, 0], self.first_y.at[x], place.over_y
            )
            for x in range(2)
        ]
        self.copies_b = [
            self.links.send(
                self.held.at[place.x_slab, y, 1], self.first_x.at[y], place.over_x
            )
            for y in range(2)
        ]

    def third(self):
        place = self.place
        for x in range(2):
            self.copies_a[x].wait_recv()
            add_into(self.held, (2 * x + place.core, place.y, 0), self.first_y, (x,))
        self.copy_a = self.links.send(
            self.held.at[place.x_slab, place.y, 0], self.last_x, place.over_x
        )
        for y in range(2):
            self.copies_b[y].wait_recv()
            add_into(self.held, (place.slab, y, 1), self.first_x, (y,))
        self.copy_b = self.links.send(
            self.held.at[place.slab, 1 - place.y, 1], self.last_y, place.over_y
        )

    def fourth(self):
        place = self.place
        self.copies = []
        for half, copy, arrived in ((0, self.copy_a, self.last_x), (1, self.copy_b, self.last_y)):
            copy.wait_recv()
            add_into(self.held, (place.slab, place.y, half), arrived, ())
            self.copies.append([
                self.links.send(
                    self.held.at[place.slab, place.y, half, place.z_at(step)],
                    self.from_z.at[half, step - 1],
                    place.over_z(step),
                )
                for step in range(1, place.depth)
            ])

    def end(self):
        place, parts = self.place, []
        for half in range(2):
            total = self.held[place.slab, place.y, half, place.z].astype(jnp.float32)
            for step in range(1, place.depth):
                self.copies[half][step - 1].wait_recv()
                total += self.from_z[half, step - 1].astype(jnp.float32)
            parts.append(total)
        return parts


class Small:
    def __init__(self, place, links, held, arrived, line):
        self.place, self.links, self.held = place, links, held
        self.arrived, self.line = arrived, line

    def begin(self):
        self.copy = self.links.send(self.held.at[0], self.arrived.at[0], self.place.over_core)

    def second(self):
        self.copy.wait_recv()
        self.held[1] = self.held[0] + self.arrived[0]
        self.copy = self.links.send(self.held.at[1], self.arrived.at[1], self.place.over_x)

    def third(self):
        self.copy.wait_recv()
        self.held[2] = self.held[1] + self.arrived[1]
        self.copy = self.links.send(self.held.at[2], self.arrived.at[2], self.place.over_y)

    def fourth(self):
        place = self.place
        self.copy.wait_recv()
        self.line[place.z] = self.held[2] + self.arrived[2]
        self.copies = [
            self.links.send(self.line.at[place.z], self.line.at[place.z], place.over_z(step))
            for step in range(1, place.depth)
        ]

    def end(self):
        wait_all(self.copies)
        total = self.line[0]
        for z in range(1, self.place.depth):
            total += self.line[z]
        return total


def scatter_buffers(shape):
    slabs, _, _, depth, rows, columns = shape
    return [
        pltpu.VMEM((2, 2, 2, depth, rows, columns), jnp.bfloat16),
        pltpu.VMEM((2, depth, rows, columns), jnp.bfloat16),
        pltpu.VMEM((2, depth, rows, columns), jnp.bfloat16),
        pltpu.VMEM((depth, rows, columns), jnp.bfloat16),
        pltpu.VMEM((depth, rows, columns), jnp.bfloat16),
        pltpu.VMEM((2, depth - 1, rows, columns), jnp.bfloat16),
    ]


def norm_parts(values):
    center = values - jnp.mean(values, -1, keepdims=True)
    inverse = lax.rsqrt(jnp.mean(center * center, -1, keepdims=True) + norm_epsilon)
    return center * inverse, inverse


def norm_back(normed, inverse, grad):
    return inverse * (
        grad
        - jnp.mean(grad, -1, keepdims=True)
        - normed * jnp.mean(grad * normed, -1, keepdims=True)
    )


def gelu_parts(values):
    below = 0.5 + 0.5 * lax.erf(values * (0.5**0.5))
    density = jnp.exp(-0.5 * values * values) * ((0.5 / math.pi) ** 0.5)
    return values * below, below + values * density


def mm(left, right):
    return jnp.dot(left, right, preferred_element_type=jnp.float32)


def mm_nt(left, right):
    return lax.dot_general(
        left, right, (((1,), (1,)), ((), ())), preferred_element_type=jnp.float32
    )


def mm_tn(left, right):
    return lax.dot_general(
        left, right, (((0,), (0,)), ((), ())), preferred_element_type=jnp.float32
    )


def span(index, size):
    return pl.ds(pl.multiple_of(index * size, size), size)


def blocks(ref, index, count):
    return jnp.concatenate([ref[index + k] for k in range(count)], 0)


def rows_of(ref, index, size):
    value = ref[span(index, size // ref.shape[1])]
    return value.reshape(size, value.shape[-1])


def put_rows(ref, index, value):
    count = value.shape[0] // ref.shape[1]
    ref[span(index, count)] = value.reshape(count, ref.shape[1], value.shape[-1])


def flat(ref, columns=slice(None)):
    block = ref[:, :, :, :, columns]
    return block.reshape(-1, block.shape[-1])


class Held(typing.NamedTuple):
    xb: typing.Any
    eb: typing.Any
    et: typing.Any
    attn_in: typing.Any
    attn_in_t: typing.Any
    own: typing.Any
    lent: typing.Any
    borrowed: typing.Any
    probs: typing.Any
    att_win: typing.Any
    att_out: typing.Any
    att_back: typing.Any
    att_rows: typing.Any
    att_t: typing.Any
    mid: typing.Any
    mlp_in: typing.Any
    mlp_in_t: typing.Any
    act: typing.Any
    slope: typing.Any
    mid_grad: typing.Any
    mid_low: typing.Any
    dwin_own: typing.Any
    dlent: typing.Any
    dborrowed: typing.Any
    qg_win: typing.Any
    qg_out: typing.Any
    qg_back: typing.Any
    qg_rows: typing.Any
    bias: typing.Any
    bias_grad: typing.Any
    up_sum: typing.Any
    att_sum: typing.Any
    out_low: typing.Any
    load_sems: typing.Any
    whole_qkv: typing.Any
    whole_proj: typing.Any
    whole_up: typing.Any
    whole_down: typing.Any


def block_kernel(slabs, clips, *refs):
    refs = list(refs)
    tokens, y_grad, units, vectors, table = refs[:5]
    masters = refs[5:9]
    block_out, x_grad, small_out = refs[9:12]
    owned = refs[12:16]
    rest = refs[16:]
    place = Place(clips)
    links = Links(rest.pop(0), rest.pop(0))
    s = Held(*rest[: len(Held._fields)])
    rest = rest[len(Held._fields) :]
    small = Small(place, links, rest.pop(0), rest.pop(0), rest.pop(0))
    flows = [Scatter(place, links, *[rest.pop(0) for _ in range(7)]) for _ in masters]
    qkv_flow, proj_flow, up_flow, down_flow = flows
    xb, eb, own, bias = s.xb, s.eb, s.own, s.bias
    tok, width = xb.shape
    unit = SHORT // slabs * BINS
    unit_count = tok // unit
    half = WIN // 2 * BINS
    per_unit = unit // half
    group = WIN * BINS
    head = width // HEADS
    pack = 128 // head
    tiles = width // 128
    score_scale = head**-0.5
    grad_scale = float(tok * slabs * clips) ** -0.5
    slots = s.lent.shape[0]

    loads = [
        pltpu.make_async_copy(tokens, xb, s.load_sems.at[0]),
        pltpu.make_async_copy(y_grad, eb, s.load_sems.at[1]),
    ]
    for load in loads:
        load.start()
    place.greet()
    gathers = [
        Gather(place, links, whole, master.shape[1])
        for whole, master in zip(
            (s.whole_qkv, s.whole_proj, s.whole_up, s.whole_down), masters
        )
    ]
    qkv_copy, proj_copy, up_copy, down_copy = gathers
    qkv_copy.begin(masters[0])

    heads = [units[HEADS_AT, i] for i in range(slots)]
    tails = [units[TAILS_AT, i] for i in range(slots)]
    used = units[USED_AT, 0]

    heads_of = lax.broadcasted_iota(jnp.int32, (HEADS, width), 1) // head
    spread = (heads_of == lax.broadcasted_iota(jnp.int32, (HEADS, width), 0)).astype(jnp.float32)
    by_offset = jnp.dot(table[...], spread, precision=HIGHEST)
    key = lax.broadcasted_iota(jnp.int32, (group, width), 0)
    query = lax.broadcasted_iota(jnp.int32, (group, width), 1) % group
    key_row, key_bin, query_row, query_bin = key // BINS, key % BINS, query // BINS, query % BINS
    key_place, query_place = (key_bin - WIN // 2) % BINS, (query_bin - WIN // 2) % BINS
    key_class = key_place // WIN + jnp.where(key_place >= WIN + WIN // 2, 1, 0)
    query_class = query_place // WIN + jnp.where(query_place >= WIN + WIN // 2, 1, 0)
    same = key_class == query_class
    offset = (query_row - key_row + WIN - 1) * (2 * WIN - 1) + query_place - key_place + WIN - 1
    offset = jnp.where(same, offset, -1)
    total = jnp.zeros((group, width), jnp.float32)
    for r in range(RELS):
        total = jnp.where(offset == r, by_offset[r : r + 1, :], total)
    total = jnp.where(same, total, masked_score)
    bias[0] = total
    bias[1] = jnp.where(key_row // (WIN // 2) == query_row // (WIN // 2), total, masked_score)
    lane = lax.broadcasted_iota(jnp.int32, (group, 128), 1) // head
    picks = [(lane == h).astype(jnp.bfloat16) for h in range(pack)]

    def stacked(block):
        return jnp.concatenate([block * pick for pick in picks], 0)

    def folded(block):
        result = block[(pack - 1) * group :]
        for h in range(pack - 2, -1, -1):
            result = jnp.where(lane == h, block[h * group : (h + 1) * group], result)
        return result

    loads[0].wait()
    chunk = 256

    @pl.loop(0, tok // chunk)
    def _(i):
        normed, _ = norm_parts(xb[span(i, chunk), :].astype(jnp.float32))
        low = (normed * vectors[0:1, :] + vectors[1:2, :]).astype(jnp.bfloat16)
        put_rows(s.attn_in, i, low)
        s.attn_in_t[:, span(i, chunk)] = low.T

    qkv_copy.second()
    proj_copy.begin(masters[1])
    up_copy.begin(masters[2])

    loads[1].wait()

    @pl.loop(0, tok // chunk)
    def _(i):
        live = lax.broadcasted_iota(jnp.int32, (chunk, width), 0) + i * chunk < used
        low = jnp.where(live, eb[span(i, chunk), :].astype(jnp.float32), 0.0)
        low = low.astype(jnp.bfloat16)
        eb[span(i, chunk), :] = low
        s.et[:, span(i, chunk)] = low.T

    qkv_copy.third()
    down_copy.begin(masters[3])
    proj_copy.second()
    qkv_copy.fourth()
    qkv_copy.end()
    up_copy.second()
    whole_qkv, whole_proj = s.whole_qkv, s.whole_proj
    whole_up, whole_down = s.whole_up, s.whole_down

    qkv_bias = jnp.concatenate(
        [vectors[2:3, :], jnp.zeros((1, width), jnp.float32), vectors[3:4, :]], 1
    )
    head_in = jnp.concatenate(
        [s.attn_in[heads[i]] for i in range(slots)], 0
    )
    put_rows(s.lent, 0, (mm(head_in, flat(whole_qkv)) + qkv_bias).astype(jnp.bfloat16))
    before = (lax.rem(place.slab + slabs - 1, slabs), place.clip)
    after = (lax.rem(place.slab + 1, slabs), place.clip)
    lend = links.send(s.lent, s.borrowed, before)

    @pl.loop(0, tok // chunk)
    def _(i):
        rows = mm(rows_of(s.attn_in, i, chunk), flat(whole_qkv)) + qkv_bias
        put_rows(own, i, rows.astype(jnp.bfloat16))

    groups_unit = unit // group

    def window(ref, u, j):
        begin = units[BEGIN_AT, u] + 2 * j
        if j < groups_unit - 1:
            return blocks(ref, begin, 2)
        return jnp.concatenate([ref[begin], ref[units[SECOND_AT, u]]], 0)

    def forward(u, j):
        rows = window(own, u, j)
        wrap = units[WRAP_AT, u] if j == groups_unit - 1 else 0
        offsets = bias[wrap]
        place_at = span(u * groups_unit + j, group)
        for t in range(tiles):
            cols = slice(128 * t, 128 * (t + 1))
            queries = stacked(rows[:, cols])
            keys = rows[:, width + 128 * t : width + 128 * (t + 1)]
            values = rows[:, 2 * width + 128 * t : 2 * width + 128 * (t + 1)]
            scores = mm_nt(keys, queries) * score_scale + offsets[:, cols]
            weights = jnp.exp(scores - jnp.max(scores, 0, keepdims=True))
            weights = weights / jnp.sum(weights, 0, keepdims=True)
            s.probs[place_at, cols] = weights
            mixed = folded(mm_tn(weights.astype(jnp.bfloat16), values))
            mixed = mixed.astype(jnp.bfloat16).reshape(2, half, 128)
            s.att_win[span(u * groups_unit + j, 2), :, cols] = mixed

    def sweep(step, exchange, give_back, first, second, third):
        @pl.loop(0, unit_count // 2)
        def _(u):
            for j in range(groups_unit - 1):
                step(u, j)

        first()
        exchange()

        @pl.loop(0, unit_count // 2)
        def _(u):
            step(2 * u, groups_unit - 1)
            step(2 * u + 1, groups_unit - 1)

        handle = give_back()
        second()

        @pl.loop(unit_count // 2, 3 * unit_count // 4)
        def _(u):
            for j in range(groups_unit - 1):
                step(u, j)

        third()

        @pl.loop(3 * unit_count // 4, unit_count)
        def _(u):
            for j in range(groups_unit - 1):
                step(u, j)

        handle()

    def give_back_from(ref, out, arrived):
        def send():
            for slot in range(slots):
                out[slot] = ref[tails[slot]]
            return take_lent(links.send(out, arrived, after), arrived, ref)

        return send

    def from_windows(ref, target, target_t=None):
        @pl.loop(0, unit_count)
        def _(u):
            front = ref[units[FRONT_AT, u]]
            back = blocks(ref, units[BACK_AT, u], per_unit - 1)
            rows = jnp.concatenate([front, back], 0)
            target[span(u, unit), :] = rows
            if target_t is not None:
                target_t[:, span(u, unit)] = rows.T

    def take_lent(copy, arrived, ref):
        def take():
            copy.wait_recv()
            ref[tok // half :] = arrived[...]

        return take

    def first():
        proj_copy.third()
        up_copy.third()

    def second():
        down_copy.second()
        proj_copy.fourth()

    def third():
        up_copy.fourth()
        down_copy.third()

    sweep(
        forward,
        take_lent(lend, s.borrowed, own),
        give_back_from(s.att_win, s.att_out, s.att_back),
        first,
        second,
        third,
    )
    from_windows(s.att_win, s.att_rows, s.att_t)

    proj_copy.end()
    mid, mlp_in = s.mid, s.mlp_in

    @pl.loop(0, tok // chunk)
    def _(i):
        rows = mm(s.att_rows[span(i, chunk), :], flat(whole_proj))
        rows = xb[span(i, chunk), :].astype(jnp.float32) + rows + vectors[4:5, :]
        mid[span(i, chunk), :] = rows
        normed, _ = norm_parts(rows)
        low = (normed * vectors[5:6, :] + vectors[6:7, :]).astype(jnp.bfloat16)
        mlp_in[span(i, chunk), :] = low
        s.mlp_in_t[:, span(i, chunk)] = low.T

    up_copy.end()
    down_copy.fourth()
    act, slope = s.act, s.slope
    wide = act.shape[1] // width

    @pl.loop(0, wide)
    def _(c):
        cols = span(c, width)

        @pl.loop(0, tok // chunk)
        def _(i):
            pre = mm(mlp_in[span(i, chunk), :], flat(whole_up, cols))
            value, derivative = gelu_parts(pre + vectors[pl.ds(8 + c, 1), :])
            act[span(i, chunk), cols] = value.astype(jnp.bfloat16)
            slope[span(i, chunk), cols] = derivative.astype(jnp.bfloat16)

    out_low = s.out_low
    down_copy.end()

    @pl.loop(0, tok // chunk)
    def _(i):
        rows = mid[span(i, chunk), :] + mm(act[span(i, chunk), :], flat(whole_down))
        live = lax.broadcasted_iota(jnp.int32, (chunk, width), 0) + i * chunk < used
        rows = jnp.where(live, rows + vectors[7:8, :], 0.0)
        out_low[span(i, chunk), :] = rows.astype(jnp.bfloat16)

    store_out = pltpu.make_async_copy(out_low, block_out, s.load_sems.at[0])
    store_out.start()

    down = down_flow.held

    @pl.loop(0, clips)
    def _(c):
        size = act.shape[1] // clips
        part = (mm(s.et[...], act[:, span(c, size)]) * grad_scale).astype(jnp.bfloat16)
        part = part.reshape(slabs, 2, -1, size)
        for h in range(2):
            down[:, c % 2, h, c // 2] = part[:, h]

    down_flow.begin()

    @pl.loop(0, wide)
    def _(c):
        cols = span(c, width)
        weights = whole_down.reshape(wide, width, width)[c]

        def step(i, sums):
            grad = mm_nt(eb[span(i, chunk), :], weights)
            low = grad * slope[span(i, chunk), cols].astype(jnp.float32)
            low = low.astype(jnp.bfloat16)
            slope[span(i, chunk), cols] = low
            return sums + jnp.sum(low.astype(jnp.float32), 0, keepdims=True)

        sums = lax.fori_loop(0, tok // chunk, step, jnp.zeros((1, width), jnp.float32))
        s.up_sum[pl.ds(c, 1), :] = sums

    up = up_flow.held

    def keep(target, slab, part):
        part = (part * grad_scale).astype(jnp.bfloat16)
        part = part.reshape(clips // 2, 2, 2, -1, part.shape[-1])
        for y in range(2):
            for h in range(2):
                target[slab, y, h] = part[:, y, h]

    @pl.loop(0, slabs)
    def _(i):
        keep(up, i, mm(s.mlp_in_t[...], slope[:, span(i, act.shape[1] // slabs)]))

    up_flow.begin()
    down_flow.second()

    mid_grad, mid_low = s.mid_grad, s.mid_low

    def mid_step(i, sums):
        grad = mm_nt(slope[span(i, chunk), :], flat(whole_up))
        normed, inverse = norm_parts(mid[span(i, chunk), :])
        out_grad = eb[span(i, chunk), :].astype(jnp.float32)
        rows = out_grad + norm_back(normed, inverse, grad * vectors[5:6, :])
        low = rows.astype(jnp.bfloat16)
        mid_grad[span(i, chunk), :] = rows
        put_rows(mid_low, i, low)
        return tuple(
            old + jnp.sum(new, 0, keepdims=True)
            for old, new in zip(sums, (low.astype(jnp.float32), grad * normed, grad, out_grad))
        )

    zero = jnp.zeros((1, width), jnp.float32)
    mid_sums = lax.fori_loop(0, tok // chunk, mid_step, (zero,) * 4)
    for row, value in zip((4, 5, 6, 7), mid_sums):
        small.held[0, row : row + 1, :] = value * grad_scale
    small.held[0, 8:12, :] = s.up_sum[...] * grad_scale
    up_flow.second()

    proj_columns = flat(whole_proj)
    head_low = jnp.concatenate(
        [mid_low[heads[i]] for i in range(slots)], 0
    )
    put_rows(s.dlent, 0, mm_nt(head_low, proj_columns).astype(jnp.bfloat16))
    lend_back = links.send(s.dlent, s.dborrowed, before)
    dwin_own = s.dwin_own

    @pl.loop(0, tok // chunk)
    def _(i):
        rows = mm_nt(rows_of(mid_low, i, chunk), flat(whole_proj))
        put_rows(dwin_own, i, rows.astype(jnp.bfloat16))

    grad = mm(s.att_t[...], mid_low[...].reshape(tok, width))
    for i in range(slabs):
        keep(proj_flow.held, i, grad[:, i * (width // slabs) : (i + 1) * (width // slabs)])
    proj_flow.begin()
    down_flow.third()

    bias_grad, qg_win = s.bias_grad, s.qg_win
    bias_grad[...] = jnp.zeros_like(bias_grad)

    def backward(u, j):
        rows = window(own, u, j)
        grads = window(dwin_own, u, j)
        place_at = span(u * groups_unit + j, group)
        for t in range(tiles):
            cols = slice(128 * t, 128 * (t + 1))
            queries = stacked(rows[:, cols])
            keys = rows[:, width + 128 * t : width + 128 * (t + 1)]
            values = rows[:, 2 * width + 128 * t : 2 * width + 128 * (t + 1)]
            mixed = stacked(grads[:, cols])
            weights = s.probs[place_at, cols]
            prob_grad = mm_nt(values, mixed)
            value_grad = mm(weights.astype(jnp.bfloat16), mixed)
            inner = jnp.sum(weights * prob_grad, 0, keepdims=True)
            score = (weights * (prob_grad - inner)).astype(jnp.bfloat16)
            bias_grad[:, cols] += score.astype(jnp.float32)
            key_grad = mm(score, queries) * score_scale
            query_grad = folded(mm_tn(score, keys)) * score_scale
            for k, value in enumerate((query_grad, key_grad, value_grad)):
                at = slice(k * width + 128 * t, k * width + 128 * (t + 1))
                value = value.astype(jnp.bfloat16).reshape(2, half, 128)
                qg_win[span(u * groups_unit + j, 2), :, at] = value

    def second_back():
        proj_flow.second()

    sweep(
        backward,
        take_lent(lend_back, s.dborrowed, dwin_own),
        give_back_from(qg_win, s.qg_out, s.qg_back),
        up_flow.third,
        second_back,
        down_flow.fourth,
    )
    qg_rows = s.qg_rows
    from_windows(qg_win, qg_rows)

    pair = 2
    for i in range(slabs // pair):
        size = 3 * width // slabs
        grad = mm(s.attn_in_t[...], qg_rows[:, i * pair * size : (i + 1) * pair * size])
        for k in range(pair):
            keep(qkv_flow.held, i * pair + k, grad[:, k * size : (k + 1) * size])
    qkv_flow.begin()
    proj_flow.third()
    up_flow.fourth()

    def in_step(i, sums):
        rows = qg_rows[span(i, chunk), :]
        grad = mm_nt(rows, flat(whole_qkv))
        normed, inverse = norm_parts(xb[span(i, chunk), :].astype(jnp.float32))
        mid[span(i, chunk), :] = mid_grad[span(i, chunk), :] + norm_back(
            normed, inverse, grad * vectors[0:1, :]
        )
        query_part = rows[:, :width].astype(jnp.float32)
        value_part = rows[:, 2 * width :].astype(jnp.float32)
        return tuple(
            old + jnp.sum(new, 0, keepdims=True)
            for old, new in zip(sums, (grad * normed, grad, query_part, value_part))
        )

    in_sums = lax.fori_loop(0, tok // chunk, in_step, (zero,) * 4)
    store_grad = pltpu.make_async_copy(mid, x_grad, s.load_sems.at[1])
    store_grad.start()
    for row, value in zip((0, 1, 2, 3), in_sums):
        small.held[0, row : row + 1, :] = value * grad_scale

    by_head = bias_grad[...]
    for r in range(RELS):
        picked = jnp.sum(jnp.where(offset == r, by_head, 0.0), 0, keepdims=True)
        s.att_sum[r : r + 1, :] = picked
    s.att_sum[RELS:, :] = jnp.zeros((128 - RELS, width), jnp.float32)
    sums = lax.dot_general(
        spread, s.att_sum[...], (((1,), (1,)), ((), ())), precision=HIGHEST
    ) * grad_scale
    for i in range(width // 128):
        small.held[0, 12:16, 128 * i : 128 * (i + 1)] = sums[4 * i : 4 * i + 4, :]

    qkv_flow.second()
    small.begin()
    proj_flow.fourth()
    small.second()
    qkv_flow.third()
    small.third()
    qkv_flow.fourth()
    small.fourth()
    for flow, out in zip(flows, owned):
        first, last = flow.end()
        if flow is down_flow:
            out[...] = jnp.concatenate([first, last], 0).T
        else:
            rows = first.shape[0]
            out[:rows, :] = first
            out[rows:, :] = last
    small_out[...] = small.end()
    store_out.wait()
    store_grad.wait()
    links.drain()


BEGIN_AT, SECOND_AT, FRONT_AT, BACK_AT, WRAP_AT, HEADS_AT, TAILS_AT, USED_AT = range(8)


def unit_table(lengths, slab_size, tok):
    unit, half = SHORT // slab_size * BINS, WIN // 2 * BINS
    count, size = tok // unit, unit // half
    at = jnp.arange(count, dtype=jnp.int32)
    segment = lengths // slab_size * BINS // unit
    ends = jnp.cumsum(segment)
    starts = ends - segment
    slots = jnp.arange(1, lengths.shape[0] + 1, dtype=jnp.int32)
    here = (starts[:, None] <= at) & (at < ends[:, None])
    inside = jnp.sum(here, 0)
    last = jnp.sum(jnp.where(here & (ends[:, None] == at + 1), slots[:, None], 0), 0)
    first = jnp.sum(jnp.where(here & (starts[:, None] == at), slots[:, None], 0), 0)
    begin = at * size + inside
    front = jnp.maximum(at * size - inside, 0)
    blocks_own = tok // half
    pad = (0, count - lengths.shape[0])
    return jnp.stack([
        begin,
        jnp.where(last > 0, blocks_own + last - 1, begin + size - 1),
        jnp.where(first > 0, blocks_own + first - 1, front),
        at * size - inside + 1,
        ((last > 0) & (lax.axis_index(SLAB) == slab_size - 1)).astype(jnp.int32),
        jnp.pad(jnp.minimum(starts, count - 1) * size, pad),
        jnp.pad(jnp.maximum(ends * size - 1, 0), pad),
        jnp.full((count,), ends[-1] * unit),
    ]).astype(jnp.int32)


def block_call(tokens, y_grad, clip_rows, vectors, table, masters, slab_size, clip_size):
    vmem, smem, anywhere = (
        pl.BlockSpec(memory_space=pltpu.VMEM),
        pl.BlockSpec(memory_space=pltpu.SMEM),
        pl.BlockSpec(memory_space=pl.ANY),
    )
    depth = clip_size // 2
    tok, width = tokens.shape
    hidden = masters[2].shape[1] * slab_size
    slots = clip_rows.shape[1]
    half = WIN // 2 * BINS
    low, full = jnp.bfloat16, jnp.float32
    helds = []
    for position, master in enumerate(masters):
        rows, columns = master.shape if position < 3 else master.shape[::-1]
        helds.append((slab_size, 2, 2, depth, rows // 2, columns))
    def buffer(*sizes):
        kind = full if sizes[-1] is full else low
        return pltpu.VMEM(sizes[:-1] if sizes[-1] is full else sizes, kind)

    def whole(master):
        return buffer(depth, 2, 2, master.shape[0] // 2, slab_size * master.shape[1])

    held = Held(
        xb=buffer(tok, width), eb=buffer(tok, width), et=buffer(width, tok),
        attn_in=buffer(tok // half, half, width), attn_in_t=buffer(width, tok),
        own=buffer(tok // half + slots, half, 3 * width), lent=buffer(slots, half, 3 * width),
        borrowed=buffer(slots, half, 3 * width),
        probs=buffer(tok, width, full), att_win=buffer(tok // half + slots, half, width),
        att_out=buffer(slots, half, width), att_back=buffer(slots, half, width), att_rows=buffer(tok, width), att_t=buffer(width, tok),
        mid=buffer(tok, width, full), mlp_in=buffer(tok, width), mlp_in_t=buffer(width, tok),
        act=buffer(tok, hidden), slope=buffer(tok, hidden), mid_grad=buffer(tok, width, full),
        mid_low=buffer(tok // half, half, width), dwin_own=buffer(tok // half + slots, half, width), dlent=buffer(slots, half, width),
        dborrowed=buffer(slots, half, width), qg_win=buffer(tok // half + slots, half, 3 * width),
        qg_out=buffer(slots, half, 3 * width), qg_back=buffer(slots, half, 3 * width), qg_rows=buffer(tok, 3 * width),
        bias=buffer(2, WIN * BINS, width, full), bias_grad=buffer(WIN * BINS, width, full),
        up_sum=buffer(hidden // width, width, full), att_sum=buffer(128, width, full),
        out_low=buffer(tok, width),
        load_sems=pltpu.SemaphoreType.DMA((2,)),
        whole_qkv=whole(masters[0]), whole_proj=whole(masters[1]),
        whole_up=whole(masters[2]), whole_down=whole(masters[3]),
    )
    copies = 4 * (2 * (depth - 1) + 9) + 4 * (2 + 4 + 2 + 2 * (depth - 1)) + 3 + depth - 1 + 4
    scratch = [pltpu.SemaphoreType.DMA((copies,)), pltpu.SemaphoreType.DMA((copies,)), *held]
    small = (16, width)
    scratch += [
        pltpu.VMEM((3,) + small, full), pltpu.VMEM((3,) + small, full), pltpu.VMEM((depth,) + small, full)
    ]
    for sizes in helds:
        scratch += [pltpu.VMEM(sizes, low)] + scatter_buffers(sizes)
    return pl.pallas_call(
        functools.partial(block_kernel, slab_size, clip_size),
        out_shape=[
            jax.ShapeDtypeStruct((tok, width), low),
            jax.ShapeDtypeStruct((tok, width), full),
            jax.ShapeDtypeStruct(small, full),
        ]
        + [jax.ShapeDtypeStruct(m.shape, full) for m in masters],
        in_specs=[anywhere, anywhere, smem] + [vmem] * 6,
        out_specs=[anywhere, anywhere] + [vmem] * 5,
        scratch_shapes=scratch,
        compiler_params=pltpu.CompilerParams(
            collective_id=0, has_side_effects=True, vmem_limit_bytes=62 << 20
        ),
        name="block",
    )(tokens, y_grad, unit_table(clip_rows[0], slab_size, tok), vectors, table, *masters)


def shards(
    tokens,
    y_grad,
    clip_rows,
    qkv_weight,
    proj_weight,
    up_weight,
    down_weight,
    qkv_m,
    proj_m,
    up_m,
    down_m,
    qkv_v,
    proj_v,
    up_v,
    down_v,
    vectors,
    vectors_m,
    vectors_v,
    table,
    table_m,
    table_v,
):
    slab_size, clip_size = lax.axis_size(SLAB), lax.axis_size(CLIP)
    masters = (qkv_weight, proj_weight, up_weight, down_weight)
    hidden = up_weight.shape[1] * slab_size
    aligned = slab_size == 4 and clip_size % 2 == 0 and all(m.shape[0] % 32 == 0 for m in masters)
    if aligned and hidden // (clip_size // 2) == tokens.shape[-1]:
        block_out, x_grad, small, *owned = block_call(
            tokens[0, 0], y_grad[0, 0], clip_rows, vectors, table, masters, slab_size, clip_size
        )
        results = [block_out[None, None], x_grad[None, None]]
        moments = ((qkv_m, qkv_v), (proj_m, proj_v), (up_m, up_v), (down_m, down_v))
        for master, (first, second), grad in zip(masters, moments, owned):
            results += adamw(master, first, second, grad, rate_matrix, weight_decay)
        rows = vectors.shape[0]
        results += adamw(vectors, vectors_m, vectors_v, small[:rows], rate_vector, 0.0)
        by_head = small[rows : rows + 4].reshape(4, -1, 128).transpose(1, 0, 2).reshape(-1, 128)
        results += adamw(
            table, table_m, table_v, by_head[: table.shape[1], :RELS].T, rate_vector, 0.0
        )
        return tuple(results)
    lengths = clip_rows[0]
    slab_count = lax.axis_size(SLAB)
    inputs = tokens[0, 0].astype(jnp.float32)
    tok_count, width = inputs.shape
    rows_dev = tok_count // BINS
    head_dim = width // HEADS
    score_scale = head_dim ** (-0.5)
    source, time_wraps, seg_starts = window_rows(
        lengths, lax.axis_index(SLAB), slab_count, rows_dev
    )
    total_rows = rows_dev + 2 * lengths.shape[0]
    head_rows = jnp.minimum(
        seg_starts[:, None] + jnp.arange(2, dtype=jnp.int32)[None, :], rows_dev - 1
    ).reshape(-1)
    windows_count = source.shape[0] * (BINS // WIN)
    bin_folds = jnp.arange(windows_count) % (BINS // WIN) == BINS // WIN - 1
    allowed = window_mask(jnp.repeat(time_wraps, BINS // WIN), bin_folds)[:, None]
    offset_hot = offset_table()
    rel_bias = (
        jnp.dot(offset_hot, table, precision=HIGHEST)
        .reshape(WIN * WIN, WIN * WIN, HEADS)
        .transpose(2, 0, 1)
    )
    used_rows = jnp.sum(lengths) // slab_count
    live_rows = (jnp.arange(tok_count) // BINS < used_rows).astype(jnp.float32)[:, None]
    part_copies = (
        lax.all_gather(qkv_weight.astype(jnp.bfloat16), CLIP, axis=0, tiled=True),
        lax.all_gather(proj_weight.astype(jnp.bfloat16), CLIP, axis=0, tiled=True),
        lax.all_gather(up_weight.astype(jnp.bfloat16), CLIP, axis=0, tiled=True),
        lax.all_gather(down_weight.astype(jnp.bfloat16), CLIP, axis=0, tiled=True),
    )
    copies = (
        lax.all_gather(part_copies[0], SLAB, axis=1, tiled=True),
        lax.all_gather(part_copies[1], SLAB, axis=1, tiled=True),
        lax.all_gather(part_copies[2], SLAB, axis=1, tiled=True),
        lax.all_gather(part_copies[3], SLAB, axis=1, tiled=True),
    )
    qkv_copy, proj_copy, up_copy, down_copy = copies
    attn_input = affine_norm(inputs, vectors[0], vectors[1]).astype(jnp.bfloat16)
    bias_row = jnp.concatenate([vectors[2], jnp.zeros_like(vectors[2]), vectors[3]])
    qkv_rows = (
        jnp.dot(attn_input, qkv_copy, preferred_element_type=jnp.float32) + bias_row
    ).astype(jnp.bfloat16)
    qkv_grid = qkv_rows.reshape(rows_dev, BINS, 3 * width)
    borrowed = from_behind(qkv_grid[head_rows], SLAB, -1)
    qkv_windows = to_windows(jnp.concatenate([qkv_grid, borrowed], 0), source)
    query_win = qkv_windows[:, :, :width].reshape(windows_count, WIN * WIN, HEADS, head_dim)
    key_win = qkv_windows[:, :, width : 2 * width].reshape(
        windows_count, WIN * WIN, HEADS, head_dim
    )
    value_win = qkv_windows[:, :, 2 * width :].reshape(windows_count, WIN * WIN, HEADS, head_dim)

    def scores_of(queries, keys_all):
        raw = (
            jnp.einsum("wqhd,wkhd->whqk", queries, keys_all, preferred_element_type=jnp.float32)
            * score_scale
            + rel_bias[None]
        )
        return jnp.where(allowed, raw, masked_score)

    scores = scores_of(query_win, key_win)
    top_score = jnp.max(scores, -1, keepdims=True)
    exp_sum = jnp.sum(jnp.exp(scores - top_score), -1, keepdims=True)
    probs_low = (jnp.exp(scores - top_score) / exp_sum).astype(jnp.bfloat16)
    attended = jnp.einsum(
        "whqk,wkhd->wqhd", probs_low, value_win, preferred_element_type=jnp.float32
    )
    attended = attended.astype(jnp.bfloat16).reshape(windows_count, WIN * WIN, width)
    spread_out = from_windows(attended, source, total_rows)
    returned = from_behind(spread_out[rows_dev:], SLAB, 1)
    attended_rows = spread_out[:rows_dev].at[head_rows].add(returned).reshape(tok_count, width)
    residual = (
        inputs + jnp.dot(attended_rows, proj_copy, preferred_element_type=jnp.float32) + vectors[4]
    )
    mlp_input = affine_norm(residual, vectors[5], vectors[6]).astype(jnp.bfloat16)
    pre_gelu = jnp.dot(mlp_input, up_copy, preferred_element_type=jnp.float32) + vectors[
        8:
    ].reshape(-1)
    activated, gelu_pull = jax.vjp(gelu_exact, pre_gelu)
    activated_low = activated.astype(jnp.bfloat16)
    block_out = (
        residual
        + jnp.dot(activated_low, down_copy, preferred_element_type=jnp.float32)
        + vectors[7]
    ) * live_rows
    out_grad = y_grad[0, 0].astype(jnp.float32) * live_rows
    out_low = out_grad.astype(jnp.bfloat16)
    down_grad = jnp.dot(activated_low.T, out_low, preferred_element_type=jnp.float32)
    act_grad = jnp.dot(out_low, down_copy.T, preferred_element_type=jnp.float32)
    pre_low = gelu_pull(act_grad)[0].astype(jnp.bfloat16)
    up_grad = jnp.dot(mlp_input.T, pre_low, preferred_element_type=jnp.float32)
    mlp_in_grad = jnp.dot(pre_low, up_copy.T, preferred_element_type=jnp.float32)
    norm_value, norm_pull = jax.vjp(affine_norm, residual, vectors[5], vectors[6])
    resid_norm_grad, gain_two_grad, shift_two_grad = norm_pull(mlp_in_grad)
    resid_grad = out_grad + resid_norm_grad
    attn_low = resid_grad.astype(jnp.bfloat16)
    proj_grad = jnp.dot(attended_rows.T, attn_low, preferred_element_type=jnp.float32)
    mixed_grad = jnp.dot(attn_low, proj_copy.T, preferred_element_type=jnp.float32).astype(
        jnp.bfloat16
    )
    mixed_grid = mixed_grad.reshape(rows_dev, BINS, width)
    sent_back = from_behind(mixed_grid[head_rows], SLAB, -1)
    grad_windows = to_windows(jnp.concatenate([mixed_grid, sent_back], 0), source)
    grad_windows = grad_windows.reshape(windows_count, WIN * WIN, HEADS, head_dim)
    probs = jnp.exp(scores_of(query_win, key_win) - top_score) / exp_sum
    prob_grad = jnp.einsum(
        "wqhd,wkhd->whqk", grad_windows, value_win, preferred_element_type=jnp.float32
    )
    value_grad = jnp.einsum(
        "whqk,wqhd->wkhd", probs_low, grad_windows, preferred_element_type=jnp.float32
    )
    score_grad = (probs * (prob_grad - jnp.sum(probs * prob_grad, -1, keepdims=True))).astype(
        jnp.bfloat16
    )
    bias_grad = (
        jnp.sum(score_grad.astype(jnp.float32), 0)
        .transpose(1, 2, 0)
        .reshape(WIN * WIN * WIN * WIN, HEADS)
    )
    table_grad = jnp.dot(offset_hot.T, bias_grad, precision=HIGHEST)
    query_grad = (
        jnp.einsum("whqk,wkhd->wqhd", score_grad, key_win, preferred_element_type=jnp.float32)
        * score_scale
    )
    key_grad = (
        jnp.einsum("whqk,wqhd->wkhd", score_grad, query_win, preferred_element_type=jnp.float32)
        * score_scale
    )
    qkv_grad_win = jnp.concatenate(
        [
            query_grad.reshape(windows_count, WIN * WIN, width),
            key_grad.reshape(windows_count, WIN * WIN, width),
            value_grad.reshape(windows_count, WIN * WIN, width),
        ],
        -1,
    ).astype(jnp.bfloat16)
    qkv_spread = from_windows(qkv_grad_win, source, total_rows)
    given_back = from_behind(qkv_spread[rows_dev:], SLAB, 1)
    qkv_grad_rows = (
        qkv_spread[:rows_dev].at[head_rows].add(given_back).reshape(tok_count, 3 * width)
    )
    qkv_w_grad = jnp.dot(attn_input.T, qkv_grad_rows, preferred_element_type=jnp.float32)
    bias_sums = jnp.sum(qkv_grad_rows.astype(jnp.float32), 0)
    attn_in_grad = jnp.dot(qkv_grad_rows, qkv_copy.T, preferred_element_type=jnp.float32)
    first_value, norm_pull_one = jax.vjp(affine_norm, inputs, vectors[0], vectors[1])
    inputs_norm_grad, gain_one_grad, shift_one_grad = norm_pull_one(attn_in_grad)
    x_grad = resid_grad + inputs_norm_grad
    vector_grad = jnp.concatenate(
        [
            jnp.stack(
                [
                    gain_one_grad,
                    shift_one_grad,
                    bias_sums[:width],
                    bias_sums[2 * width :],
                    jnp.sum(attn_low.astype(jnp.float32), 0),
                    gain_two_grad,
                    shift_two_grad,
                    jnp.sum(out_grad, 0),
                ]
            ),
            jnp.sum(pre_low.astype(jnp.float32), 0).reshape(-1, width),
        ],
        0,
    )
    grad_scale = float(tok_count * slab_count * lax.axis_size(CLIP)) ** (-0.5)
    part_sums = (
        lax.psum_scatter(
            (qkv_w_grad * grad_scale).astype(jnp.bfloat16), SLAB, scatter_dimension=1, tiled=True
        ).astype(jnp.float32),
        lax.psum_scatter(
            (proj_grad * grad_scale).astype(jnp.bfloat16), SLAB, scatter_dimension=1, tiled=True
        ).astype(jnp.float32),
        lax.psum_scatter(
            (up_grad * grad_scale).astype(jnp.bfloat16), SLAB, scatter_dimension=1, tiled=True
        ).astype(jnp.float32),
        lax.psum_scatter(
            (down_grad * grad_scale).astype(jnp.bfloat16), SLAB, scatter_dimension=1, tiled=True
        ).astype(jnp.float32),
    )
    owned = (
        lax.psum_scatter(part_sums[0], CLIP, scatter_dimension=0, tiled=True),
        lax.psum_scatter(part_sums[1], CLIP, scatter_dimension=0, tiled=True),
        lax.psum_scatter(part_sums[2], CLIP, scatter_dimension=0, tiled=True),
        lax.psum_scatter(part_sums[3], CLIP, scatter_dimension=0, tiled=True),
    )
    small_sums = lax.psum((vector_grad * grad_scale, table_grad * grad_scale), (SLAB, CLIP))
    qkv_new, qkv_m_new, qkv_v_new = adamw(
        qkv_weight, qkv_m, qkv_v, owned[0], rate_matrix, weight_decay
    )
    proj_new, proj_m_new, proj_v_new = adamw(
        proj_weight, proj_m, proj_v, owned[1], rate_matrix, weight_decay
    )
    up_new, up_m_new, up_v_new = adamw(up_weight, up_m, up_v, owned[2], rate_matrix, weight_decay)
    down_new, down_m_new, down_v_new = adamw(
        down_weight, down_m, down_v, owned[3], rate_matrix, weight_decay
    )
    vectors_new, vectors_m_new, vectors_v_new = adamw(
        vectors, vectors_m, vectors_v, small_sums[0], rate_vector, 0.0
    )
    table_new, table_m_new, table_v_new = adamw(
        table, table_m, table_v, small_sums[1], rate_vector, 0.0
    )
    out_shape = (1, 1, tok_count, width)
    return (
        block_out.astype(jnp.bfloat16).reshape(out_shape),
        x_grad.reshape(out_shape),
        qkv_new,
        qkv_m_new,
        qkv_v_new,
        proj_new,
        proj_m_new,
        proj_v_new,
        up_new,
        up_m_new,
        up_v_new,
        down_new,
        down_m_new,
        down_v_new,
        vectors_new,
        vectors_m_new,
        vectors_v_new,
        table_new,
        table_m_new,
        table_v_new,
    )


def solution(mesh):
    return jax.shard_map(
        shards,
        mesh=mesh,
        in_specs=(
            P(CLIP, SLAB, None, None),
            P(CLIP, SLAB, None, None),
            P(CLIP, None),
            P(CLIP, SLAB),
            P(CLIP, SLAB),
            P(CLIP, SLAB),
            P(CLIP, SLAB),
            P(CLIP, SLAB),
            P(CLIP, SLAB),
            P(CLIP, SLAB),
            P(CLIP, SLAB),
            P(CLIP, SLAB),
            P(CLIP, SLAB),
            P(CLIP, SLAB),
            P(CLIP, SLAB),
            P(),
            P(),
            P(),
            P(),
            P(),
            P(),
        ),
        out_specs=(
            P(CLIP, SLAB, None, None),
            P(CLIP, SLAB, None, None),
            P(CLIP, SLAB),
            P(CLIP, SLAB),
            P(CLIP, SLAB),
            P(CLIP, SLAB),
            P(CLIP, SLAB),
            P(CLIP, SLAB),
            P(CLIP, SLAB),
            P(CLIP, SLAB),
            P(CLIP, SLAB),
            P(CLIP, SLAB),
            P(CLIP, SLAB),
            P(CLIP, SLAB),
            P(),
            P(),
            P(),
            P(),
            P(),
            P(),
        ),
        check_vma=False,
    )
```

```python
import functools
import itertools
import math
import typing

import jax
import jax.numpy as jnp
from jax import lax
from jax.experimental import pallas as pl
from jax.experimental.pallas import tpu as pltpu
from jax.sharding import PartitionSpec as P

HEADS = 16
BINS = 8
WIN = 4
STEP = 10
RELS = 49
SLAB, CLIP = "slab", "clip"
SHORT = 64


HIGHEST = lax.Precision.HIGHEST
norm_epsilon = 1e-06
beta_first = 0.5
beta_second = 0.5
adam_epsilon = 1e-08
rate_matrix = 0.05
rate_vector = 0.5
weight_decay = 0.05
masked_score = -1e30


def from_behind(block, axis, distance):
    devices = range(lax.axis_size(axis))
    route = [((i - distance) % len(devices), i) for i in devices]
    return lax.ppermute(block, axis, route)


def layer_norm(values):
    center = values - jnp.mean(values, -1, keepdims=True)
    spread = jnp.mean(center * center, -1, keepdims=True)
    return center * lax.rsqrt(spread + norm_epsilon)


def affine_norm(values, gain, offset):
    return layer_norm(values) * gain + offset


def gelu_exact(values):
    return jax.nn.gelu(values, approximate=False)


def window_rows(lengths, slab_index, slab_count, rows_dev):
    segment = lengths // slab_count
    seg_ends = jnp.cumsum(segment)
    seg_starts = seg_ends - segment
    row_base = WIN * jnp.arange(rows_dev // WIN, dtype=jnp.int32)
    inside = (row_base[:, None] >= seg_starts[None, :]) & (row_base[:, None] < seg_ends[None, :])
    in_clip = jnp.any(inside, axis=1)
    slot_ids = jnp.arange(lengths.shape[0], dtype=jnp.int32)
    clip_end = jnp.sum(jnp.where(inside, seg_ends[None, :], 0), axis=1)
    clip_slot = jnp.sum(jnp.where(inside, slot_ids[None, :], 0), axis=1)
    row_ids = (
        row_base[:, None]
        + jnp.where(in_clip, WIN // 2, 0)[:, None]
        + jnp.arange(WIN, dtype=jnp.int32)[None, :]
    )
    beyond = in_clip[:, None] & (row_ids >= clip_end[:, None])
    source = jnp.where(
        beyond, rows_dev + 2 * clip_slot[:, None] + row_ids - clip_end[:, None], row_ids
    )
    time_wraps = in_clip & (row_base + WIN == clip_end) & (slab_index == slab_count - 1)
    return (source, time_wraps, seg_starts)


def window_mask(time_wraps, bin_folds):
    positions = jnp.arange(WIN * WIN, dtype=jnp.int32)
    row_half = positions // WIN >= WIN // 2
    bin_half = positions % WIN >= WIN // 2
    same_row = row_half[:, None] == row_half[None, :]
    same_bin = bin_half[:, None] == bin_half[None, :]
    return (~time_wraps[:, None, None] | same_row[None]) & (
        ~bin_folds[:, None, None] | same_bin[None]
    )


def offset_table():
    positions = jnp.arange(WIN * WIN, dtype=jnp.int32)
    row_pos = positions // WIN
    bin_pos = positions % WIN
    offsets = (row_pos[:, None] - row_pos[None, :] + WIN - 1) * (2 * WIN - 1) + (
        bin_pos[:, None] - bin_pos[None, :] + WIN - 1
    )
    return (offsets.reshape(-1)[:, None] == jnp.arange(RELS, dtype=jnp.int32)[None, :]).astype(
        jnp.float32
    )


def to_windows(extended, source):
    gathered = jnp.roll(extended[source], -(WIN // 2), axis=2)
    win_rows = source.shape[0]
    width = extended.shape[-1]
    gathered = gathered.reshape(win_rows, WIN, BINS // WIN, WIN, width).transpose(0, 2, 1, 3, 4)
    return gathered.reshape(win_rows * (BINS // WIN), WIN * WIN, width)


def from_windows(windows, source, total_rows):
    win_rows = source.shape[0]
    width = windows.shape[-1]
    placed = windows.reshape(win_rows, BINS // WIN, WIN, WIN, width).transpose(0, 2, 1, 3, 4)
    placed = jnp.roll(placed.reshape(win_rows, WIN, BINS, width), WIN // 2, axis=2)
    blank = jnp.zeros((total_rows, BINS, width), windows.dtype)
    return blank.at[source.reshape(-1)].set(placed.reshape(win_rows * WIN, BINS, width))


def adamw(weight, first, second, grad, rate, decay):
    first = beta_first * first + (1.0 - beta_first) * grad
    second = beta_second * second + (1.0 - beta_second) * grad * grad
    fix_first = 1.0 - beta_first**STEP
    fix_second = 1.0 - beta_second**STEP
    update = first / fix_first / (jnp.sqrt(second / fix_second) + adam_epsilon)
    return (weight - rate * (update + decay * weight), first, second)


MESH = pl.DeviceIdType.MESH


class Links:
    def __init__(self, send_sems, recv_sems):
        self.send_sems, self.recv_sems = send_sems, recv_sems
        self.count, self.started = 0, []

    def send(self, source, target, device):
        copy = pltpu.make_async_remote_copy(
            src_ref=source,
            dst_ref=target,
            send_sem=self.send_sems.at[self.count],
            recv_sem=self.recv_sems.at[self.count],
            device_id=device,
            device_id_type=MESH,
        )
        copy.start()
        self.count += 1
        self.started.append(copy)
        return copy

    def drain(self):
        for copy in self.started:
            copy.wait_send()


class Place:
    def __init__(self, clip_size):
        self.slab, self.clip = lax.axis_index(SLAB), lax.axis_index(CLIP)
        self.x, self.core = self.slab // 2, self.slab % 2
        self.z, self.y = self.clip // 2, self.clip % 2
        self.depth = clip_size // 2
        self.over_core = (self.x * 2 + 1 - self.core, self.clip)
        self.over_x = ((1 - self.x) * 2 + self.core, self.clip)
        self.over_y = (self.slab, self.z * 2 + 1 - self.y)
        self.over_diagonal = ((1 - self.x) * 2 + 1 - self.core, self.clip)
        self.x_slab = (1 - self.x) * 2 + self.core
        self.core_slab = self.x * 2 + 1 - self.core
        self.partners = [self.over_core, self.over_x, self.over_y, self.over_diagonal]
        self.partners += [self.over_z(step) for step in range(1, self.depth)]

    def z_at(self, step):
        return lax.rem(self.z + step, self.depth)

    def over_z(self, step):
        return (self.slab, self.z_at(step) * 2 + self.y)

    def greet(self):
        barrier = pltpu.get_barrier_semaphore()
        for partner in self.partners:
            pl.semaphore_signal(barrier, inc=1, device_id=partner, device_id_type=MESH)

    def meet(self):
        pl.semaphore_wait(pltpu.get_barrier_semaphore(), len(self.partners))


def wait_all(copies):
    for copy in copies:
        copy.wait_recv()


class Gather:
    def __init__(self, place, links, whole, width, rows, columns):
        self.place, self.links, self.whole = place, links, whole
        self.width, self.rows, self.columns = width, rows, columns

    def move(self, device, z, y, half, slab):
        start, size = self.columns(slab)
        lanes = pl.ds(pl.multiple_of(slab * self.width + start, 128), size)
        block = self.whole.at[z, y, half, self.rows, lanes]
        return self.links.send(block, block, device)

    def first(self):
        place = self.place
        self.copies = [
            self.move(place.over_z(step), place.z, place.y, EVERY, place.slab)
            for step in range(1, place.depth)
        ]

    def second(self):
        place = self.place
        wait_all(self.copies)
        self.first_x = self.move(place.over_x, EVERY, place.y, 0, place.slab)
        self.first_y = self.move(place.over_y, EVERY, place.y, 1, place.slab)

    def third(self):
        place = self.place
        self.first_x.wait_recv()
        self.last_y = [
            self.move(place.over_y, EVERY, place.y, 0, slab) for slab in (place.slab, place.x_slab)
        ]
        self.first_y.wait_recv()
        self.last_x = self.move(place.over_x, EVERY, EVERY, 1, place.slab)

    def fourth(self):
        place = self.place
        wait_all(self.last_y)
        self.last_x.wait_recv()
        self.copies = [
            self.move(place.over_core, EVERY, EVERY, EVERY, slab)
            for slab in (place.slab, place.x_slab)
        ]

    def last(self):
        wait_all(self.copies)


class Scatter:
    def __init__(self, place, links, buffers, columns):
        self.place, self.links, self.columns = place, links, columns
        self.held, self.from_core, self.first_y, self.first_x = buffers[:4]
        self.last_x, self.last_y, self.from_z = buffers[4:]

    def lanes(self, slab):
        start, size = self.columns(slab)
        return pl.ds(pl.multiple_of(start, 128), size)

    def add(self, index, arrived, slab):
        lanes = self.lanes(slab)
        index = (slab, *index, EVERY, lanes)
        self.held[index] = self.held[index] + arrived[..., lanes]

    def first(self):
        place = self.place
        self.copies = []
        for x in range(2):
            slab = 2 * x + 1 - place.core
            lanes = self.lanes(slab)
            source = self.held.at[slab, :, :, :, :, lanes]
            target = self.from_core.at[x, :, :, :, :, lanes]
            self.copies.append(self.links.send(source, target, place.over_core))

    def second(self):
        place = self.place
        for x in range(2):
            self.copies[x].wait_recv()
            self.add((EVERY, EVERY, EVERY), self.from_core.at[x], 2 * x + place.core)
        self.copies = []
        for x in range(2):
            slab = 2 * x + place.core
            lanes = self.lanes(slab)
            source = self.held.at[slab, 1 - place.y, 0, :, :, lanes]
            target = self.first_y.at[x, :, :, lanes]
            self.copies.append(self.links.send(source, target, place.over_y))
        lanes = self.lanes(place.x_slab)
        source = self.held.at[place.x_slab, :, 1, :, :, lanes]
        target = self.first_x.at[:, :, :, lanes]
        self.copy = self.links.send(source, target, place.over_x)

    def third(self):
        place = self.place
        for x in range(2):
            self.copies[x].wait_recv()
            self.add((place.y, 0, EVERY), self.first_y.at[x], 2 * x + place.core)
        lanes = self.lanes(place.x_slab)
        source = self.held.at[place.x_slab, place.y, 0, :, :, lanes]
        copy_x = self.links.send(source, self.last_x.at[:, :, lanes], place.over_x)
        self.copy.wait_recv()
        self.add((EVERY, 1, EVERY), self.first_x, place.slab)
        lanes = self.lanes(place.slab)
        source = self.held.at[place.slab, 1 - place.y, 1, :, :, lanes]
        copy_y = self.links.send(source, self.last_y.at[:, :, lanes], place.over_y)
        self.copies = [copy_x, copy_y]

    def fourth(self):
        place = self.place
        lanes = self.lanes(place.slab)
        for half, arrived in enumerate((self.last_x, self.last_y)):
            self.copies[half].wait_recv()
            self.add((place.y, half, EVERY), arrived, place.slab)
        self.copies = []
        for step in range(1, place.depth):
            source = self.held.at[place.slab, place.y, :, place.z_at(step), :, lanes]
            target = self.from_z.at[step - 1, :, :, lanes]
            self.copies.append(self.links.send(source, target, place.over_z(step)))

    def last(self):
        place = self.place
        lanes = self.lanes(place.slab)
        total = self.held[place.slab, place.y, :, place.z, :, lanes].astype(jnp.float32)
        for step in range(1, place.depth):
            self.copies[step - 1].wait_recv()
            total += self.from_z[step - 1, :, :, lanes].astype(jnp.float32)
        return total, lanes


class Small:
    def __init__(self, place, links, held, arrived, line):
        self.place, self.links, self.held = place, links, held
        self.arrived, self.line = arrived, line

    def first(self):
        self.copy = self.links.send(self.held.at[0], self.arrived.at[0], self.place.over_core)

    def second(self):
        self.copy.wait_recv()
        self.held[1] = self.held[0] + self.arrived[0]
        self.copy = self.links.send(self.held.at[1], self.arrived.at[1], self.place.over_x)

    def third(self):
        self.copy.wait_recv()
        self.held[2] = self.held[1] + self.arrived[1]
        self.copy = self.links.send(self.held.at[2], self.arrived.at[2], self.place.over_y)

    def fourth(self):
        place = self.place
        self.copy.wait_recv()
        self.line[place.z] = self.held[2] + self.arrived[2]
        self.copies = [
            self.links.send(self.line.at[place.z], self.line.at[place.z], place.over_z(step))
            for step in range(1, place.depth)
        ]

    def last(self):
        wait_all(self.copies)
        total = self.line[0]
        for z in range(1, self.place.depth):
            total += self.line[z]
        return total


class Queue:
    def __init__(self, steps):
        self.steps = list(steps)

    def take(self, count=1):
        for _ in range(min(count, len(self.steps))):
            for stage in self.steps.pop(0):
                stage()

    def until(self, stage):
        while any(stage in step for step in self.steps):
            self.take()


def staggered(flows, ahead, lag):
    steps = []
    for k in range(len(flows) + lag):
        step = [flows[k].third] if k < len(flows) else []
        step += [flows[k + ahead].second] if k + ahead < len(flows) else []
        step += [flows[k - lag].fourth] if 0 <= k - lag < len(flows) else []
        steps.append(step)
    return steps


EVERY = slice(None)


def cut(total, count):
    size = total // count
    return [lambda slab, k=k: (k * size, size) for k in range(count)]


def turned(total, count):
    size = total // count
    return [lambda slab, k=k: (lax.rem(slab + k, count) * size, size) for k in range(count)]


def scatter_buffers(shape):
    slabs, _, _, depth, rows, columns = shape
    return [
        pltpu.VMEM((2, 2, 2, depth, rows, columns), jnp.bfloat16),
        pltpu.VMEM((2, depth, rows, columns), jnp.bfloat16),
        pltpu.VMEM((2, depth, rows, columns), jnp.bfloat16),
        pltpu.VMEM((depth, rows, columns), jnp.bfloat16),
        pltpu.VMEM((depth, rows, columns), jnp.bfloat16),
        pltpu.VMEM((depth - 1, 2, rows, columns), jnp.bfloat16),
    ]


def norm_parts(values):
    center = values - jnp.mean(values, -1, keepdims=True)
    inverse = lax.rsqrt(jnp.mean(center * center, -1, keepdims=True) + norm_epsilon)
    return center * inverse, inverse


def norm_back(normed, inverse, grad):
    return inverse * (
        grad
        - jnp.mean(grad, -1, keepdims=True)
        - normed * jnp.mean(grad * normed, -1, keepdims=True)
    )


def gelu_parts(values):
    below = 0.5 + 0.5 * lax.erf(values * (0.5**0.5))
    density = jnp.exp(-0.5 * values * values) * ((0.5 / math.pi) ** 0.5)
    return values * below, below + values * density


def mm(left, right):
    return jnp.dot(left, right, preferred_element_type=jnp.float32)


def mm_nt(left, right):
    return lax.dot_general(
        left, right, (((1,), (1,)), ((), ())), preferred_element_type=jnp.float32
    )


def mm_tn(left, right):
    return lax.dot_general(
        left, right, (((0,), (0,)), ((), ())), preferred_element_type=jnp.float32
    )


def span(index, size):
    return pl.ds(pl.multiple_of(index * size, size), size)


def blocks(ref, index, count):
    return jnp.concatenate([ref[index + k] for k in range(count)], 0)


def rows_of(ref, index, size):
    value = ref[span(index, size // ref.shape[1])]
    return value.reshape(size, value.shape[-1])


def put_rows(ref, index, value):
    count = value.shape[0] // ref.shape[1]
    ref[span(index, count)] = value.reshape(count, ref.shape[1], value.shape[-1])


def flat(ref, columns=slice(None)):
    block = ref[:, :, :, :, columns]
    return block.reshape(-1, block.shape[-1])


class Held(typing.NamedTuple):
    xb: typing.Any
    eb: typing.Any
    et: typing.Any
    attn_in: typing.Any
    attn_in_t: typing.Any
    own: typing.Any
    lent: typing.Any
    borrowed: typing.Any
    probs: typing.Any
    att_win: typing.Any
    att_out: typing.Any
    att_back: typing.Any
    att_rows: typing.Any
    att_t: typing.Any
    mid: typing.Any
    mlp_in: typing.Any
    mlp_in_t: typing.Any
    act: typing.Any
    slope: typing.Any
    mid_grad: typing.Any
    mid_low: typing.Any
    dwin_own: typing.Any
    dlent: typing.Any
    dborrowed: typing.Any
    qg_win: typing.Any
    qg_out: typing.Any
    qg_back: typing.Any
    qg_rows: typing.Any
    bias: typing.Any
    bias_grad: typing.Any
    up_sum: typing.Any
    att_sum: typing.Any
    out_low: typing.Any
    load_sems: typing.Any
    whole_qkv: typing.Any
    whole_proj: typing.Any
    whole_up: typing.Any
    whole_down: typing.Any


def block_kernel(slabs, clips, *refs):
    refs = list(refs)
    tokens, y_grad, units, vectors, table = refs[:5]
    masters = refs[5:9]
    block_out, x_grad, small_out = refs[9:12]
    owned = refs[12:16]
    rest = refs[16:]
    place = Place(clips)
    links = Links(rest.pop(0), rest.pop(0))
    s = Held(*rest[: len(Held._fields)])
    rest = rest[len(Held._fields) :]
    small = Small(place, links, rest.pop(0), rest.pop(0), rest.pop(0))
    qkv_parts, proj_parts, up_parts, down_parts = [
        [rest.pop(0) for _ in range(7)] for _ in masters
    ]
    qkv_flows = [Scatter(place, links, qkv_parts, c) for c in turned(masters[0].shape[1], 3)]
    proj_flow = Scatter(place, links, proj_parts, cut(masters[1].shape[1], 1)[0])
    up_flows = [Scatter(place, links, up_parts, c) for c in cut(masters[2].shape[1], 2)]
    down_flows = [Scatter(place, links, down_parts, c) for c in cut(masters[3].shape[0], 2)]
    xb, eb, own, bias = s.xb, s.eb, s.own, s.bias
    tok, width = xb.shape
    unit = SHORT // slabs * BINS
    unit_count = tok // unit
    half = WIN // 2 * BINS
    per_unit = unit // half
    group = WIN * BINS
    head = width // HEADS
    pack = 128 // head
    tiles = width // 128
    score_scale = head**-0.5
    grad_scale = float(tok * slabs * clips) ** -0.5
    slots = s.lent.shape[0]

    loads = [
        pltpu.make_async_copy(tokens, xb, s.load_sems.at[0]),
        pltpu.make_async_copy(y_grad, eb, s.load_sems.at[1]),
    ]
    for load in loads:
        load.start()
    place.greet()
    wholes = (s.whole_qkv, s.whole_proj, s.whole_up, s.whole_down)
    for whole, master in zip(wholes, masters):
        rows, width_own = whole.shape[3], master.shape[1]
        lanes = pl.ds(pl.multiple_of(place.slab * width_own, 128), width_own)
        for h in range(2):
            block = master[h * rows : (h + 1) * rows, :].astype(jnp.bfloat16)
            whole[place.z, place.y, h, :, lanes] = block

    def gathers(index, ranges, rows=(EVERY,)):
        return [
            Gather(place, links, wholes[index], masters[index].shape[1], r, c)
            for r in rows
            for c in ranges
        ]

    qkv_copies = gathers(0, turned(masters[0].shape[1], 3))
    proj_copies = gathers(1, cut(masters[1].shape[1], 1))
    up_copies = gathers(2, cut(masters[2].shape[1], 4))
    quarter = s.whole_down.shape[3] // 4
    down_copies = gathers(
        3, cut(masters[3].shape[1], 1), [pl.ds(k * quarter, quarter) for k in range(4)]
    )
    later = proj_copies + up_copies
    later = proj_copies + up_copies + down_copies
    queue = Queue(
        [
            [flow.first for flow in qkv_copies],
            [flow.second for flow in qkv_copies] + [flow.first for flow in later[:3]],
            [flow.third for flow in qkv_copies] + [flow.first for flow in later[3:]],
            [flow.second for flow in later[:3]],
            [flow.fourth for flow in qkv_copies],
        ]
        + staggered(later, 3, 2)
    )
    place.meet()
    queue.until(qkv_copies[-1].first)

    heads = [units[HEADS_AT, i] for i in range(slots)]
    tails = [units[TAILS_AT, i] for i in range(slots)]
    used = units[USED_AT, 0]

    heads_of = lax.broadcasted_iota(jnp.int32, (HEADS, width), 1) // head
    spread = (heads_of == lax.broadcasted_iota(jnp.int32, (HEADS, width), 0)).astype(jnp.float32)
    by_offset = jnp.dot(table[...], spread, precision=HIGHEST)
    key = lax.broadcasted_iota(jnp.int32, (group, width), 0)
    query = lax.broadcasted_iota(jnp.int32, (group, width), 1) % group
    key_row, key_bin, query_row, query_bin = key // BINS, key % BINS, query // BINS, query % BINS
    key_place, query_place = (key_bin - WIN // 2) % BINS, (query_bin - WIN // 2) % BINS
    key_class = key_place // WIN + jnp.where(key_place >= WIN + WIN // 2, 1, 0)
    query_class = query_place // WIN + jnp.where(query_place >= WIN + WIN // 2, 1, 0)
    same = key_class == query_class
    offset = (query_row - key_row + WIN - 1) * (2 * WIN - 1) + query_place - key_place + WIN - 1
    offset = jnp.where(same, offset, -1)
    total = jnp.zeros((group, width), jnp.float32)
    for r in range(RELS):
        total = jnp.where(offset == r, by_offset[r : r + 1, :], total)
    total = jnp.where(same, total, masked_score)
    bias[0] = total
    bias[1] = jnp.where(key_row // (WIN // 2) == query_row // (WIN // 2), total, masked_score)
    lane = lax.broadcasted_iota(jnp.int32, (group, 128), 1) // head
    picks = [(lane == h).astype(jnp.bfloat16) for h in range(pack)]

    def stacked(block):
        return jnp.concatenate([block * pick for pick in picks], 0)

    def folded(block):
        result = block[(pack - 1) * group :]
        for h in range(pack - 2, -1, -1):
            result = jnp.where(lane == h, block[h * group : (h + 1) * group], result)
        return result

    loads[0].wait()
    chunk = 256

    @pl.loop(0, tok // chunk)
    def _(i):
        normed, _ = norm_parts(xb[span(i, chunk), :].astype(jnp.float32))
        low = (normed * vectors[0:1, :] + vectors[1:2, :]).astype(jnp.bfloat16)
        put_rows(s.attn_in, i, low)
        s.attn_in_t[:, span(i, chunk)] = low.T

    queue.until(qkv_copies[-1].second)

    loads[1].wait()

    @pl.loop(0, tok // chunk)
    def _(i):
        live = lax.broadcasted_iota(jnp.int32, (chunk, width), 0) + i * chunk < used
        low = jnp.where(live, eb[span(i, chunk), :].astype(jnp.float32), 0.0)
        low = low.astype(jnp.bfloat16)
        eb[span(i, chunk), :] = low
        s.et[:, span(i, chunk)] = low.T

    queue.until(qkv_copies[-1].fourth)
    for flow in qkv_copies:
        flow.last()
    whole_qkv, whole_proj = s.whole_qkv, s.whole_proj
    whole_up, whole_down = s.whole_up, s.whole_down

    qkv_bias = jnp.concatenate(
        [vectors[2:3, :], jnp.zeros((1, width), jnp.float32), vectors[3:4, :]], 1
    )
    head_in = jnp.concatenate(
        [s.attn_in[heads[i]] for i in range(slots)], 0
    )
    put_rows(s.lent, 0, (mm(head_in, flat(whole_qkv)) + qkv_bias).astype(jnp.bfloat16))
    before = (lax.rem(place.slab + slabs - 1, slabs), place.clip)
    after = (lax.rem(place.slab + 1, slabs), place.clip)
    lend = links.send(s.lent, s.borrowed, before)
    queue.take()

    @pl.loop(0, tok // chunk)
    def _(i):
        rows = mm(rows_of(s.attn_in, i, chunk), flat(whole_qkv)) + qkv_bias
        put_rows(own, i, rows.astype(jnp.bfloat16))

    queue.take()

    groups_unit = unit // group

    def window(ref, u, j):
        begin = units[BEGIN_AT, u] + 2 * j
        if j < groups_unit - 1:
            return blocks(ref, begin, 2)
        return jnp.concatenate([ref[begin], ref[units[SECOND_AT, u]]], 0)

    def parts(rows):
        return [
            [rows[:, k * width + 128 * t : k * width + 128 * (t + 1)] for t in range(tiles)]
            for k in range(rows.shape[1] // width)
        ]

    def forward(works):
        rows = [parts(window(own, u, j)) for u, j in works]
        wraps = [units[WRAP_AT, u] if j == groups_unit - 1 else 0 for u, j in works]
        scores = [
            jnp.concatenate([mm_nt(k, stacked(q)) for q, k in zip(queries, keys)], 1)
            for queries, keys, _ in rows
        ]
        scores = [score * score_scale + bias[wrap] for score, wrap in zip(scores, wraps)]
        weights = [jnp.exp(score - jnp.max(score, 0, keepdims=True)) for score in scores]
        weights = [weight * (1.0 / jnp.sum(weight, 0, keepdims=True)) for weight in weights]
        lows = [weight.astype(jnp.bfloat16) for weight in weights]
        for (u, j), weight in zip(works, weights):
            s.probs[span(u * groups_unit + j, group), :] = weight
        mixed = [
            [mm_tn(low[:, 128 * t : 128 * (t + 1)], v) for t, v in enumerate(values)]
            for low, (_, _, values) in zip(lows, rows)
        ]
        for (u, j), products in zip(works, mixed):
            out = jnp.concatenate([folded(product) for product in products], 1)
            out = out.astype(jnp.bfloat16).reshape(2, half, width)
            s.att_win[span(u * groups_unit + j, 2)] = out

    def sweep(step, exchange, give_back, first, second, third):
        @pl.loop(0, unit_count // 2)
        def _(u):
            step([(u, j) for j in range(groups_unit - 1)])

        first()
        exchange()

        @pl.loop(0, unit_count // 2)
        def _(u):
            step([(2 * u, groups_unit - 1), (2 * u + 1, groups_unit - 1)])

        handle = give_back()
        second()

        @pl.loop(unit_count // 2, 3 * unit_count // 4)
        def _(u):
            step([(u, j) for j in range(groups_unit - 1)])

        third()

        @pl.loop(3 * unit_count // 4, unit_count)
        def _(u):
            step([(u, j) for j in range(groups_unit - 1)])

        handle()

    def give_back_from(ref, out, arrived):
        def send():
            for slot in range(slots):
                out[slot] = ref[tails[slot]]
            return take_lent(links.send(out, arrived, after), arrived, ref)

        return send

    def from_windows(ref, target, target_t=None):
        @pl.loop(0, unit_count)
        def _(u):
            front = ref[units[FRONT_AT, u]]
            back = blocks(ref, units[BACK_AT, u], per_unit - 1)
            rows = jnp.concatenate([front, back], 0)
            target[span(u, unit), :] = rows
            if target_t is not None:
                target_t[:, span(u, unit)] = rows.T

    def take_lent(copy, arrived, ref):
        def take():
            copy.wait_recv()
            ref[tok // half :] = arrived[...]

        return take

    def taking(source, count):
        return lambda: source.take(count)

    sweep(
        forward,
        take_lent(lend, s.borrowed, own),
        give_back_from(s.att_win, s.att_out, s.att_back),
        taking(queue, 1),
        taking(queue, 1),
        taking(queue, 1),
    )
    from_windows(s.att_win, s.att_rows, s.att_t)

    queue.take()
    for flow in proj_copies:
        flow.last()
    mid, mlp_in = s.mid, s.mlp_in

    @pl.loop(0, tok // chunk)
    def _(i):
        rows = mm(s.att_rows[span(i, chunk), :], flat(whole_proj))
        rows = xb[span(i, chunk), :].astype(jnp.float32) + rows + vectors[4:5, :]
        mid[span(i, chunk), :] = rows
        normed, _ = norm_parts(rows)
        low = (normed * vectors[5:6, :] + vectors[6:7, :]).astype(jnp.bfloat16)
        mlp_in[span(i, chunk), :] = low
        s.mlp_in_t[:, span(i, chunk)] = low.T

    act, slope = s.act, s.slope
    wide = act.shape[1] // width
    for k, flow in enumerate(up_copies):
        queue.until(flow.fourth)
        flow.last()
        size = width // len(up_copies)
        lanes = [slice(c * width + k * size, c * width + (k + 1) * size) for c in range(wide)]
        piece = slice(k * size, (k + 1) * size)
        shift = jnp.concatenate([vectors[8 + c : 9 + c, piece] for c in range(wide)], 1)

        @pl.loop(0, tok // chunk)
        def _(i):
            weights = jnp.concatenate([flat(whole_up, at) for at in lanes], 1)
            pre = mm(mlp_in[span(i, chunk), :], weights)
            value, derivative = gelu_parts(pre + shift)
            value, derivative = value.astype(jnp.bfloat16), derivative.astype(jnp.bfloat16)
            for c, at in enumerate(lanes):
                act[span(i, chunk), at] = value[:, c * size : (c + 1) * size]
                slope[span(i, chunk), at] = derivative[:, c * size : (c + 1) * size]

        queue.take()

    down = down_parts[0]

    @pl.loop(0, clips)
    def _(c):
        size = act.shape[1] // clips
        part = (mm(s.et[...], act[:, span(c, size)]) * grad_scale).astype(jnp.bfloat16)
        part = part.reshape(slabs, 2, -1, size)
        for h in range(2):
            down[:, c % 2, h, c // 2] = part[:, h]

    for flow in down_flows:
        flow.first()

    queue.until(down_copies[-1].fourth)
    for flow in down_copies:
        flow.last()

    def pre_back(c):
        cols = span(c, width)
        weights = whole_down[c].reshape(width, width)

        def step(i, sums):
            grad = mm_nt(eb[span(i, chunk), :], weights)
            low = grad * slope[span(i, chunk), cols].astype(jnp.float32)
            low = low.astype(jnp.bfloat16)
            slope[span(i, chunk), cols] = low
            return sums + jnp.sum(low.astype(jnp.float32), 0, keepdims=True)

        sums = lax.fori_loop(0, tok // chunk, step, jnp.zeros((1, width), jnp.float32))
        s.up_sum[c : c + 1, :] = sums

    for c in range(wide):
        pre_back(c)
        if c == 1:
            down_flows[0].second()
        if c == 2:
            down_flows[1].second()

    up = up_parts[0]

    def keep(target, slab, part):
        part = (part * grad_scale).astype(jnp.bfloat16)
        part = part.reshape(clips // 2, 2, 2, -1, part.shape[-1])
        for y in range(2):
            for h in range(2):
                target[slab, y, h] = part[:, y, h]

    @pl.loop(0, slabs)
    def _(i):
        keep(up, i, mm(s.mlp_in_t[...], slope[:, span(i, act.shape[1] // slabs)]))

    for flow in up_flows:
        flow.first()
    down_flows[0].third()
    down_flows[1].third()

    mid_grad, mid_low = s.mid_grad, s.mid_low

    def mid_step(i, sums):
        grad = mm_nt(slope[span(i, chunk), :], flat(whole_up))
        normed, inverse = norm_parts(mid[span(i, chunk), :])
        out_grad = eb[span(i, chunk), :].astype(jnp.float32)
        rows = out_grad + norm_back(normed, inverse, grad * vectors[5:6, :])
        low = rows.astype(jnp.bfloat16)
        mid_grad[span(i, chunk), :] = rows
        put_rows(mid_low, i, low)
        return tuple(
            old + jnp.sum(new, 0, keepdims=True)
            for old, new in zip(sums, (low.astype(jnp.float32), grad * normed, grad, out_grad))
        )

    zero = jnp.zeros((1, width), jnp.float32)
    mid_sums = lax.fori_loop(0, tok // chunk, mid_step, (zero,) * 4)
    for row, value in zip((4, 5, 6, 7), mid_sums):
        small.held[0, row : row + 1, :] = value * grad_scale
    small.held[0, 8:12, :] = s.up_sum[...] * grad_scale
    up_flows[0].second()
    up_flows[1].second()
    down_flows[0].fourth()

    proj_columns = flat(whole_proj)
    head_low = jnp.concatenate(
        [mid_low[heads[i]] for i in range(slots)], 0
    )
    put_rows(s.dlent, 0, mm_nt(head_low, proj_columns).astype(jnp.bfloat16))
    lend_back = links.send(s.dlent, s.dborrowed, before)
    dwin_own = s.dwin_own

    @pl.loop(0, tok // chunk)
    def _(i):
        rows = mm_nt(rows_of(mid_low, i, chunk), flat(whole_proj))
        put_rows(dwin_own, i, rows.astype(jnp.bfloat16))

    grad = mm(s.att_t[...], mid_low[...].reshape(tok, width))
    for i in range(slabs):
        keep(proj_flow.held, i, grad[:, i * (width // slabs) : (i + 1) * (width // slabs)])
    proj_flow.first()
    down_flows[1].fourth()
    up_flows[0].third()

    bias_grad, qg_win = s.bias_grad, s.qg_win
    bias_grad[...] = jnp.zeros_like(bias_grad)

    def backward(works):
        rows = [parts(window(own, u, j)) for u, j in works]
        places = [span(u * groups_unit + j, group) for u, j in works]
        mixed = [[stacked(g) for g in parts(window(dwin_own, u, j))[0]] for u, j in works]
        weights = [s.probs[at, :] for at in places]
        lows = [weight.astype(jnp.bfloat16) for weight in weights]
        prob_grads = [
            jnp.concatenate([mm_nt(v, g) for v, g in zip(values, grads)], 1)
            for (_, _, values), grads in zip(rows, mixed)
        ]
        value_grads = [
            [mm(low[:, 128 * t : 128 * (t + 1)], g) for t, g in enumerate(grads)]
            for low, grads in zip(lows, mixed)
        ]
        scores = [
            (weight * (grad - jnp.sum(weight * grad, 0, keepdims=True))).astype(jnp.bfloat16)
            for weight, grad in zip(weights, prob_grads)
        ]
        bias_grad[...] += sum(score.astype(jnp.float32) for score in scores)
        key_grads = [
            [
                mm(score[:, 128 * t : 128 * (t + 1)], stacked(q)) * score_scale
                for t, q in enumerate(queries)
            ]
            for score, (queries, _, _) in zip(scores, rows)
        ]
        query_grads = [
            [
                folded(mm_tn(score[:, 128 * t : 128 * (t + 1)], k)) * score_scale
                for t, k in enumerate(keys)
            ]
            for score, (_, keys, _) in zip(scores, rows)
        ]
        for (u, j), *grads in zip(works, query_grads, key_grads, value_grads):
            out = jnp.concatenate([tile for grad in grads for tile in grad], 1)
            out = out.astype(jnp.bfloat16).reshape(2, half, 3 * width)
            qg_win[span(u * groups_unit + j, 2)] = out

    def after_first():
        up_flows[1].third()
        proj_flow.second()

    def after_second():
        up_flows[0].fourth()

    def after_third():
        up_flows[1].fourth()
        proj_flow.third()

    sweep(
        backward,
        take_lent(lend_back, s.dborrowed, dwin_own),
        give_back_from(qg_win, s.qg_out, s.qg_back),
        after_first,
        after_second,
        after_third,
    )
    qg_rows = s.qg_rows
    from_windows(qg_win, qg_rows)

    pair = 2
    for i in range(slabs // pair):
        size = 3 * width // slabs
        grad = mm(s.attn_in_t[...], qg_rows[:, i * pair * size : (i + 1) * pair * size])
        for k in range(pair):
            keep(qkv_parts[0], i * pair + k, grad[:, k * size : (k + 1) * size])
    for flow in qkv_flows:
        flow.first()
    proj_flow.fourth()


    def in_step(i, sums):
        rows = qg_rows[span(i, chunk), :]
        grad = mm_nt(rows, flat(whole_qkv))
        normed, inverse = norm_parts(xb[span(i, chunk), :].astype(jnp.float32))
        back = norm_back(normed, inverse, grad * vectors[0:1, :])
        mid_grad[span(i, chunk), :] = mid_grad[span(i, chunk), :] + back
        query_part = rows[:, :width].astype(jnp.float32)
        value_part = rows[:, 2 * width :].astype(jnp.float32)
        return tuple(
            old + jnp.sum(new, 0, keepdims=True)
            for old, new in zip(sums, (grad * normed, grad, query_part, value_part))
        )

    in_sums = lax.fori_loop(0, tok // chunk, in_step, (zero,) * 4)
    store_grad = pltpu.make_async_copy(mid_grad, x_grad, s.load_sems.at[1])
    store_grad.start()
    for row, value in zip((0, 1, 2, 3), in_sums):
        small.held[0, row : row + 1, :] = value * grad_scale

    by_head = bias_grad[...]
    for r in range(RELS):
        picked = jnp.sum(jnp.where(offset == r, by_head, 0.0), 0, keepdims=True)
        s.att_sum[r : r + 1, :] = picked
    s.att_sum[RELS:, :] = jnp.zeros((128 - RELS, width), jnp.float32)
    sums = lax.dot_general(
        spread, s.att_sum[...], (((1,), (1,)), ((), ())), precision=HIGHEST
    ) * grad_scale
    for i in range(width // 128):
        small.held[0, 12:16, 128 * i : 128 * (i + 1)] = sums[4 * i : 4 * i + 4, :]

    small.first()
    for flow in qkv_flows:
        flow.second()
    small.second()

    out_low = s.out_low

    @pl.loop(0, tok // chunk)
    def _(i):
        rows = mid[span(i, chunk), :] + mm(act[span(i, chunk), :], flat(whole_down))
        live = lax.broadcasted_iota(jnp.int32, (chunk, width), 0) + i * chunk < used
        rows = jnp.where(live, rows + vectors[7:8, :], 0.0)
        out_low[span(i, chunk), :] = rows.astype(jnp.bfloat16)

    store_out = pltpu.make_async_copy(out_low, block_out, s.load_sems.at[0])
    store_out.start()

    for flow in qkv_flows:
        flow.third()
    small.third()

    def finish(flows, out, turn):
        for flow in flows:
            total, lanes = flow.last()
            rows = total.shape[1]
            if turn:
                out[lanes, :] = total.reshape(2 * rows, -1).T
            else:
                out[:rows, lanes] = total[0]
                out[rows:, lanes] = total[1]

    finish(down_flows, owned[3], True)
    finish(up_flows, owned[2], False)
    finish([proj_flow], owned[1], False)
    for flow in qkv_flows:
        flow.fourth()
    small.fourth()
    finish(qkv_flows, owned[0], False)
    small_out[...] = small.last()
    store_out.wait()
    store_grad.wait()
    links.drain()


BEGIN_AT, SECOND_AT, FRONT_AT, BACK_AT, WRAP_AT, HEADS_AT, TAILS_AT, USED_AT = range(8)


def unit_table(lengths, slab_size, tok):
    unit, half = SHORT // slab_size * BINS, WIN // 2 * BINS
    count, size = tok // unit, unit // half
    at = jnp.arange(count, dtype=jnp.int32)
    segment = lengths // slab_size * BINS // unit
    ends = jnp.cumsum(segment)
    starts = ends - segment
    slots = jnp.arange(1, lengths.shape[0] + 1, dtype=jnp.int32)
    here = (starts[:, None] <= at) & (at < ends[:, None])
    inside = jnp.sum(here, 0)
    last = jnp.sum(jnp.where(here & (ends[:, None] == at + 1), slots[:, None], 0), 0)
    first = jnp.sum(jnp.where(here & (starts[:, None] == at), slots[:, None], 0), 0)
    begin = at * size + inside
    front = jnp.maximum(at * size - inside, 0)
    blocks_own = tok // half
    pad = (0, count - lengths.shape[0])
    return jnp.stack([
        begin,
        jnp.where(last > 0, blocks_own + last - 1, begin + size - 1),
        jnp.where(first > 0, blocks_own + first - 1, front),
        at * size - inside + 1,
        ((last > 0) & (lax.axis_index(SLAB) == slab_size - 1)).astype(jnp.int32),
        jnp.pad(jnp.minimum(starts, count - 1) * size, pad),
        jnp.pad(jnp.maximum(ends * size - 1, 0), pad),
        jnp.full((count,), ends[-1] * unit),
    ]).astype(jnp.int32)


def block_call(tokens, y_grad, clip_rows, vectors, table, masters, slab_size, clip_size):
    vmem, smem, anywhere = (
        pl.BlockSpec(memory_space=pltpu.VMEM),
        pl.BlockSpec(memory_space=pltpu.SMEM),
        pl.BlockSpec(memory_space=pl.ANY),
    )
    depth = clip_size // 2
    tok, width = tokens.shape
    hidden = masters[2].shape[1] * slab_size
    slots = clip_rows.shape[1]
    half = WIN // 2 * BINS
    low, full = jnp.bfloat16, jnp.float32
    helds = []
    for position, master in enumerate(masters):
        rows, columns = master.shape if position < 3 else master.shape[::-1]
        helds.append((slab_size, 2, 2, depth, rows // 2, columns))
    def buffer(*sizes):
        kind = full if sizes[-1] is full else low
        return pltpu.VMEM(sizes[:-1] if sizes[-1] is full else sizes, kind)

    def whole(master):
        return buffer(depth, 2, 2, master.shape[0] // 2, slab_size * master.shape[1])

    held = Held(
        xb=buffer(tok, width), eb=buffer(tok, width), et=buffer(width, tok),
        attn_in=buffer(tok // half, half, width), attn_in_t=buffer(width, tok),
        own=buffer(tok // half + slots, half, 3 * width), lent=buffer(slots, half, 3 * width),
        borrowed=buffer(slots, half, 3 * width),
        probs=buffer(tok, width, full), att_win=buffer(tok // half + slots, half, width),
        att_out=buffer(slots, half, width), att_back=buffer(slots, half, width), att_rows=buffer(tok, width), att_t=buffer(width, tok),
        mid=buffer(tok, width, full), mlp_in=buffer(tok, width), mlp_in_t=buffer(width, tok),
        act=buffer(tok, hidden), slope=buffer(tok, hidden), mid_grad=buffer(tok, width, full),
        mid_low=buffer(tok // half, half, width), dwin_own=buffer(tok // half + slots, half, width), dlent=buffer(slots, half, width),
        dborrowed=buffer(slots, half, width), qg_win=buffer(tok // half + slots, half, 3 * width),
        qg_out=buffer(slots, half, 3 * width), qg_back=buffer(slots, half, 3 * width), qg_rows=buffer(tok, 3 * width),
        bias=buffer(2, WIN * BINS, width, full), bias_grad=buffer(WIN * BINS, width, full),
        up_sum=buffer(hidden // width, width, full), att_sum=buffer(128, width, full),
        out_low=buffer(tok, width),
        load_sems=pltpu.SemaphoreType.DMA((2,)),
        whole_qkv=whole(masters[0]), whole_proj=whole(masters[1]),
        whole_up=whole(masters[2]), whole_down=whole(masters[3]),
    )
    copies = 12 * (depth - 1 + 7) + 8 * (7 + depth - 1) + 3 + depth - 1 + 4
    scratch = [pltpu.SemaphoreType.DMA((copies,)), pltpu.SemaphoreType.DMA((copies,)), *held]
    small = (16, width)
    scratch += [
        pltpu.VMEM((3,) + small, full), pltpu.VMEM((3,) + small, full), pltpu.VMEM((depth,) + small, full)
    ]
    for sizes in helds:
        scratch += [pltpu.VMEM(sizes, low)] + scatter_buffers(sizes)
    return pl.pallas_call(
        functools.partial(block_kernel, slab_size, clip_size),
        out_shape=[
            jax.ShapeDtypeStruct((tok, width), low),
            jax.ShapeDtypeStruct((tok, width), full),
            jax.ShapeDtypeStruct(small, full),
        ]
        + [jax.ShapeDtypeStruct(m.shape, full) for m in masters],
        in_specs=[anywhere, anywhere, smem] + [vmem] * 6,
        out_specs=[anywhere, anywhere] + [vmem] * 5,
        scratch_shapes=scratch,
        compiler_params=pltpu.CompilerParams(
            collective_id=0, has_side_effects=True, vmem_limit_bytes=62 << 20
        ),
        name="block",
    )(tokens, y_grad, unit_table(clip_rows[0], slab_size, tok), vectors, table, *masters)


def shards(
    tokens,
    y_grad,
    clip_rows,
    qkv_weight,
    proj_weight,
    up_weight,
    down_weight,
    qkv_m,
    proj_m,
    up_m,
    down_m,
    qkv_v,
    proj_v,
    up_v,
    down_v,
    vectors,
    vectors_m,
    vectors_v,
    table,
    table_m,
    table_v,
):
    slab_size, clip_size = lax.axis_size(SLAB), lax.axis_size(CLIP)
    masters = (qkv_weight, proj_weight, up_weight, down_weight)
    hidden = up_weight.shape[1] * slab_size
    aligned = slab_size == 4 and clip_size % 2 == 0 and all(m.shape[0] % 32 == 0 for m in masters)
    if aligned and hidden // (clip_size // 2) == tokens.shape[-1]:
        block_out, x_grad, small, *owned = block_call(
            tokens[0, 0], y_grad[0, 0], clip_rows, vectors, table, masters, slab_size, clip_size
        )
        results = [block_out[None, None], x_grad[None, None]]
        moments = ((qkv_m, qkv_v), (proj_m, proj_v), (up_m, up_v), (down_m, down_v))
        for master, (first, second), grad in zip(masters, moments, owned):
            results += adamw(master, first, second, grad, rate_matrix, weight_decay)
        rows = vectors.shape[0]
        results += adamw(vectors, vectors_m, vectors_v, small[:rows], rate_vector, 0.0)
        by_head = small[rows : rows + 4].reshape(4, -1, 128).transpose(1, 0, 2).reshape(-1, 128)
        results += adamw(
            table, table_m, table_v, by_head[: table.shape[1], :RELS].T, rate_vector, 0.0
        )
        return tuple(results)
    lengths = clip_rows[0]
    slab_count = lax.axis_size(SLAB)
    inputs = tokens[0, 0].astype(jnp.float32)
    tok_count, width = inputs.shape
    rows_dev = tok_count // BINS
    head_dim = width // HEADS
    score_scale = head_dim ** (-0.5)
    source, time_wraps, seg_starts = window_rows(
        lengths, lax.axis_index(SLAB), slab_count, rows_dev
    )
    total_rows = rows_dev + 2 * lengths.shape[0]
    head_rows = jnp.minimum(
        seg_starts[:, None] + jnp.arange(2, dtype=jnp.int32)[None, :], rows_dev - 1
    ).reshape(-1)
    windows_count = source.shape[0] * (BINS // WIN)
    bin_folds = jnp.arange(windows_count) % (BINS // WIN) == BINS // WIN - 1
    allowed = window_mask(jnp.repeat(time_wraps, BINS // WIN), bin_folds)[:, None]
    offset_hot = offset_table()
    rel_bias = (
        jnp.dot(offset_hot, table, precision=HIGHEST)
        .reshape(WIN * WIN, WIN * WIN, HEADS)
        .transpose(2, 0, 1)
    )
    used_rows = jnp.sum(lengths) // slab_count
    live_rows = (jnp.arange(tok_count) // BINS < used_rows).astype(jnp.float32)[:, None]
    part_copies = (
        lax.all_gather(qkv_weight.astype(jnp.bfloat16), CLIP, axis=0, tiled=True),
        lax.all_gather(proj_weight.astype(jnp.bfloat16), CLIP, axis=0, tiled=True),
        lax.all_gather(up_weight.astype(jnp.bfloat16), CLIP, axis=0, tiled=True),
        lax.all_gather(down_weight.astype(jnp.bfloat16), CLIP, axis=0, tiled=True),
    )
    copies = (
        lax.all_gather(part_copies[0], SLAB, axis=1, tiled=True),
        lax.all_gather(part_copies[1], SLAB, axis=1, tiled=True),
        lax.all_gather(part_copies[2], SLAB, axis=1, tiled=True),
        lax.all_gather(part_copies[3], SLAB, axis=1, tiled=True),
    )
    qkv_copy, proj_copy, up_copy, down_copy = copies
    attn_input = affine_norm(inputs, vectors[0], vectors[1]).astype(jnp.bfloat16)
    bias_row = jnp.concatenate([vectors[2], jnp.zeros_like(vectors[2]), vectors[3]])
    qkv_rows = (
        jnp.dot(attn_input, qkv_copy, preferred_element_type=jnp.float32) + bias_row
    ).astype(jnp.bfloat16)
    qkv_grid = qkv_rows.reshape(rows_dev, BINS, 3 * width)
    borrowed = from_behind(qkv_grid[head_rows], SLAB, -1)
    qkv_windows = to_windows(jnp.concatenate([qkv_grid, borrowed], 0), source)
    query_win = qkv_windows[:, :, :width].reshape(windows_count, WIN * WIN, HEADS, head_dim)
    key_win = qkv_windows[:, :, width : 2 * width].reshape(
        windows_count, WIN * WIN, HEADS, head_dim
    )
    value_win = qkv_windows[:, :, 2 * width :].reshape(windows_count, WIN * WIN, HEADS, head_dim)

    def scores_of(queries, keys_all):
        raw = (
            jnp.einsum("wqhd,wkhd->whqk", queries, keys_all, preferred_element_type=jnp.float32)
            * score_scale
            + rel_bias[None]
        )
        return jnp.where(allowed, raw, masked_score)

    scores = scores_of(query_win, key_win)
    top_score = jnp.max(scores, -1, keepdims=True)
    exp_sum = jnp.sum(jnp.exp(scores - top_score), -1, keepdims=True)
    probs_low = (jnp.exp(scores - top_score) / exp_sum).astype(jnp.bfloat16)
    attended = jnp.einsum(
        "whqk,wkhd->wqhd", probs_low, value_win, preferred_element_type=jnp.float32
    )
    attended = attended.astype(jnp.bfloat16).reshape(windows_count, WIN * WIN, width)
    spread_out = from_windows(attended, source, total_rows)
    returned = from_behind(spread_out[rows_dev:], SLAB, 1)
    attended_rows = spread_out[:rows_dev].at[head_rows].add(returned).reshape(tok_count, width)
    residual = (
        inputs + jnp.dot(attended_rows, proj_copy, preferred_element_type=jnp.float32) + vectors[4]
    )
    mlp_input = affine_norm(residual, vectors[5], vectors[6]).astype(jnp.bfloat16)
    pre_gelu = jnp.dot(mlp_input, up_copy, preferred_element_type=jnp.float32) + vectors[
        8:
    ].reshape(-1)
    activated, gelu_pull = jax.vjp(gelu_exact, pre_gelu)
    activated_low = activated.astype(jnp.bfloat16)
    block_out = (
        residual
        + jnp.dot(activated_low, down_copy, preferred_element_type=jnp.float32)
        + vectors[7]
    ) * live_rows
    out_grad = y_grad[0, 0].astype(jnp.float32) * live_rows
    out_low = out_grad.astype(jnp.bfloat16)
    down_grad = jnp.dot(activated_low.T, out_low, preferred_element_type=jnp.float32)
    act_grad = jnp.dot(out_low, down_copy.T, preferred_element_type=jnp.float32)
    pre_low = gelu_pull(act_grad)[0].astype(jnp.bfloat16)
    up_grad = jnp.dot(mlp_input.T, pre_low, preferred_element_type=jnp.float32)
    mlp_in_grad = jnp.dot(pre_low, up_copy.T, preferred_element_type=jnp.float32)
    norm_value, norm_pull = jax.vjp(affine_norm, residual, vectors[5], vectors[6])
    resid_norm_grad, gain_two_grad, shift_two_grad = norm_pull(mlp_in_grad)
    resid_grad = out_grad + resid_norm_grad
    attn_low = resid_grad.astype(jnp.bfloat16)
    proj_grad = jnp.dot(attended_rows.T, attn_low, preferred_element_type=jnp.float32)
    mixed_grad = jnp.dot(attn_low, proj_copy.T, preferred_element_type=jnp.float32).astype(
        jnp.bfloat16
    )
    mixed_grid = mixed_grad.reshape(rows_dev, BINS, width)
    sent_back = from_behind(mixed_grid[head_rows], SLAB, -1)
    grad_windows = to_windows(jnp.concatenate([mixed_grid, sent_back], 0), source)
    grad_windows = grad_windows.reshape(windows_count, WIN * WIN, HEADS, head_dim)
    probs = jnp.exp(scores_of(query_win, key_win) - top_score) / exp_sum
    prob_grad = jnp.einsum(
        "wqhd,wkhd->whqk", grad_windows, value_win, preferred_element_type=jnp.float32
    )
    value_grad = jnp.einsum(
        "whqk,wqhd->wkhd", probs_low, grad_windows, preferred_element_type=jnp.float32
    )
    score_grad = (probs * (prob_grad - jnp.sum(probs * prob_grad, -1, keepdims=True))).astype(
        jnp.bfloat16
    )
    bias_grad = (
        jnp.sum(score_grad.astype(jnp.float32), 0)
        .transpose(1, 2, 0)
        .reshape(WIN * WIN * WIN * WIN, HEADS)
    )
    table_grad = jnp.dot(offset_hot.T, bias_grad, precision=HIGHEST)
    query_grad = (
        jnp.einsum("whqk,wkhd->wqhd", score_grad, key_win, preferred_element_type=jnp.float32)
        * score_scale
    )
    key_grad = (
        jnp.einsum("whqk,wqhd->wkhd", score_grad, query_win, preferred_element_type=jnp.float32)
        * score_scale
    )
    qkv_grad_win = jnp.concatenate(
        [
            query_grad.reshape(windows_count, WIN * WIN, width),
            key_grad.reshape(windows_count, WIN * WIN, width),
            value_grad.reshape(windows_count, WIN * WIN, width),
        ],
        -1,
    ).astype(jnp.bfloat16)
    qkv_spread = from_windows(qkv_grad_win, source, total_rows)
    given_back = from_behind(qkv_spread[rows_dev:], SLAB, 1)
    qkv_grad_rows = (
        qkv_spread[:rows_dev].at[head_rows].add(given_back).reshape(tok_count, 3 * width)
    )
    qkv_w_grad = jnp.dot(attn_input.T, qkv_grad_rows, preferred_element_type=jnp.float32)
    bias_sums = jnp.sum(qkv_grad_rows.astype(jnp.float32), 0)
    attn_in_grad = jnp.dot(qkv_grad_rows, qkv_copy.T, preferred_element_type=jnp.float32)
    first_value, norm_pull_one = jax.vjp(affine_norm, inputs, vectors[0], vectors[1])
    inputs_norm_grad, gain_one_grad, shift_one_grad = norm_pull_one(attn_in_grad)
    x_grad = resid_grad + inputs_norm_grad
    vector_grad = jnp.concatenate(
        [
            jnp.stack(
                [
                    gain_one_grad,
                    shift_one_grad,
                    bias_sums[:width],
                    bias_sums[2 * width :],
                    jnp.sum(attn_low.astype(jnp.float32), 0),
                    gain_two_grad,
                    shift_two_grad,
                    jnp.sum(out_grad, 0),
                ]
            ),
            jnp.sum(pre_low.astype(jnp.float32), 0).reshape(-1, width),
        ],
        0,
    )
    grad_scale = float(tok_count * slab_count * lax.axis_size(CLIP)) ** (-0.5)
    part_sums = (
        lax.psum_scatter(
            (qkv_w_grad * grad_scale).astype(jnp.bfloat16), SLAB, scatter_dimension=1, tiled=True
        ).astype(jnp.float32),
        lax.psum_scatter(
            (proj_grad * grad_scale).astype(jnp.bfloat16), SLAB, scatter_dimension=1, tiled=True
        ).astype(jnp.float32),
        lax.psum_scatter(
            (up_grad * grad_scale).astype(jnp.bfloat16), SLAB, scatter_dimension=1, tiled=True
        ).astype(jnp.float32),
        lax.psum_scatter(
            (down_grad * grad_scale).astype(jnp.bfloat16), SLAB, scatter_dimension=1, tiled=True
        ).astype(jnp.float32),
    )
    owned = (
        lax.psum_scatter(part_sums[0], CLIP, scatter_dimension=0, tiled=True),
        lax.psum_scatter(part_sums[1], CLIP, scatter_dimension=0, tiled=True),
        lax.psum_scatter(part_sums[2], CLIP, scatter_dimension=0, tiled=True),
        lax.psum_scatter(part_sums[3], CLIP, scatter_dimension=0, tiled=True),
    )
    small_sums = lax.psum((vector_grad * grad_scale, table_grad * grad_scale), (SLAB, CLIP))
    qkv_new, qkv_m_new, qkv_v_new = adamw(
        qkv_weight, qkv_m, qkv_v, owned[0], rate_matrix, weight_decay
    )
    proj_new, proj_m_new, proj_v_new = adamw(
        proj_weight, proj_m, proj_v, owned[1], rate_matrix, weight_decay
    )
    up_new, up_m_new, up_v_new = adamw(up_weight, up_m, up_v, owned[2], rate_matrix, weight_decay)
    down_new, down_m_new, down_v_new = adamw(
        down_weight, down_m, down_v, owned[3], rate_matrix, weight_decay
    )
    vectors_new, vectors_m_new, vectors_v_new = adamw(
        vectors, vectors_m, vectors_v, small_sums[0], rate_vector, 0.0
    )
    table_new, table_m_new, table_v_new = adamw(
        table, table_m, table_v, small_sums[1], rate_vector, 0.0
    )
    out_shape = (1, 1, tok_count, width)
    return (
        block_out.astype(jnp.bfloat16).reshape(out_shape),
        x_grad.reshape(out_shape),
        qkv_new,
        qkv_m_new,
        qkv_v_new,
        proj_new,
        proj_m_new,
        proj_v_new,
        up_new,
        up_m_new,
        up_v_new,
        down_new,
        down_m_new,
        down_v_new,
        vectors_new,
        vectors_m_new,
        vectors_v_new,
        table_new,
        table_m_new,
        table_v_new,
    )


def solution(mesh):
    return jax.shard_map(
        shards,
        mesh=mesh,
        in_specs=(
            P(CLIP, SLAB, None, None),
            P(CLIP, SLAB, None, None),
            P(CLIP, None),
            P(CLIP, SLAB),
            P(CLIP, SLAB),
            P(CLIP, SLAB),
            P(CLIP, SLAB),
            P(CLIP, SLAB),
            P(CLIP, SLAB),
            P(CLIP, SLAB),
            P(CLIP, SLAB),
            P(CLIP, SLAB),
            P(CLIP, SLAB),
            P(CLIP, SLAB),
            P(CLIP, SLAB),
            P(),
            P(),
            P(),
            P(),
            P(),
            P(),
        ),
        out_specs=(
            P(CLIP, SLAB, None, None),
            P(CLIP, SLAB, None, None),
            P(CLIP, SLAB),
            P(CLIP, SLAB),
            P(CLIP, SLAB),
            P(CLIP, SLAB),
            P(CLIP, SLAB),
            P(CLIP, SLAB),
            P(CLIP, SLAB),
            P(CLIP, SLAB),
            P(CLIP, SLAB),
            P(CLIP, SLAB),
            P(CLIP, SLAB),
            P(CLIP, SLAB),
            P(),
            P(),
            P(),
            P(),
            P(),
            P(),
        ),
        check_vma=False,
    )
```

```python
import functools
import itertools
import math
import typing

import jax
import jax.numpy as jnp
from jax import lax
from jax.experimental import pallas as pl
from jax.experimental.pallas import tpu as pltpu
from jax.sharding import PartitionSpec as P

HEADS = 16
BINS = 8
WIN = 4
STEP = 10
RELS = 49
SLAB, CLIP = "slab", "clip"
SHORT = 64


HIGHEST = lax.Precision.HIGHEST
norm_epsilon = 1e-06
beta_first = 0.5
beta_second = 0.5
adam_epsilon = 1e-08
rate_matrix = 0.05
rate_vector = 0.5
weight_decay = 0.05
masked_score = -1e30


def from_behind(block, axis, distance):
    devices = range(lax.axis_size(axis))
    route = [((i - distance) % len(devices), i) for i in devices]
    return lax.ppermute(block, axis, route)


def layer_norm(values):
    center = values - jnp.mean(values, -1, keepdims=True)
    spread = jnp.mean(center * center, -1, keepdims=True)
    return center * lax.rsqrt(spread + norm_epsilon)


def affine_norm(values, gain, offset):
    return layer_norm(values) * gain + offset


def gelu_exact(values):
    return jax.nn.gelu(values, approximate=False)


def window_rows(lengths, slab_index, slab_count, rows_dev):
    segment = lengths // slab_count
    seg_ends = jnp.cumsum(segment)
    seg_starts = seg_ends - segment
    row_base = WIN * jnp.arange(rows_dev // WIN, dtype=jnp.int32)
    inside = (row_base[:, None] >= seg_starts[None, :]) & (row_base[:, None] < seg_ends[None, :])
    in_clip = jnp.any(inside, axis=1)
    slot_ids = jnp.arange(lengths.shape[0], dtype=jnp.int32)
    clip_end = jnp.sum(jnp.where(inside, seg_ends[None, :], 0), axis=1)
    clip_slot = jnp.sum(jnp.where(inside, slot_ids[None, :], 0), axis=1)
    row_ids = (
        row_base[:, None]
        + jnp.where(in_clip, WIN // 2, 0)[:, None]
        + jnp.arange(WIN, dtype=jnp.int32)[None, :]
    )
    beyond = in_clip[:, None] & (row_ids >= clip_end[:, None])
    source = jnp.where(
        beyond, rows_dev + 2 * clip_slot[:, None] + row_ids - clip_end[:, None], row_ids
    )
    time_wraps = in_clip & (row_base + WIN == clip_end) & (slab_index == slab_count - 1)
    return (source, time_wraps, seg_starts)


def window_mask(time_wraps, bin_folds):
    positions = jnp.arange(WIN * WIN, dtype=jnp.int32)
    row_half = positions // WIN >= WIN // 2
    bin_half = positions % WIN >= WIN // 2
    same_row = row_half[:, None] == row_half[None, :]
    same_bin = bin_half[:, None] == bin_half[None, :]
    return (~time_wraps[:, None, None] | same_row[None]) & (
        ~bin_folds[:, None, None] | same_bin[None]
    )


def offset_table():
    positions = jnp.arange(WIN * WIN, dtype=jnp.int32)
    row_pos = positions // WIN
    bin_pos = positions % WIN
    offsets = (row_pos[:, None] - row_pos[None, :] + WIN - 1) * (2 * WIN - 1) + (
        bin_pos[:, None] - bin_pos[None, :] + WIN - 1
    )
    return (offsets.reshape(-1)[:, None] == jnp.arange(RELS, dtype=jnp.int32)[None, :]).astype(
        jnp.float32
    )


def to_windows(extended, source):
    gathered = jnp.roll(extended[source], -(WIN // 2), axis=2)
    win_rows = source.shape[0]
    width = extended.shape[-1]
    gathered = gathered.reshape(win_rows, WIN, BINS // WIN, WIN, width).transpose(0, 2, 1, 3, 4)
    return gathered.reshape(win_rows * (BINS // WIN), WIN * WIN, width)


def from_windows(windows, source, total_rows):
    win_rows = source.shape[0]
    width = windows.shape[-1]
    placed = windows.reshape(win_rows, BINS // WIN, WIN, WIN, width).transpose(0, 2, 1, 3, 4)
    placed = jnp.roll(placed.reshape(win_rows, WIN, BINS, width), WIN // 2, axis=2)
    blank = jnp.zeros((total_rows, BINS, width), windows.dtype)
    return blank.at[source.reshape(-1)].set(placed.reshape(win_rows * WIN, BINS, width))


def adamw(weight, first, second, grad, rate, decay):
    first = beta_first * first + (1.0 - beta_first) * grad
    second = beta_second * second + (1.0 - beta_second) * grad * grad
    fix_first = 1.0 - beta_first**STEP
    fix_second = 1.0 - beta_second**STEP
    update = first / fix_first / (jnp.sqrt(second / fix_second) + adam_epsilon)
    return (weight - rate * (update + decay * weight), first, second)


MESH = pl.DeviceIdType.MESH


class Links:
    def __init__(self, send_sems, recv_sems):
        self.send_sems, self.recv_sems = send_sems, recv_sems
        self.count, self.started = 0, []

    def send(self, source, target, device):
        copy = pltpu.make_async_remote_copy(
            src_ref=source,
            dst_ref=target,
            send_sem=self.send_sems.at[self.count],
            recv_sem=self.recv_sems.at[self.count],
            device_id=device,
            device_id_type=MESH,
        )
        copy.start()
        self.count += 1
        self.started.append(copy)
        return copy

    def drain(self):
        for copy in self.started:
            copy.wait_send()


class Place:
    def __init__(self, clip_size):
        self.slab, self.clip = lax.axis_index(SLAB), lax.axis_index(CLIP)
        self.x, self.core = self.slab // 2, self.slab % 2
        self.z, self.y = self.clip // 2, self.clip % 2
        self.depth = clip_size // 2
        self.over_core = (self.x * 2 + 1 - self.core, self.clip)
        self.over_x = ((1 - self.x) * 2 + self.core, self.clip)
        self.over_y = (self.slab, self.z * 2 + 1 - self.y)
        self.over_diagonal = ((1 - self.x) * 2 + 1 - self.core, self.clip)
        self.x_slab = (1 - self.x) * 2 + self.core
        self.core_slab = self.x * 2 + 1 - self.core
        self.partners = [self.over_core, self.over_x, self.over_y, self.over_diagonal]
        self.partners += [self.over_z(step) for step in range(1, self.depth)]

    def z_at(self, step):
        return lax.rem(self.z + step, self.depth)

    def over_z(self, step):
        return (self.slab, self.z_at(step) * 2 + self.y)

    def greet(self):
        barrier = pltpu.get_barrier_semaphore()
        for partner in self.partners:
            pl.semaphore_signal(barrier, inc=1, device_id=partner, device_id_type=MESH)

    def meet(self):
        pl.semaphore_wait(pltpu.get_barrier_semaphore(), len(self.partners))


def wait_all(copies):
    for copy in copies:
        copy.wait_recv()


class Gather:
    def __init__(self, place, links, whole, width, rows, columns):
        self.place, self.links, self.whole = place, links, whole
        self.width, self.rows, self.columns = width, rows, columns

    def move(self, device, z, y, half, slab):
        start, size = self.columns(slab)
        lanes = pl.ds(pl.multiple_of(slab * self.width + start, 128), size)
        block = self.whole.at[z, y, half, self.rows, lanes]
        return self.links.send(block, block, device)

    def first(self):
        place = self.place
        self.copies = [
            self.move(place.over_z(step), place.z, place.y, EVERY, place.slab)
            for step in range(1, place.depth)
        ]

    def second(self):
        place = self.place
        wait_all(self.copies)
        self.first_x = self.move(place.over_x, EVERY, place.y, 0, place.slab)
        self.first_y = self.move(place.over_y, EVERY, place.y, 1, place.slab)

    def third(self):
        place = self.place
        self.first_x.wait_recv()
        self.last_y = [
            self.move(place.over_y, EVERY, place.y, 0, slab) for slab in (place.slab, place.x_slab)
        ]
        self.first_y.wait_recv()
        self.last_x = self.move(place.over_x, EVERY, EVERY, 1, place.slab)

    def fourth(self):
        place = self.place
        wait_all(self.last_y)
        self.last_x.wait_recv()
        self.copies = [
            self.move(place.over_core, EVERY, EVERY, EVERY, slab)
            for slab in (place.slab, place.x_slab)
        ]

    def last(self):
        wait_all(self.copies)


class Scatter:
    def __init__(self, place, links, buffers, columns):
        self.place, self.links, self.columns = place, links, columns
        self.held, self.from_core, self.first_y, self.first_x = buffers[:4]
        self.last_x, self.last_y, self.from_z = buffers[4:]

    def lanes(self, slab):
        start, size = self.columns(slab)
        return pl.ds(pl.multiple_of(start, 128), size)

    def add(self, index, arrived, slab):
        lanes = self.lanes(slab)
        index = (slab, *index, EVERY, lanes)
        self.held[index] = self.held[index] + arrived[..., lanes]

    def first(self):
        place = self.place
        self.copies = []
        for x in range(2):
            slab = 2 * x + 1 - place.core
            lanes = self.lanes(slab)
            source = self.held.at[slab, :, :, :, :, lanes]
            target = self.from_core.at[x, :, :, :, :, lanes]
            self.copies.append(self.links.send(source, target, place.over_core))

    def second(self):
        place = self.place
        for x in range(2):
            self.copies[x].wait_recv()
            self.add((EVERY, EVERY, EVERY), self.from_core.at[x], 2 * x + place.core)
        self.copies = []
        for x in range(2):
            slab = 2 * x + place.core
            lanes = self.lanes(slab)
            source = self.held.at[slab, 1 - place.y, 0, :, :, lanes]
            target = self.first_y.at[x, :, :, lanes]
            self.copies.append(self.links.send(source, target, place.over_y))
        lanes = self.lanes(place.x_slab)
        source = self.held.at[place.x_slab, :, 1, :, :, lanes]
        target = self.first_x.at[:, :, :, lanes]
        self.copy = self.links.send(source, target, place.over_x)

    def third(self):
        place = self.place
        for x in range(2):
            self.copies[x].wait_recv()
            self.add((place.y, 0, EVERY), self.first_y.at[x], 2 * x + place.core)
        lanes = self.lanes(place.x_slab)
        source = self.held.at[place.x_slab, place.y, 0, :, :, lanes]
        copy_x = self.links.send(source, self.last_x.at[:, :, lanes], place.over_x)
        self.copy.wait_recv()
        self.add((EVERY, 1, EVERY), self.first_x, place.slab)
        lanes = self.lanes(place.slab)
        source = self.held.at[place.slab, 1 - place.y, 1, :, :, lanes]
        copy_y = self.links.send(source, self.last_y.at[:, :, lanes], place.over_y)
        self.copies = [copy_x, copy_y]

    def fourth(self):
        place = self.place
        lanes = self.lanes(place.slab)
        for half, arrived in enumerate((self.last_x, self.last_y)):
            self.copies[half].wait_recv()
            self.add((place.y, half, EVERY), arrived, place.slab)
        self.copies = []
        for step in range(1, place.depth):
            source = self.held.at[place.slab, place.y, :, place.z_at(step), :, lanes]
            target = self.from_z.at[step - 1, :, :, lanes]
            self.copies.append(self.links.send(source, target, place.over_z(step)))

    def last(self):
        place = self.place
        lanes = self.lanes(place.slab)
        total = self.held[place.slab, place.y, :, place.z, :, lanes].astype(jnp.float32)
        for step in range(1, place.depth):
            self.copies[step - 1].wait_recv()
            total += self.from_z[step - 1, :, :, lanes].astype(jnp.float32)
        return total, lanes


class Small:
    def __init__(self, place, links, held, arrived, line):
        self.place, self.links, self.held = place, links, held
        self.arrived, self.line = arrived, line

    def first(self):
        self.copy = self.links.send(self.held.at[0], self.arrived.at[0], self.place.over_core)

    def second(self):
        self.copy.wait_recv()
        self.held[1] = self.held[0] + self.arrived[0]
        self.copy = self.links.send(self.held.at[1], self.arrived.at[1], self.place.over_x)

    def third(self):
        self.copy.wait_recv()
        self.held[2] = self.held[1] + self.arrived[1]
        self.copy = self.links.send(self.held.at[2], self.arrived.at[2], self.place.over_y)

    def fourth(self):
        place = self.place
        self.copy.wait_recv()
        self.line[place.z] = self.held[2] + self.arrived[2]
        self.copies = [
            self.links.send(self.line.at[place.z], self.line.at[place.z], place.over_z(step))
            for step in range(1, place.depth)
        ]

    def last(self):
        wait_all(self.copies)
        total = self.line[0]
        for z in range(1, self.place.depth):
            total += self.line[z]
        return total


class Queue:
    def __init__(self, steps):
        self.steps = list(steps)

    def take(self, count=1):
        for _ in range(min(count, len(self.steps))):
            for stage in self.steps.pop(0):
                stage()

    def until(self, stage):
        while any(stage in step for step in self.steps):
            self.take()


def staggered(flows, ahead, lag):
    steps = []
    for k in range(len(flows) + lag):
        step = [flows[k].third] if k < len(flows) else []
        step += [flows[k + ahead].second] if k + ahead < len(flows) else []
        step += [flows[k - lag].fourth] if 0 <= k - lag < len(flows) else []
        steps.append(step)
    return steps


EVERY = slice(None)


def cut(total, count):
    size = total // count
    return [lambda slab, k=k: (k * size, size) for k in range(count)]


def turned(total, count):
    size = total // count
    return [lambda slab, k=k: ((slab + k) % count * size, size) for k in range(count)]


def scatter_buffers(shape):
    slabs, _, _, depth, rows, columns = shape
    return [
        pltpu.VMEM((2, 2, 2, depth, rows, columns), jnp.bfloat16),
        pltpu.VMEM((2, depth, rows, columns), jnp.bfloat16),
        pltpu.VMEM((2, depth, rows, columns), jnp.bfloat16),
        pltpu.VMEM((depth, rows, columns), jnp.bfloat16),
        pltpu.VMEM((depth, rows, columns), jnp.bfloat16),
        pltpu.VMEM((depth - 1, 2, rows, columns), jnp.bfloat16),
    ]


def norm_parts(values):
    center = values - jnp.mean(values, -1, keepdims=True)
    inverse = lax.rsqrt(jnp.mean(center * center, -1, keepdims=True) + norm_epsilon)
    return center * inverse, inverse


def norm_back(normed, inverse, grad):
    return inverse * (
        grad
        - jnp.mean(grad, -1, keepdims=True)
        - normed * jnp.mean(grad * normed, -1, keepdims=True)
    )


def gelu_parts(values):
    below = 0.5 + 0.5 * lax.erf(values * (0.5**0.5))
    density = jnp.exp(-0.5 * values * values) * ((0.5 / math.pi) ** 0.5)
    return values * below, below + values * density


def mm(left, right):
    return jnp.dot(left, right, preferred_element_type=jnp.float32)


def mm_nt(left, right):
    return lax.dot_general(
        left, right, (((1,), (1,)), ((), ())), preferred_element_type=jnp.float32
    )


def mm_tn(left, right):
    return lax.dot_general(
        left, right, (((0,), (0,)), ((), ())), preferred_element_type=jnp.float32
    )


def span(index, size):
    return pl.ds(pl.multiple_of(index * size, size), size)


def blocks(ref, index, count):
    return jnp.concatenate([ref[index + k] for k in range(count)], 0)


def rows_of(ref, index, size):
    value = ref[span(index, size // ref.shape[1])]
    return value.reshape(size, value.shape[-1])


def put_rows(ref, index, value):
    count = value.shape[0] // ref.shape[1]
    ref[span(index, count)] = value.reshape(count, ref.shape[1], value.shape[-1])


def flat(ref, columns=slice(None)):
    block = ref[:, :, :, :, columns]
    return block.reshape(-1, block.shape[-1])


class Held(typing.NamedTuple):
    xb: typing.Any
    eb: typing.Any
    et: typing.Any
    attn_in: typing.Any
    attn_in_t: typing.Any
    own: typing.Any
    lent: typing.Any
    borrowed: typing.Any
    probs: typing.Any
    att_win: typing.Any
    att_out: typing.Any
    att_back: typing.Any
    att_rows: typing.Any
    att_t: typing.Any
    mid: typing.Any
    mlp_in: typing.Any
    mlp_in_t: typing.Any
    act: typing.Any
    slope: typing.Any
    mid_grad: typing.Any
    mid_low: typing.Any
    dwin_own: typing.Any
    dlent: typing.Any
    dborrowed: typing.Any
    qg_win: typing.Any
    qg_out: typing.Any
    qg_back: typing.Any
    qg_rows: typing.Any
    bias: typing.Any
    bias_grad: typing.Any
    up_sum: typing.Any
    att_sum: typing.Any
    units: typing.Any
    load_sems: typing.Any
    whole_qkv: typing.Any
    whole_proj: typing.Any
    whole_up: typing.Any
    whole_down: typing.Any


def block_kernel(slabs, clips, *refs):
    refs = list(refs)
    tokens, y_grad, clip_rows, vectors, table = refs[:5]
    masters = refs[5:9]
    block_out, x_grad, small_out = refs[9:12]
    owned = refs[12:16]
    rest = refs[16:]
    place = Place(clips)
    links = Links(rest.pop(0), rest.pop(0))
    s = Held(*rest[: len(Held._fields)])
    rest = rest[len(Held._fields) :]
    small = Small(place, links, rest.pop(0), rest.pop(0), rest.pop(0))
    qkv_parts, proj_parts, up_parts, down_parts = [
        [rest.pop(0) for _ in range(7)] for _ in masters
    ]
    qkv_flows = [Scatter(place, links, qkv_parts, c) for c in turned(masters[0].shape[1], 3)]
    proj_flow = Scatter(place, links, proj_parts, cut(masters[1].shape[1], 1)[0])
    up_flows = [Scatter(place, links, up_parts, c) for c in cut(masters[2].shape[1], 2)]
    down_flows = [Scatter(place, links, down_parts, c) for c in cut(masters[3].shape[0], 2)]
    xb, eb, own, bias = s.xb, s.eb, s.own, s.bias
    tok, width = xb.shape
    unit = SHORT // slabs * BINS
    unit_count = tok // unit
    half = WIN // 2 * BINS
    per_unit = unit // half
    group = WIN * BINS
    head = width // HEADS
    pack = 128 // head
    tiles = width // 128
    score_scale = head**-0.5
    grad_scale = float(tok * slabs * clips) ** -0.5
    slots = s.lent.shape[1]

    loads = [
        pltpu.make_async_copy(tokens, xb, s.load_sems.at[0]),
        pltpu.make_async_copy(y_grad, eb, s.load_sems.at[1]),
    ]
    for load in loads:
        load.start()
    place.greet()
    wholes = (s.whole_qkv, s.whole_proj, s.whole_up, s.whole_down)
    for whole, master in zip(wholes, masters):
        rows, width_own = whole.shape[3], master.shape[1]
        lanes = pl.ds(pl.multiple_of(place.slab * width_own, 128), width_own)
        for h in range(2):
            block = master[h * rows : (h + 1) * rows, :].astype(jnp.bfloat16)
            whole[place.z, place.y, h, :, lanes] = block

    def gathers(index, ranges, rows=(EVERY,)):
        return [
            Gather(place, links, wholes[index], masters[index].shape[1], r, c)
            for r in rows
            for c in ranges
        ]

    qkv_copies = gathers(0, turned(masters[0].shape[1], 3))
    proj_copies = gathers(1, cut(masters[1].shape[1], 1))
    up_copies = gathers(2, cut(masters[2].shape[1], 4))
    quarter = s.whole_down.shape[3] // 4
    down_copies = gathers(
        3, cut(masters[3].shape[1], 1), [pl.ds(k * quarter, quarter) for k in range(4)]
    )
    later = proj_copies + up_copies
    later = proj_copies + up_copies + down_copies
    copy_0, copy_1, copy_2 = qkv_copies
    queue = Queue(
        [
            [flow.first for flow in qkv_copies],
            [flow.second for flow in qkv_copies] + [flow.first for flow in later[:3]],
            [flow.third for flow in qkv_copies] + [flow.first for flow in later[3:]],
            [copy_0.fourth, copy_1.fourth] + [flow.second for flow in later[:3]],
            [copy_2.fourth],
        ]
        + staggered(later, 3, 2)
    )
    place.meet()
    queue.until(qkv_copies[-1].first)

    units, count = s.units, tok // unit
    starts, ends, position = [], [], 0
    for slot in range(slots):
        starts.append(position)
        position = position + clip_rows[0, slot] // (slabs * unit // BINS)
        ends.append(position)
    for u in range(count):
        inside, last, first = 0, 0, 0
        for slot in range(slots):
            here = jnp.where((starts[slot] <= u) & (u < ends[slot]), 1, 0)
            inside += here
            last += here * jnp.where(ends[slot] == u + 1, 1 + slot, 0)
            first += here * jnp.where(starts[slot] == u, 1 + slot, 0)
        begin, back = u * per_unit + inside, u * per_unit - inside
        units[BEGIN_AT, u] = begin
        units[SECOND_AT, u] = jnp.where(last > 0, tok // half + last - 1, begin + per_unit - 1)
        units[FRONT_AT, u] = jnp.where(first > 0, tok // half + first - 1, jnp.maximum(back, 0))
        units[BACK_AT, u] = back + 1
        units[WRAP_AT, u] = jnp.where((last > 0) & (place.slab == slabs - 1), 1, 0)
    heads = [jnp.minimum(starts[slot], count - 1) * per_unit for slot in range(slots)]
    tails = [jnp.maximum(ends[slot] * per_unit - 1, 0) for slot in range(slots)]
    used = position * unit

    heads_of = lax.broadcasted_iota(jnp.int32, (HEADS, width), 1) // head
    spread = (heads_of == lax.broadcasted_iota(jnp.int32, (HEADS, width), 0)).astype(jnp.float32)
    by_offset = lax.dot_general(
        table[...], spread, (((0,), (0,)), ((), ())), precision=HIGHEST
    )
    key = lax.broadcasted_iota(jnp.int32, (group, width), 0)
    query = lax.broadcasted_iota(jnp.int32, (group, width), 1) % group
    key_row, key_bin, query_row, query_bin = key // BINS, key % BINS, query // BINS, query % BINS
    key_place, query_place = (key_bin - WIN // 2) % BINS, (query_bin - WIN // 2) % BINS
    key_class = key_place // WIN + jnp.where(key_place >= WIN + WIN // 2, 1, 0)
    query_class = query_place // WIN + jnp.where(query_place >= WIN + WIN // 2, 1, 0)
    same = key_class == query_class
    offset = (query_row - key_row + WIN - 1) * (2 * WIN - 1) + query_place - key_place + WIN - 1
    offset = jnp.where(same, offset, -1)
    total = jnp.zeros((group, width), jnp.float32)
    for r in range(RELS):
        total = jnp.where(offset == r, by_offset[r : r + 1, :], total)
    total = jnp.where(same, total, masked_score)
    apart = jnp.where(key_row // (WIN // 2) == query_row // (WIN // 2), total, masked_score)
    for t in range(tiles):
        bias[2 * t] = total[:, 128 * t : 128 * (t + 1)]
        bias[2 * t + 1] = apart[:, 128 * t : 128 * (t + 1)]
    lane = lax.broadcasted_iota(jnp.int32, (group, 128), 1) // head
    picks = [(lane == h).astype(jnp.bfloat16) for h in range(pack)]

    def stacked(block):
        return jnp.concatenate([block * pick for pick in picks], 0)

    def folded(block):
        result = block[(pack - 1) * group :]
        for h in range(pack - 2, -1, -1):
            result = jnp.where(lane == h, block[h * group : (h + 1) * group], result)
        return result

    loads[0].wait()
    chunk, wide_chunk = 256, 512

    @pl.loop(0, tok // chunk)
    def _(i):
        normed, _ = norm_parts(xb[span(i, chunk), :].astype(jnp.float32))
        low = (normed * vectors[0:1, :] + vectors[1:2, :]).astype(jnp.bfloat16)
        put_rows(s.attn_in, i, low)
        s.attn_in_t[:, span(i, chunk)] = low.T

    queue.until(qkv_copies[-1].second)

    loads[1].wait()

    @pl.loop(0, tok // chunk)
    def _(i):
        live = lax.broadcasted_iota(jnp.int32, (chunk, width), 0) + i * chunk < used
        low = jnp.where(live, eb[span(i, chunk), :].astype(jnp.float32), 0.0)
        low = low.astype(jnp.bfloat16)
        eb[span(i, chunk), :] = low
        s.et[:, span(i, chunk)] = low.T

    queue.until(copy_0.fourth)
    whole_qkv, whole_proj = s.whole_qkv, s.whole_proj
    whole_up, whole_down = s.whole_up, s.whole_down
    before = (lax.rem(place.slab + slabs - 1, slabs), place.clip)
    after = (lax.rem(place.slab + 1, slabs), place.clip)

    qkv_bias = jnp.concatenate(
        [vectors[2:3, :], jnp.zeros((1, width), jnp.float32), vectors[3:4, :]], 1
    )
    head_in = jnp.concatenate([s.attn_in[heads[i]] for i in range(slots)], 0)
    lends, lends_back, gives, gives_back = {}, {}, {}, {}

    def ranges(t):
        return [slice(k * width + 128 * t, k * width + 128 * (t + 1)) for k in range(3)]

    def project(t):
        shift = jnp.concatenate([qkv_bias[:, at] for at in ranges(t)], 1)
        weights = jnp.concatenate([flat(whole_qkv, at) for at in ranges(t)], 1)
        rows = (mm(head_in, weights) + shift).astype(jnp.bfloat16)
        s.lent[t] = rows.reshape(slots, half, -1)
        lends[t] = links.send(s.lent.at[t], s.borrowed.at[t], before)

        @pl.loop(0, tok // wide_chunk)
        def _(i):
            weights = jnp.concatenate([flat(whole_qkv, at) for at in ranges(t)], 1)
            rows = (mm(rows_of(s.attn_in, i, wide_chunk), weights) + shift).astype(jnp.bfloat16)
            own[t, span(i, wide_chunk // half)] = rows.reshape(wide_chunk // half, half, -1)

    groups_unit = unit // group

    def window(ref, t, u, j):
        begin = units[BEGIN_AT, u] + 2 * j
        second = begin + 1 if j < groups_unit - 1 else units[SECOND_AT, u]
        return jnp.concatenate([ref[t, begin], ref[t, second]], 0)

    def parts(rows):
        return [rows[:, 128 * k : 128 * (k + 1)] for k in range(3)]

    def forward(t, works):
        rows = [parts(window(own, t, u, j)) for u, j in works]
        wraps = [units[WRAP_AT, u] if j == groups_unit - 1 else 0 for u, j in works]
        scores = [mm_nt(k, stacked(q)) for q, k, _ in rows]
        scores = [score * score_scale + bias[2 * t + wrap] for score, wrap in zip(scores, wraps)]
        weights = [jnp.exp(score - jnp.max(score, 0, keepdims=True)) for score in scores]
        weights = [weight * (1.0 / jnp.sum(weight, 0, keepdims=True)) for weight in weights]
        for (u, j), weight in zip(works, weights):
            s.probs[span(u * groups_unit + j, group), 128 * t : 128 * (t + 1)] = weight
        mixed = [
            mm_tn(weight.astype(jnp.bfloat16), v) for weight, (_, _, v) in zip(weights, rows)
        ]
        for (u, j), product in zip(works, mixed):
            out = folded(product).astype(jnp.bfloat16).reshape(2, half, 128)
            s.att_win[t, span(u * groups_unit + j, 2)] = out

    units_step = 4

    def inner(step, t):
        @pl.loop(0, unit_count // units_step)
        def _(i):
            step(
                t,
                [
                    (i * units_step + k, j)
                    for k in range(units_step)
                    for j in range(groups_unit - 1)
                ],
            )

    def outer(step, t, lent, arrived, ref):
        if lent is not None:
            lent.wait_recv()
            ref[t, tok // half :] = arrived[t]
        step(t, [(u, groups_unit - 1) for u in range(unit_count)])

    def give_back(ref, t, out, arrived):
        for slot in range(slots):
            out[t, slot] = ref[t, tails[slot]]
        return links.send(out.at[t], arrived.at[t], after)

    def from_windows(ref, t, given, arrived, store):
        given.wait_recv()
        ref[t, tok // half :] = arrived[t]

        @pl.loop(0, unit_count)
        def _(u):
            back = units[BACK_AT, u]
            rows = [ref[t, units[FRONT_AT, u]]] + [ref[t, back + k] for k in range(per_unit - 1)]
            store(t, u, jnp.concatenate(rows, 0))

    def place_attended(t, u, rows):
        cols = slice(128 * t, 128 * (t + 1))
        s.att_rows[span(u, unit), cols] = rows
        s.att_t[cols, span(u, unit)] = rows.T

    def outer_forward(t):
        outer(forward, t, lends[t], s.borrowed, own)
        gives[t] = give_back(s.att_win, t, s.att_out, s.att_back)

    copy_0.last()
    project(0)
    inner(forward, 0)
    queue.until(copy_2.fourth)
    copy_1.last()
    project(1)
    queue.take()
    inner(forward, 1)
    copy_2.last()
    outer_forward(0)
    for t in range(2, tiles):
        project(t)
    queue.take()
    inner(forward, 2)
    queue.take()
    outer_forward(1)
    outer_forward(2)
    queue.take()
    for t in range(3, tiles):
        outer_forward(t)
        queue.take()
        inner(forward, t)
    queue.take()
    for t in range(tiles):
        from_windows(s.att_win, t, gives[t], s.att_back, place_attended)

    queue.take()
    for flow in proj_copies:
        flow.last()
    mid, mlp_in = s.mid, s.mlp_in

    @pl.loop(0, tok // wide_chunk)
    def _(i):
        rows = mm(s.att_rows[span(i, wide_chunk), :], flat(whole_proj))
        rows = xb[span(i, wide_chunk), :].astype(jnp.float32) + rows + vectors[4:5, :]
        mid[span(i, wide_chunk), :] = rows
        normed, _ = norm_parts(rows)
        low = (normed * vectors[5:6, :] + vectors[6:7, :]).astype(jnp.bfloat16)
        mlp_in[span(i, wide_chunk), :] = low
        s.mlp_in_t[:, span(i, wide_chunk)] = low.T

    act, slope = s.act, s.slope
    wide = act.shape[1] // width
    for k, flow in enumerate(up_copies):
        queue.until(flow.fourth)
        flow.last()
        size = width // len(up_copies)
        lanes = [slice(c * width + k * size, c * width + (k + 1) * size) for c in range(wide)]
        piece = slice(k * size, (k + 1) * size)
        shift = jnp.concatenate([vectors[8 + c : 9 + c, piece] for c in range(wide)], 1)

        @pl.loop(0, 1)
        def _(i):
            weights = jnp.concatenate([flat(whole_up, at) for at in lanes], 1)
            pre = mm(mlp_in[span(i, tok), :], weights)
            value, derivative = gelu_parts(pre + shift)
            value, derivative = value.astype(jnp.bfloat16), derivative.astype(jnp.bfloat16)
            for c, at in enumerate(lanes):
                act[span(i, tok), at] = value[:, c * size : (c + 1) * size]
                slope[span(i, tok), at] = derivative[:, c * size : (c + 1) * size]

        queue.take()

    down = down_parts[0]

    @pl.loop(0, clips)
    def _(c):
        size = act.shape[1] // clips
        part = (mm(s.et[...], act[:, span(c, size)]) * grad_scale).astype(jnp.bfloat16)
        part = part.reshape(slabs, 2, -1, size)
        for h in range(2):
            down[:, c % 2, h, c // 2] = part[:, h]

    for flow in down_flows:
        flow.first()

    queue.until(down_copies[-1].fourth)
    for flow in down_copies:
        flow.last()

    def pre_back(c):
        cols = span(c, width)
        weights = whole_down[c].reshape(width, width)

        def step(i, sums):
            grad = mm_nt(eb[span(i, tok), :], weights)
            low = grad * slope[span(i, tok), cols].astype(jnp.float32)
            low = low.astype(jnp.bfloat16)
            slope[span(i, tok), cols] = low
            return sums + jnp.sum(low.astype(jnp.float32), 0, keepdims=True)

        sums = lax.fori_loop(0, 1, step, jnp.zeros((1, width), jnp.float32))
        s.up_sum[c : c + 1, :] = sums

    for c in range(wide):
        pre_back(c)

    up = up_parts[0]

    def keep(target, slab, part, lanes=EVERY):
        part = (part * grad_scale).astype(jnp.bfloat16)
        part = part.reshape(clips // 2, 2, 2, -1, part.shape[-1])
        for y in range(2):
            for h in range(2):
                target[slab, y, h, :, :, lanes] = part[:, y, h]

    def up_grad(i):
        keep(up, i, mm(s.mlp_in_t[...], slope[:, span(i, act.shape[1] // slabs)]))

    pl.loop(0, slabs // 2)(up_grad)
    for flow in down_flows:
        flow.second()
    pl.loop(slabs // 2, slabs)(up_grad)
    for flow in up_flows:
        flow.first()

    mid_grad, mid_low = s.mid_grad, s.mid_low

    def mid_step(i, sums):
        grad = mm_nt(slope[span(i, tok), :], flat(whole_up))
        normed, inverse = norm_parts(mid[span(i, tok), :])
        out_grad = eb[span(i, tok), :].astype(jnp.float32)
        rows = out_grad + norm_back(normed, inverse, grad * vectors[5:6, :])
        low = rows.astype(jnp.bfloat16)
        mid_grad[span(i, tok), :] = rows
        put_rows(mid_low, i, low)
        return tuple(
            old + jnp.sum(new, 0, keepdims=True)
            for old, new in zip(sums, (low.astype(jnp.float32), grad * normed, grad, out_grad))
        )

    zero = jnp.zeros((1, width), jnp.float32)
    mid_sums = lax.fori_loop(0, 1, mid_step, (zero,) * 4)
    for row, value in zip((4, 5, 6, 7), mid_sums):
        small.held[0, row : row + 1, :] = value * grad_scale
    small.held[0, 8:12, :] = s.up_sum[...] * grad_scale

    proj_columns = flat(whole_proj)
    head_low = jnp.concatenate(
        [mid_low[heads[i]] for i in range(slots)], 0
    )
    rows = mm_nt(head_low, proj_columns).astype(jnp.bfloat16)
    for t in range(tiles):
        s.dlent[t] = rows[:, 128 * t : 128 * (t + 1)].reshape(slots, half, 128)
    lend_back = links.send(s.dlent, s.dborrowed, before)
    dwin_own = s.dwin_own

    @pl.loop(0, tok // wide_chunk)
    def _(i):
        rows = mm_nt(rows_of(mid_low, i, wide_chunk), flat(whole_proj))
        rows = rows.astype(jnp.bfloat16)
        for t in range(tiles):
            part = rows[:, 128 * t : 128 * (t + 1)].reshape(-1, half, 128)
            dwin_own[t, span(i, part.shape[0])] = part

    grad = mm(s.att_t[...], mid_low[...].reshape(tok, width))
    for i in range(slabs):
        keep(proj_flow.held, i, grad[:, i * (width // slabs) : (i + 1) * (width // slabs)])
    proj_flow.first()
    for flow in up_flows:
        flow.second()

    bias_grad, qg_win = s.bias_grad, s.qg_win
    bias_grad[...] = jnp.zeros_like(bias_grad)

    def backward(t, works):
        cols = slice(128 * t, 128 * (t + 1))
        rows = [parts(window(own, t, u, j)) for u, j in works]
        mixed = [stacked(window(dwin_own, t, u, j)) for u, j in works]
        weights = [s.probs[span(u * groups_unit + j, group), cols] for u, j in works]
        prob_grads = [mm_nt(v, g) for (_, _, v), g in zip(rows, mixed)]
        value_grads = [mm(weight.astype(jnp.bfloat16), g) for weight, g in zip(weights, mixed)]
        scores = [
            (weight * (grad - jnp.sum(weight * grad, 0, keepdims=True))).astype(jnp.bfloat16)
            for weight, grad in zip(weights, prob_grads)
        ]
        bias_grad[:, cols] += sum(score.astype(jnp.float32) for score in scores)
        key_grads = [mm(score, stacked(q)) * score_scale for score, (q, _, _) in zip(scores, rows)]
        query_grads = [
            folded(mm_tn(score, k)) * score_scale for score, (_, k, _) in zip(scores, rows)
        ]
        for (u, j), *grads in zip(works, query_grads, key_grads, value_grads):
            out = jnp.concatenate(grads, 1).astype(jnp.bfloat16)
            qg_win[t, span(u * groups_unit + j, 2)] = out.reshape(2, half, -1)

    qg_rows = s.qg_rows

    def place_grads(t, u, rows):
        for k, at in enumerate(ranges(t)):
            qg_rows[span(u, unit), at] = rows[:, 128 * k : 128 * (k + 1)]

    def qkv_grad(flow):
        starts = []
        for slab in range(slabs):
            start, size = flow.columns(slab)
            starts.append((int(start) + slab * 3 * width // slabs, int(start), size))
        rows = jnp.concatenate([qg_rows[:, at : at + size] for at, _, size in starts], 1)
        grad = mm(s.attn_in_t[...], rows)
        for slab, (_, start, size) in enumerate(starts):
            part = grad[:, slab * size : (slab + 1) * size]
            keep(qkv_parts[0], slab, part, slice(start, start + size))

    inner(backward, 0)
    for flow in down_flows:
        flow.third()
    lend_back.wait_recv()
    dwin_own[:, tok // half :] = s.dborrowed[...]
    for t in range(tiles):
        outer(backward, t, None, None, None)
        gives_back[t] = give_back(qg_win, t, s.qg_out, s.qg_back)
    proj_flow.second()
    inner(backward, 1)
    for flow in up_flows:
        flow.third()
    for t in range(2):
        from_windows(qg_win, t, gives_back[t], s.qg_back, place_grads)
    qkv_grad(qkv_flows[0])
    qkv_flows[0].first()
    inner(backward, 2)
    for flow in down_flows:
        flow.fourth()
    from_windows(qg_win, 2, gives_back[2], s.qg_back, place_grads)
    qkv_grad(qkv_flows[1])
    qkv_flows[1].first()
    qkv_flows[0].second()
    inner(backward, 3)
    from_windows(qg_win, 3, gives_back[3], s.qg_back, place_grads)
    qkv_grad(qkv_flows[2])
    qkv_flows[2].first()
    qkv_flows[1].second()
    proj_flow.third()
    for flow in up_flows:
        flow.fourth()

    def in_step(i, sums):
        rows = qg_rows[span(i, wide_chunk), :]
        grad = mm_nt(rows, flat(whole_qkv))
        normed, inverse = norm_parts(xb[span(i, wide_chunk), :].astype(jnp.float32))
        back = norm_back(normed, inverse, grad * vectors[0:1, :])
        mid_grad[span(i, wide_chunk), :] = mid_grad[span(i, wide_chunk), :] + back
        query_part = rows[:, :width].astype(jnp.float32)
        value_part = rows[:, 2 * width :].astype(jnp.float32)
        return tuple(
            old + jnp.sum(new, 0, keepdims=True)
            for old, new in zip(sums, (grad * normed, grad, query_part, value_part))
        )

    in_sums = lax.fori_loop(0, tok // wide_chunk, in_step, (zero,) * 4)
    store_grad = pltpu.make_async_copy(mid_grad, x_grad, s.load_sems.at[1])
    store_grad.start()
    for row, value in zip((0, 1, 2, 3), in_sums):
        small.held[0, row : row + 1, :] = value * grad_scale

    by_head = bias_grad[...]
    for r in range(RELS):
        picked = jnp.sum(jnp.where(offset == r, by_head, 0.0), 0, keepdims=True)
        s.att_sum[r : r + 1, :] = picked
    s.att_sum[RELS:, :] = jnp.zeros((128 - RELS, width), jnp.float32)
    sums = lax.dot_general(
        spread, s.att_sum[...], (((1,), (1,)), ((), ())), precision=HIGHEST
    ) * grad_scale
    for i in range(width // 128):
        small.held[0, 12:16, 128 * i : 128 * (i + 1)] = sums[4 * i : 4 * i + 4, :]

    small.first()
    qkv_flows[2].second()
    qkv_flows[0].third()
    qkv_flows[1].third()
    proj_flow.fourth()
    small.second()

    out_low = s.att_rows

    @pl.loop(0, tok // wide_chunk)
    def _(i):
        rows = mid[span(i, wide_chunk), :] + mm(act[span(i, wide_chunk), :], flat(whole_down))
        live = lax.broadcasted_iota(jnp.int32, (wide_chunk, width), 0) + i * wide_chunk < used
        rows = jnp.where(live, rows + vectors[7:8, :], 0.0)
        out_low[span(i, wide_chunk), :] = rows.astype(jnp.bfloat16)

    store_out = pltpu.make_async_copy(out_low, block_out, s.load_sems.at[0])
    store_out.start()

    def finish(flows, out, turn):
        for flow in flows:
            total, lanes = flow.last()
            rows = total.shape[1]
            if turn:
                out[lanes, :] = total.reshape(2 * rows, -1).T
            else:
                out[:rows, lanes] = total[0]
                out[rows:, lanes] = total[1]

    finish(down_flows, owned[3], True)
    qkv_flows[2].third()
    qkv_flows[0].fourth()
    qkv_flows[1].fourth()
    small.third()
    finish(up_flows, owned[2], False)
    finish([proj_flow], owned[1], False)
    qkv_flows[2].fourth()
    small.fourth()
    finish(qkv_flows, owned[0], False)
    small_out[...] = small.last()
    store_out.wait()
    store_grad.wait()
    links.drain()


BEGIN_AT, SECOND_AT, FRONT_AT, BACK_AT, WRAP_AT = range(5)


def block_call(tokens, y_grad, clip_rows, vectors, table, masters, slab_size, clip_size):
    vmem, smem, anywhere = (
        pl.BlockSpec(memory_space=pltpu.VMEM),
        pl.BlockSpec(memory_space=pltpu.SMEM),
        pl.BlockSpec(memory_space=pl.ANY),
    )
    depth = clip_size // 2
    tok, width = tokens.shape
    hidden = masters[2].shape[1] * slab_size
    slots = clip_rows.shape[1]
    half = WIN // 2 * BINS
    tiles = width // 128
    low, full = jnp.bfloat16, jnp.float32
    helds = []
    for position, master in enumerate(masters):
        rows, columns = master.shape if position < 3 else master.shape[::-1]
        helds.append((slab_size, 2, 2, depth, rows // 2, columns))
    def buffer(*sizes):
        kind = full if sizes[-1] is full else low
        return pltpu.VMEM(sizes[:-1] if sizes[-1] is full else sizes, kind)

    def whole(master):
        return buffer(depth, 2, 2, master.shape[0] // 2, slab_size * master.shape[1])

    held = Held(
        xb=buffer(tok, width), eb=buffer(tok, width), et=buffer(width, tok),
        attn_in=buffer(tok // half, half, width), attn_in_t=buffer(width, tok),
        own=buffer(tiles, tok // half + slots, half, 384), lent=buffer(tiles, slots, half, 384),
        borrowed=buffer(tiles, slots, half, 384),
        probs=buffer(tok, width, full), att_win=buffer(tiles, tok // half + slots, half, 128),
        att_out=buffer(tiles, slots, half, 128), att_back=buffer(tiles, slots, half, 128), att_rows=buffer(tok, width), att_t=buffer(width, tok),
        mid=buffer(tok, width, full), mlp_in=buffer(tok, width), mlp_in_t=buffer(width, tok),
        act=buffer(tok, hidden), slope=buffer(tok, hidden), mid_grad=buffer(tok, width, full),
        mid_low=buffer(tok // half, half, width), dwin_own=buffer(tiles, tok // half + slots, half, 128), dlent=buffer(tiles, slots, half, 128),
        dborrowed=buffer(tiles, slots, half, 128), qg_win=buffer(tiles, tok // half + slots, half, 384),
        qg_out=buffer(tiles, slots, half, 384), qg_back=buffer(tiles, slots, half, 384), qg_rows=buffer(tok, 3 * width),
        bias=buffer(2 * tiles, WIN * BINS, 128, full), bias_grad=buffer(WIN * BINS, width, full),
        up_sum=buffer(hidden // width, width, full), att_sum=buffer(128, width, full),
        units=pltpu.SMEM((5, tok // (SHORT // slab_size * BINS)), jnp.int32),
        load_sems=pltpu.SemaphoreType.DMA((2,)),
        whole_qkv=whole(masters[0]), whole_proj=whole(masters[1]),
        whole_up=whole(masters[2]), whole_down=whole(masters[3]),
    )
    copies = 12 * (depth - 1 + 7) + 8 * (7 + depth - 1) + 3 + depth - 1 + 16
    scratch = [pltpu.SemaphoreType.DMA((copies,)), pltpu.SemaphoreType.DMA((copies,)), *held]
    small = (16, width)
    scratch += [
        pltpu.VMEM((3,) + small, full), pltpu.VMEM((3,) + small, full), pltpu.VMEM((depth,) + small, full)
    ]
    for sizes in helds:
        scratch += [pltpu.VMEM(sizes, low)] + scatter_buffers(sizes)
    return pl.pallas_call(
        functools.partial(block_kernel, slab_size, clip_size),
        out_shape=[
            jax.ShapeDtypeStruct((tok, width), low),
            jax.ShapeDtypeStruct((tok, width), full),
            jax.ShapeDtypeStruct(small, full),
        ]
        + [jax.ShapeDtypeStruct(m.shape, full) for m in masters],
        in_specs=[anywhere, anywhere, smem] + [vmem] * 6,
        out_specs=[anywhere, anywhere] + [vmem] * 5,
        scratch_shapes=scratch,
        compiler_params=pltpu.CompilerParams(
            collective_id=0, has_side_effects=True, vmem_limit_bytes=62 << 20
        ),
        name="block",
    )(tokens, y_grad, clip_rows, vectors, table.T, *masters)


def finish_kernel(block_out, x_grad, small, *refs):
    weights, grads = refs[:18], refs[18:22]
    block_out_to, x_grad_to = refs[22:24]
    results, (held_out, held_grad, sems) = refs[24:-3], refs[-3:]
    passing = [
        pltpu.make_async_copy(block_out, held_out, sems.at[0]),
        pltpu.make_async_copy(x_grad, held_grad, sems.at[1]),
    ]
    for copy in passing:
        copy.start()
    rows = weights[12].shape[0]
    table = jnp.concatenate(
        [small[rows:, 128 * i : 128 * (i + 1)] for i in range(small.shape[1] // 128)], 0
    )
    values = [grad[...] for grad in grads] + [small[:rows, :], table[:, :RELS]]
    for k, grad in enumerate(values):
        weight, first, second = [ref[...] for ref in weights[3 * k : 3 * k + 3]]
        rate, decay = (rate_matrix, weight_decay) if k < len(grads) else (rate_vector, 0.0)
        for ref, value in zip(
            results[3 * k : 3 * k + 3], adamw(weight, first, second, grad, rate, decay)
        ):
            ref[...] = value
    passed = [
        pltpu.make_async_copy(held_out, block_out_to, sems.at[2]),
        pltpu.make_async_copy(held_grad, x_grad_to, sems.at[3]),
    ]
    for before, after in zip(passing, passed):
        before.wait()
        after.start()
    for copy in passed:
        copy.wait()


def finish_call(block_out, x_grad, small, weights, grads):
    vmem, anywhere = pl.BlockSpec(memory_space=pltpu.VMEM), pl.BlockSpec(memory_space=pl.ANY)
    like = [jax.ShapeDtypeStruct(a.shape, a.dtype) for a in (block_out, x_grad, *weights)]
    return pl.pallas_call(
        finish_kernel,
        out_shape=like,
        in_specs=[anywhere, anywhere] + [vmem] * (1 + len(weights) + len(grads)),
        out_specs=[anywhere, anywhere] + [vmem] * len(weights),
        scratch_shapes=[
            pltpu.VMEM(block_out.shape, block_out.dtype),
            pltpu.VMEM(x_grad.shape, x_grad.dtype),
            pltpu.SemaphoreType.DMA((4,)),
        ],
        compiler_params=pltpu.CompilerParams(vmem_limit_bytes=62 << 20),
        name="finish",
    )(block_out, x_grad, small, *weights, *grads)


def shards(
    tokens,
    y_grad,
    clip_rows,
    qkv_weight,
    proj_weight,
    up_weight,
    down_weight,
    qkv_m,
    proj_m,
    up_m,
    down_m,
    qkv_v,
    proj_v,
    up_v,
    down_v,
    vectors,
    vectors_m,
    vectors_v,
    table,
    table_m,
    table_v,
):
    slab_size, clip_size = lax.axis_size(SLAB), lax.axis_size(CLIP)
    masters = (qkv_weight, proj_weight, up_weight, down_weight)
    hidden = up_weight.shape[1] * slab_size
    aligned = slab_size == 4 and clip_size % 2 == 0 and all(m.shape[0] % 32 == 0 for m in masters)
    if aligned and hidden // (clip_size // 2) == tokens.shape[-1]:
        block_out, x_grad, small, *owned = block_call(
            tokens[0, 0], y_grad[0, 0], clip_rows, vectors, table, masters, slab_size, clip_size
        )
        weights = (
            qkv_weight, qkv_m, qkv_v, proj_weight, proj_m, proj_v,
            up_weight, up_m, up_v, down_weight, down_m, down_v,
            vectors, vectors_m, vectors_v, table.T, table_m.T, table_v.T,
        )
        results = finish_call(block_out, x_grad, small, weights, owned)
        results = [results[0][None, None], results[1][None, None], *results[2:]]
        results[-3:] = [result.T for result in results[-3:]]
        return tuple(results)
    lengths = clip_rows[0]
    slab_count = lax.axis_size(SLAB)
    inputs = tokens[0, 0].astype(jnp.float32)
    tok_count, width = inputs.shape
    rows_dev = tok_count // BINS
    head_dim = width // HEADS
    score_scale = head_dim ** (-0.5)
    source, time_wraps, seg_starts = window_rows(
        lengths, lax.axis_index(SLAB), slab_count, rows_dev
    )
    total_rows = rows_dev + 2 * lengths.shape[0]
    head_rows = jnp.minimum(
        seg_starts[:, None] + jnp.arange(2, dtype=jnp.int32)[None, :], rows_dev - 1
    ).reshape(-1)
    windows_count = source.shape[0] * (BINS // WIN)
    bin_folds = jnp.arange(windows_count) % (BINS // WIN) == BINS // WIN - 1
    allowed = window_mask(jnp.repeat(time_wraps, BINS // WIN), bin_folds)[:, None]
    offset_hot = offset_table()
    rel_bias = (
        jnp.dot(offset_hot, table, precision=HIGHEST)
        .reshape(WIN * WIN, WIN * WIN, HEADS)
        .transpose(2, 0, 1)
    )
    used_rows = jnp.sum(lengths) // slab_count
    live_rows = (jnp.arange(tok_count) // BINS < used_rows).astype(jnp.float32)[:, None]
    part_copies = (
        lax.all_gather(qkv_weight.astype(jnp.bfloat16), CLIP, axis=0, tiled=True),
        lax.all_gather(proj_weight.astype(jnp.bfloat16), CLIP, axis=0, tiled=True),
        lax.all_gather(up_weight.astype(jnp.bfloat16), CLIP, axis=0, tiled=True),
        lax.all_gather(down_weight.astype(jnp.bfloat16), CLIP, axis=0, tiled=True),
    )
    copies = (
        lax.all_gather(part_copies[0], SLAB, axis=1, tiled=True),
        lax.all_gather(part_copies[1], SLAB, axis=1, tiled=True),
        lax.all_gather(part_copies[2], SLAB, axis=1, tiled=True),
        lax.all_gather(part_copies[3], SLAB, axis=1, tiled=True),
    )
    qkv_copy, proj_copy, up_copy, down_copy = copies
    attn_input = affine_norm(inputs, vectors[0], vectors[1]).astype(jnp.bfloat16)
    bias_row = jnp.concatenate([vectors[2], jnp.zeros_like(vectors[2]), vectors[3]])
    qkv_rows = (
        jnp.dot(attn_input, qkv_copy, preferred_element_type=jnp.float32) + bias_row
    ).astype(jnp.bfloat16)
    qkv_grid = qkv_rows.reshape(rows_dev, BINS, 3 * width)
    borrowed = from_behind(qkv_grid[head_rows], SLAB, -1)
    qkv_windows = to_windows(jnp.concatenate([qkv_grid, borrowed], 0), source)
    query_win = qkv_windows[:, :, :width].reshape(windows_count, WIN * WIN, HEADS, head_dim)
    key_win = qkv_windows[:, :, width : 2 * width].reshape(
        windows_count, WIN * WIN, HEADS, head_dim
    )
    value_win = qkv_windows[:, :, 2 * width :].reshape(windows_count, WIN * WIN, HEADS, head_dim)

    def scores_of(queries, keys_all):
        raw = (
            jnp.einsum("wqhd,wkhd->whqk", queries, keys_all, preferred_element_type=jnp.float32)
            * score_scale
            + rel_bias[None]
        )
        return jnp.where(allowed, raw, masked_score)

    scores = scores_of(query_win, key_win)
    top_score = jnp.max(scores, -1, keepdims=True)
    exp_sum = jnp.sum(jnp.exp(scores - top_score), -1, keepdims=True)
    probs_low = (jnp.exp(scores - top_score) / exp_sum).astype(jnp.bfloat16)
    attended = jnp.einsum(
        "whqk,wkhd->wqhd", probs_low, value_win, preferred_element_type=jnp.float32
    )
    attended = attended.astype(jnp.bfloat16).reshape(windows_count, WIN * WIN, width)
    spread_out = from_windows(attended, source, total_rows)
    returned = from_behind(spread_out[rows_dev:], SLAB, 1)
    attended_rows = spread_out[:rows_dev].at[head_rows].add(returned).reshape(tok_count, width)
    residual = (
        inputs + jnp.dot(attended_rows, proj_copy, preferred_element_type=jnp.float32) + vectors[4]
    )
    mlp_input = affine_norm(residual, vectors[5], vectors[6]).astype(jnp.bfloat16)
    pre_gelu = jnp.dot(mlp_input, up_copy, preferred_element_type=jnp.float32) + vectors[
        8:
    ].reshape(-1)
    activated, gelu_pull = jax.vjp(gelu_exact, pre_gelu)
    activated_low = activated.astype(jnp.bfloat16)
    block_out = (
        residual
        + jnp.dot(activated_low, down_copy, preferred_element_type=jnp.float32)
        + vectors[7]
    ) * live_rows
    out_grad = y_grad[0, 0].astype(jnp.float32) * live_rows
    out_low = out_grad.astype(jnp.bfloat16)
    down_grad = jnp.dot(activated_low.T, out_low, preferred_element_type=jnp.float32)
    act_grad = jnp.dot(out_low, down_copy.T, preferred_element_type=jnp.float32)
    pre_low = gelu_pull(act_grad)[0].astype(jnp.bfloat16)
    up_grad = jnp.dot(mlp_input.T, pre_low, preferred_element_type=jnp.float32)
    mlp_in_grad = jnp.dot(pre_low, up_copy.T, preferred_element_type=jnp.float32)
    norm_value, norm_pull = jax.vjp(affine_norm, residual, vectors[5], vectors[6])
    resid_norm_grad, gain_two_grad, shift_two_grad = norm_pull(mlp_in_grad)
    resid_grad = out_grad + resid_norm_grad
    attn_low = resid_grad.astype(jnp.bfloat16)
    proj_grad = jnp.dot(attended_rows.T, attn_low, preferred_element_type=jnp.float32)
    mixed_grad = jnp.dot(attn_low, proj_copy.T, preferred_element_type=jnp.float32).astype(
        jnp.bfloat16
    )
    mixed_grid = mixed_grad.reshape(rows_dev, BINS, width)
    sent_back = from_behind(mixed_grid[head_rows], SLAB, -1)
    grad_windows = to_windows(jnp.concatenate([mixed_grid, sent_back], 0), source)
    grad_windows = grad_windows.reshape(windows_count, WIN * WIN, HEADS, head_dim)
    probs = jnp.exp(scores_of(query_win, key_win) - top_score) / exp_sum
    prob_grad = jnp.einsum(
        "wqhd,wkhd->whqk", grad_windows, value_win, preferred_element_type=jnp.float32
    )
    value_grad = jnp.einsum(
        "whqk,wqhd->wkhd", probs_low, grad_windows, preferred_element_type=jnp.float32
    )
    score_grad = (probs * (prob_grad - jnp.sum(probs * prob_grad, -1, keepdims=True))).astype(
        jnp.bfloat16
    )
    bias_grad = (
        jnp.sum(score_grad.astype(jnp.float32), 0)
        .transpose(1, 2, 0)
        .reshape(WIN * WIN * WIN * WIN, HEADS)
    )
    table_grad = jnp.dot(offset_hot.T, bias_grad, precision=HIGHEST)
    query_grad = (
        jnp.einsum("whqk,wkhd->wqhd", score_grad, key_win, preferred_element_type=jnp.float32)
        * score_scale
    )
    key_grad = (
        jnp.einsum("whqk,wqhd->wkhd", score_grad, query_win, preferred_element_type=jnp.float32)
        * score_scale
    )
    qkv_grad_win = jnp.concatenate(
        [
            query_grad.reshape(windows_count, WIN * WIN, width),
            key_grad.reshape(windows_count, WIN * WIN, width),
            value_grad.reshape(windows_count, WIN * WIN, width),
        ],
        -1,
    ).astype(jnp.bfloat16)
    qkv_spread = from_windows(qkv_grad_win, source, total_rows)
    given_back = from_behind(qkv_spread[rows_dev:], SLAB, 1)
    qkv_grad_rows = (
        qkv_spread[:rows_dev].at[head_rows].add(given_back).reshape(tok_count, 3 * width)
    )
    qkv_w_grad = jnp.dot(attn_input.T, qkv_grad_rows, preferred_element_type=jnp.float32)
    bias_sums = jnp.sum(qkv_grad_rows.astype(jnp.float32), 0)
    attn_in_grad = jnp.dot(qkv_grad_rows, qkv_copy.T, preferred_element_type=jnp.float32)
    first_value, norm_pull_one = jax.vjp(affine_norm, inputs, vectors[0], vectors[1])
    inputs_norm_grad, gain_one_grad, shift_one_grad = norm_pull_one(attn_in_grad)
    x_grad = resid_grad + inputs_norm_grad
    vector_grad = jnp.concatenate(
        [
            jnp.stack(
                [
                    gain_one_grad,
                    shift_one_grad,
                    bias_sums[:width],
                    bias_sums[2 * width :],
                    jnp.sum(attn_low.astype(jnp.float32), 0),
                    gain_two_grad,
                    shift_two_grad,
                    jnp.sum(out_grad, 0),
                ]
            ),
            jnp.sum(pre_low.astype(jnp.float32), 0).reshape(-1, width),
        ],
        0,
    )
    grad_scale = float(tok_count * slab_count * lax.axis_size(CLIP)) ** (-0.5)
    part_sums = (
        lax.psum_scatter(
            (qkv_w_grad * grad_scale).astype(jnp.bfloat16), SLAB, scatter_dimension=1, tiled=True
        ).astype(jnp.float32),
        lax.psum_scatter(
            (proj_grad * grad_scale).astype(jnp.bfloat16), SLAB, scatter_dimension=1, tiled=True
        ).astype(jnp.float32),
        lax.psum_scatter(
            (up_grad * grad_scale).astype(jnp.bfloat16), SLAB, scatter_dimension=1, tiled=True
        ).astype(jnp.float32),
        lax.psum_scatter(
            (down_grad * grad_scale).astype(jnp.bfloat16), SLAB, scatter_dimension=1, tiled=True
        ).astype(jnp.float32),
    )
    owned = (
        lax.psum_scatter(part_sums[0], CLIP, scatter_dimension=0, tiled=True),
        lax.psum_scatter(part_sums[1], CLIP, scatter_dimension=0, tiled=True),
        lax.psum_scatter(part_sums[2], CLIP, scatter_dimension=0, tiled=True),
        lax.psum_scatter(part_sums[3], CLIP, scatter_dimension=0, tiled=True),
    )
    small_sums = lax.psum((vector_grad * grad_scale, table_grad * grad_scale), (SLAB, CLIP))
    qkv_new, qkv_m_new, qkv_v_new = adamw(
        qkv_weight, qkv_m, qkv_v, owned[0], rate_matrix, weight_decay
    )
    proj_new, proj_m_new, proj_v_new = adamw(
        proj_weight, proj_m, proj_v, owned[1], rate_matrix, weight_decay
    )
    up_new, up_m_new, up_v_new = adamw(up_weight, up_m, up_v, owned[2], rate_matrix, weight_decay)
    down_new, down_m_new, down_v_new = adamw(
        down_weight, down_m, down_v, owned[3], rate_matrix, weight_decay
    )
    vectors_new, vectors_m_new, vectors_v_new = adamw(
        vectors, vectors_m, vectors_v, small_sums[0], rate_vector, 0.0
    )
    table_new, table_m_new, table_v_new = adamw(
        table, table_m, table_v, small_sums[1], rate_vector, 0.0
    )
    out_shape = (1, 1, tok_count, width)
    return (
        block_out.astype(jnp.bfloat16).reshape(out_shape),
        x_grad.reshape(out_shape),
        qkv_new,
        qkv_m_new,
        qkv_v_new,
        proj_new,
        proj_m_new,
        proj_v_new,
        up_new,
        up_m_new,
        up_v_new,
        down_new,
        down_m_new,
        down_v_new,
        vectors_new,
        vectors_m_new,
        vectors_v_new,
        table_new,
        table_m_new,
        table_v_new,
    )


def solution(mesh):
    return jax.shard_map(
        shards,
        mesh=mesh,
        in_specs=(
            P(CLIP, SLAB, None, None),
            P(CLIP, SLAB, None, None),
            P(CLIP, None),
            P(CLIP, SLAB),
            P(CLIP, SLAB),
            P(CLIP, SLAB),
            P(CLIP, SLAB),
            P(CLIP, SLAB),
            P(CLIP, SLAB),
            P(CLIP, SLAB),
            P(CLIP, SLAB),
            P(CLIP, SLAB),
            P(CLIP, SLAB),
            P(CLIP, SLAB),
            P(CLIP, SLAB),
            P(),
            P(),
            P(),
            P(),
            P(),
            P(),
        ),
        out_specs=(
            P(CLIP, SLAB, None, None),
            P(CLIP, SLAB, None, None),
            P(CLIP, SLAB),
            P(CLIP, SLAB),
            P(CLIP, SLAB),
            P(CLIP, SLAB),
            P(CLIP, SLAB),
            P(CLIP, SLAB),
            P(CLIP, SLAB),
            P(CLIP, SLAB),
            P(CLIP, SLAB),
            P(CLIP, SLAB),
            P(CLIP, SLAB),
            P(CLIP, SLAB),
            P(),
            P(),
            P(),
            P(),
            P(),
            P(),
        ),
        check_vma=False,
    )
```
